32 devices in a mesh: dp: 2 (over core), seq: 16 (over z, y, x).
Axes of the slice: x: 2, y: 2, z: 4, core: 2. Of those that a mesh axis runs over, the one named last changes fastest.
Arguments:
- tokens: bfloat16 [2, 2, 2048, 768], P(None, 'dp', 'seq'), may hold values from -6 to 6
- cotangent: bfloat16 [2, 2, 2048, 768], P(None, 'dp', 'seq'), may hold values from -6 to 6
- segments: int32 [2, 2, 2048], P(None, 'dp', 'seq'), may hold values from 0 to 3, never falling along the last dimension, each value on 1 to 1024 neighbouring positions
- norm_gain: bfloat16 [768], P('seq'), may hold values from 0.5 to 1.5
- w_in: bfloat16 [768, 3352], P('seq'), may hold values from -0.21875 to 0.21875
- conv_weight: bfloat16 [4, 1792], P(None, 'seq'), may hold values from -3 to 3
- conv_bias: bfloat16 [1792], P('seq'), may hold values from -1.75 to 1.75
- step_bias: float32 [24], replicated, may hold values from -6 to -2
- log_rate: float32 [24], replicated, may hold values from -9 to 0
- skip_gain: float32 [24], replicated, may hold values from 0.5 to 1.5
- gate_gain: bfloat16 [1536], P('seq'), may hold values from 0.5 to 1.5
- w_out: bfloat16 [1536, 768], P('seq'), may hold values from -0.15625 to 0.15625
Outputs:
- activations: bfloat16 [2, 2, 2048, 768], P(None, 'dp', 'seq')
- grad_tokens: bfloat16 [2, 2, 2048, 768], P(None, 'dp', 'seq')
- grad_norm_gain: float32 [768], P('seq')
- grad_w_in: float32 [768, 3352], P('seq')
- grad_conv_weight: float32 [4, 1792], P(None, 'seq')
- grad_conv_bias: float32 [1792], P('seq')
- grad_step_bias: float32 [24], replicated
- grad_log_rate: float32 [24], replicated
- grad_skip_gain: float32 [24], replicated
- grad_gate_gain: float32 [1536], P('seq')
- grad_w_out: float32 [1536, 768], P('seq')
The draws below stay inside these ranges and needn't reach their ends.
Inputs may be any that keep to these rules, and one draw needn't show every extreme that they name: `segments`: within each sequence the numbers never fall; a change of number starts a document.
All inputs are finite; a program needn't handle non-finite values.
Results may differ from the reference program's by a relative error of at most 0.0095.
Values may be sent and summed in bfloat16 or wider, within the bound.
A program may use at most 448 MiB of HBM per device.

```python
import math
import jax
import jax.numpy as jnp
import numpy as np
from jax import lax

D = 768
DI = 1536
H = 24
P_SIZE = 64
N = 128
KC = 4
CH = 1792
E = 3352
L_DEV = 128
MB = 2
SEQS = 2
LEN = 2048
DOCS = 4
DOC_MOST = 1024


def draw_log_rate(key, part):
    return jax.random.uniform(key, (H,), jnp.float32, -9.0, 0.0)


def levels(stream_key, extent, cuts, least, top_value):
    gain, own = 1.0, jax.random.fold_in(stream_key, 6)
    for dim, parts in cuts:
        heights = jnp.exp(jax.random.uniform(jax.random.fold_in(own, dim), (parts,), jnp.float32, least / len(cuts), top_value / len(cuts)))
        gain = gain * jnp.repeat(heights, extent[dim] // parts).reshape([-1 if axis == dim else 1 for axis in range(len(extent))])
    return gain


def profile(amount, total, limit, slope):
    weights = [(1 << 20) // math.isqrt(standing ** slope) + 1 for standing in range(2, amount + 1)]
    rest, given = total - limit - (amount - 1), [1] * (amount - 1)
    while rest > 0:
        free = [i for i in range(amount - 1) if given[i] < limit]
        pool, remaining = sum([weights[i] for i in free]), rest
        for i in free:
            more = min(limit - given[i], max(1, remaining * weights[i] // pool), rest)
            given[i] = given[i] + more
            rest = rest - more
    return np.array([limit] + given)


def ragged_sizes(rng, amount, total, limit, skew):
    if amount == 2:
        one = jax.random.randint(rng, (), max(1, total - limit), min(limit, total - 1) + 1)
        return jnp.stack([one, total - one])
    lengths = jnp.asarray(profile(amount, total, limit, skew), jnp.int32)
    couples = (amount - 1) // 2
    giver, taker = lengths[1:1 + 2 * couples:2], lengths[2:2 + 2 * couples:2]
    margin = jnp.minimum(giver - 1, limit - taker)
    moved = jax.random.randint(jax.random.fold_in(rng, 1), (couples,), 0, 1 << 20) % (margin + 1)
    lengths = lengths.at[1:1 + 2 * couples:2].set(giver - moved).at[2:2 + 2 * couples:2].set(taker + moved)
    return lengths[jax.random.permutation(jax.random.fold_in(rng, 2), amount)]


def noise(stream_key, extent, scale, bound, cuts=(), dtype=jnp.bfloat16):
    entries = scale * jax.random.normal(stream_key, extent, jnp.float32)
    if cuts:
        entries = entries * levels(stream_key, extent, cuts, -0.22, 0.18)
    return jnp.clip(entries, -bound, bound).astype(dtype)


def setup_inputs(seed: int = 0) -> dict:
    arg_keys = jax.random.split(jax.random.key(seed), 13)
    tokens = noise(arg_keys[0], (MB, SEQS, LEN, D), 1.0, 6.0, ((1, 2), (2, 16)))
    cotangent = noise(arg_keys[1], (MB, SEQS, LEN, D), 1.0, 6.0, ((1, 2), (2, 16)))
    segments = jax.vmap(lambda own: jnp.searchsorted(jnp.cumsum(ragged_sizes(own, DOCS, LEN, DOC_MOST, 2)), jnp.arange(LEN), side="right"))(jax.random.split(arg_keys[2], MB * SEQS)).reshape((MB, SEQS, LEN)).astype(jnp.int32)
    norm_gain = jnp.clip(1.0 + 0.1 * jax.random.normal(arg_keys[3], (D,), jnp.float32), 0.5, 1.5).astype(jnp.bfloat16)
    w_in = noise(arg_keys[4], (D, E), D ** -0.5, 0.21875, ((0, 16),))
    conv_weight = noise(arg_keys[5], (KC, CH), KC ** -0.5, 3.0, ((1, 16),))
    conv_bias = noise(arg_keys[6], (CH,), 0.3, 1.75, ((0, 16),))
    step_bias = jnp.clip(jax.random.uniform(arg_keys[7], (H,), jnp.float32, -6.0, -2.0), -6.0, -2.0)
    log_rate = draw_log_rate(jax.random.fold_in(arg_keys[12], 71), 0)
    skip_gain = jnp.clip(jax.random.uniform(arg_keys[9], (H,), jnp.float32, 0.5, 1.5), 0.5, 1.5)
    gate_gain = jnp.clip(1.0 + 0.1 * jax.random.normal(arg_keys[10], (DI,), jnp.float32), 0.5, 1.5).astype(jnp.bfloat16)
    w_out = noise(arg_keys[11], (DI, D), DI ** -0.5, 0.15625, ((0, 16),))
    return {"tokens": tokens, "cotangent": cotangent, "segments": segments, "norm_gain": norm_gain, "w_in": w_in, "conv_weight": conv_weight, "conv_bias": conv_bias, "step_bias": step_bias, "log_rate": log_rate, "skip_gain": skip_gain, "gate_gain": gate_gain, "w_out": w_out}


@jax.custom_vjp
def low(v):
    return lax.optimization_barrier(v.astype(jnp.bfloat16)).astype(jnp.float32)

@jax.custom_vjp
def low_back(v):
    return v

def low_keep(v):
    return (low(v), None)

def low_pass(kept, grad):
    return (grad,)

def back_keep(v):
    return (v, None)

def back_low(kept, grad):
    return (low(grad),)
low.defvjp(low_keep, low_pass)
low_back.defvjp(back_keep, back_low)
EPSILON = 1e-05
HIGHEST = lax.Precision.HIGHEST

def rms_scale(values, gain_vec):
    return values * lax.rsqrt(lax.optimization_barrier(jnp.mean(values * values, axis=-1, keepdims=True)) + EPSILON) * gain_vec

def causal_conv(padded, seg_pad, seg_one, kernel, offset):
    length_t = seg_one.shape[0]
    total = jnp.zeros((length_t, padded.shape[1]), jnp.float32) + offset[None, :]
    for tap_index in range(KC):
        window = padded[tap_index:tap_index + length_t]
        same_doc = (seg_pad[tap_index:tap_index + length_t] == seg_one).astype(jnp.float32)
        total = total + kernel[tap_index][None, :] * window * same_doc[:, None]
    return total

def cumulative(step_size, rate):
    return jnp.cumsum(step_size * rate[None, :], axis=0)

def block_state(inner, b_proj, step_size, rate, seg_one, previous):
    cum_decay = cumulative(step_size, rate)
    last_seg = seg_one[-1]
    to_end = jnp.where((seg_one == last_seg)[:, None], jnp.exp(cum_decay[-1][None, :] - cum_decay), 0.0) * step_size
    state_part = jnp.einsum('uhp,un->hpn', inner * to_end[:, :, None], b_proj, precision=HIGHEST)
    through = jnp.logical_and(seg_one[0] == last_seg, seg_one[0] == previous).astype(jnp.float32)
    return (state_part, jnp.exp(cum_decay[-1]) * through)

def block_output(inner, b_proj, c_proj, step_size, rate, state_in, seg_one, previous):
    cum_decay = cumulative(step_size, rate)
    length_t = seg_one.shape[0]
    row_index = lax.broadcasted_iota(jnp.int32, (length_t, length_t), 0)
    col_index = lax.broadcasted_iota(jnp.int32, (length_t, length_t), 1)
    allowed = jnp.logical_and(row_index >= col_index, seg_one[:, None] == seg_one[None, :])[:, :, None]
    spread = cum_decay[:, None, :] - cum_decay[None, :, :]
    decays = jnp.where(allowed, jnp.exp(jnp.where(allowed, spread, 0.0)), 0.0)
    scores = jnp.dot(c_proj, b_proj.T, precision=HIGHEST)
    weights = decays * scores[:, :, None] * step_size[None, :, :]
    local_part = jnp.einsum('tuh,uhp->thp', weights, inner, precision=HIGHEST)
    carried = (seg_one == previous).astype(jnp.float32)[:, None] * jnp.exp(cum_decay)
    return local_part + carried[:, :, None] * jnp.einsum('tn,hpn->thp', c_proj, state_in, precision=HIGHEST)

def sequence_layer(resid, seg_one, norm_gain, w_in, conv_weight, conv_bias, step_bias, log_rate, skip_gain, gate_gain, w_out):
    normed = low(rms_scale(resid, norm_gain))
    proj_out = low_back(jnp.dot(normed, w_in, precision=HIGHEST))
    gate_in = proj_out[:, :DI]
    xbc_cols = proj_out[:, DI:DI + CH]
    padded = jnp.concatenate([jnp.zeros((KC - 1, CH), jnp.float32), xbc_cols], axis=0)
    seg_pad = jnp.concatenate([jnp.zeros((KC - 1,), jnp.float32), seg_one])
    activated = jax.nn.silu(causal_conv(padded, seg_pad, seg_one, conv_weight, conv_bias))
    inner = activated[:, :DI].reshape(LEN, H, P_SIZE)
    b_proj = activated[:, DI:DI + N]
    c_proj = activated[:, DI + N:]
    step_size = jax.nn.softplus(proj_out[:, DI + CH:] + step_bias[None, :])
    rate = -jnp.exp(log_rate)
    blocks = LEN // L_DEV
    pieces = (inner.reshape(blocks, L_DEV, H, P_SIZE), b_proj.reshape(blocks, L_DEV, N), c_proj.reshape(blocks, L_DEV, N), step_size.reshape(blocks, L_DEV, H), seg_one.reshape(blocks, L_DEV))

    def advance(carry, piece):
        state_in, previous = carry
        inner_b, b_b, c_b, step_b, seg_b = piece
        mixed_b = block_output(inner_b, b_b, c_b, step_b, rate, state_in, seg_b, previous)
        state_part, through = block_state(inner_b, b_b, step_b, rate, seg_b, previous)
        return ((through[:, None, None] * state_in + state_part, seg_b[-1]), mixed_b)
    start = (jnp.zeros((H, P_SIZE, N), jnp.float32), jnp.zeros((), jnp.float32))
    _, mixed = lax.scan(jax.checkpoint(advance), start, pieces)
    mixed = mixed.reshape(LEN, H, P_SIZE) + skip_gain[None, :, None] * inner
    gated = mixed.reshape(LEN, DI) * jax.nn.silu(gate_in)
    gated_low = low(rms_scale(gated, gate_gain))
    branch = low_back(jnp.dot(gated_low, w_out, precision=HIGHEST))
    return resid + branch

def reference(tokens, cotangent, segments, norm_gain, w_in, conv_weight, conv_bias, step_bias, log_rate, skip_gain, gate_gain, w_out):
    params = (norm_gain.astype(jnp.float32), w_in.astype(jnp.float32), conv_weight.astype(jnp.float32), conv_bias.astype(jnp.float32), step_bias.astype(jnp.float32), log_rate.astype(jnp.float32), skip_gain.astype(jnp.float32), gate_gain.astype(jnp.float32), w_out.astype(jnp.float32))
    inputs = tokens.astype(jnp.float32).reshape(MB * SEQS, LEN, D)
    seg_all = segments.reshape(MB * SEQS, LEN).astype(jnp.float32) + 1.0
    cot_all = cotangent.astype(jnp.float32).reshape(MB * SEQS, LEN, D)

    def forward(inputs_f, params_f):

        def one_seq(carry, item):
            resid, seg_one = item
            return (carry, sequence_layer(resid, seg_one, *params_f))
        _, outputs = lax.scan(jax.checkpoint(one_seq), jnp.zeros((), jnp.float32), (inputs_f, seg_all))
        return outputs
    outputs, pullback = jax.vjp(forward, inputs, params)
    grad_inputs, grad_params = pullback(cot_all)
    activations = outputs.reshape(MB, SEQS, LEN, D).astype(jnp.bfloat16)
    grad_tokens = grad_inputs.reshape(MB, SEQS, LEN, D).astype(jnp.bfloat16)
    return (activations, grad_tokens, grad_params[0], grad_params[1], grad_params[2], grad_params[3], grad_params[4], grad_params[5], grad_params[6], grad_params[7], grad_params[8])
```

```python
import functools
from functools import partial

import jax
import jax.numpy as jnp
from jax import lax
from jax.experimental import pallas as pl
from jax.experimental.pallas import tpu as pltpu
from jax.sharding import PartitionSpec as P

DI = 1536
H = 24
P_SIZE = 64
N = 128
KC = 4
CH = 1792


MESH = pl.DeviceIdType.MESH


def chip(x, y, z):
    return z * 4 + y * 2 + x


def place():
    core = lax.axis_index("dp")
    at = lax.axis_index("seq")
    return at % 2, (at // 2) % 2, at // 4, core


def meet_all(planes):
    barrier = pltpu.get_barrier_semaphore()
    me = lax.axis_index("seq")
    core = lax.axis_index("dp")
    count = planes * 4

    def greet(k, carry):
        other = lax.rem(me + k, count)
        for far in range(2):

            @pl.when(jnp.logical_or(k > 0, far != core))
            def _():
                pl.semaphore_signal(barrier, inc=1, device_id=(far, other), device_id_type=MESH)

        return carry

    lax.fori_loop(0, count, greet, 0)
    pl.semaphore_wait(barrier, 2 * count - 1)


UP, DOWN, SIDE_X, SIDE_Y, HALF_X, HALF_Y, MATE_Z, MATE_X, MATE_Y, MATE_HX, MATE_HY = range(11)


class Gather:
    def __init__(self, whole, rows, quarter, sems, planes):
        self.whole, self.rows, self.quarter, self.sems, self.planes = whole, rows, quarter, sems, planes
        self.x, self.y, self.z, self.core = place()

    def region(self, block, core, part=None):
        width = self.whole.shape[1] // 2
        start = pl.multiple_of(block * self.rows, 16)
        left = pl.multiple_of(core * width, 128)
        if part is None:
            return self.whole.at[pl.ds(start, self.rows), pl.ds(left, width)]
        if self.quarter == "rows":
            half = self.rows // 2
            return self.whole.at[pl.ds(pl.multiple_of(start + part * half, 16), half), pl.ds(left, width)]
        half = width // 2
        return self.whole.at[pl.ds(start, self.rows), pl.ds(pl.multiple_of(left + part * half, 128), half)]

    def copy(self, kind, far, block, core, part, device):
        region = self.region(block, core, part)
        return pltpu.make_async_remote_copy(
            src_ref=region,
            dst_ref=region,
            send_sem=self.sems.at[0, kind, far],
            recv_sem=self.sems.at[1, kind, far],
            device_id=device,
            device_id_type=MESH,
        )

    def transfers(self, far):
        x, y, z, c = self.x, self.y, self.z, self.core
        own = chip(x, y, far)
        by_x, by_y, across = chip(1 - x, y, far), chip(x, 1 - y, far), chip(1 - x, 1 - y, far)
        mate = (1 - c, chip(x, y, z))
        to_x, to_y = (c, chip(1 - x, y, z)), (c, chip(x, 1 - y, z))
        return {
            UP: (own, None, (c, chip(x, y, z + 1))),
            DOWN: (own, None, (c, chip(x, y, z - 1))),
            SIDE_X: (own, None, to_x),
            SIDE_Y: (own, None, to_y),
            HALF_X: (by_y, 1, to_x),
            HALF_Y: (by_x, 0, to_y),
            MATE_Z: (own, None, mate),
            MATE_X: (by_x, None, mate),
            MATE_Y: (by_y, None, mate),
            MATE_HX: (across, 1, mate),
            MATE_HY: (across, 0, mate),
        }

    def send(self, kind, far):
        block, part, device = self.transfers(far)[kind]
        self.copy(kind, far, block, self.core, part, device).start()

    def sent(self, kind, far):
        block, part, device = self.transfers(far)[kind]
        self.copy(kind, far, block, self.core, part, device).wait_send()

    def arrived(self, kind, far):
        x, y = self.x, self.y
        block, part, core = {
            UP: (chip(x, y, far), None, 0),
            DOWN: (chip(x, y, far), None, 0),
            SIDE_X: (chip(1 - x, y, far), None, 0),
            SIDE_Y: (chip(x, 1 - y, far), None, 0),
            HALF_X: (chip(1 - x, 1 - y, far), 1, 0),
            HALF_Y: (chip(1 - x, 1 - y, far), 0, 0),
            MATE_Z: (chip(x, y, far), None, 1),
            MATE_X: (chip(1 - x, y, far), None, 1),
            MATE_Y: (chip(x, 1 - y, far), None, 1),
            MATE_HX: (chip(1 - x, 1 - y, far), 1, 1),
            MATE_HY: (chip(1 - x, 1 - y, far), 0, 1),
        }[kind]
        owner = self.core if core == 0 else 1 - self.core
        self.copy(kind, far, block, owner, part, (1 - self.core, chip(x, y, self.z))).wait_recv()

    def each(self, distance, act):
        for sign in (-1, 1) if distance else (1,):
            far = self.z + sign * distance
            if distance:
                pl.when(jnp.logical_and(far >= 0, far < self.planes))(functools.partial(act, far, sign))
            else:
                act(far, sign)

    def column(self, distance):
        def act(far, sign):
            if distance:
                self.arrived(UP if sign < 0 else DOWN, far)
            if sign < 0 or not distance:
                pl.when(self.z < self.planes - 1)(lambda: self.send(UP, far))
            if sign > 0:
                pl.when(self.z > 0)(lambda: self.send(DOWN, far))
            self.send(SIDE_X, far)
            self.send(SIDE_Y, far)
            if distance:
                self.send(MATE_Z, far)

        self.each(distance, act)

    def sides(self, distance):
        def act(far, sign):
            self.arrived(SIDE_X, far)
            self.send(HALF_Y, far)
            self.send(MATE_X, far)
            self.arrived(SIDE_Y, far)
            self.send(HALF_X, far)
            self.send(MATE_Y, far)

        self.each(distance, act)

    def diagonal(self, distance):
        def act(far, sign):
            self.arrived(HALF_Y, far)
            self.send(MATE_HY, far)
            self.arrived(HALF_X, far)
            self.send(MATE_HX, far)

        self.each(distance, act)

    def finish(self):
        for distance in range(self.planes):

            def act(far, sign):
                if sign < 0 or not distance:
                    pl.when(self.z < self.planes - 1)(lambda: self.sent(UP, far))
                if sign > 0:
                    pl.when(self.z > 0)(lambda: self.sent(DOWN, far))
                for kind in (SIDE_X, SIDE_Y, HALF_X, HALF_Y, MATE_X, MATE_Y, MATE_HX, MATE_HY):
                    self.sent(kind, far)
                for kind in (MATE_X, MATE_Y, MATE_HX, MATE_HY):
                    self.arrived(kind, far)
                if distance:
                    self.sent(MATE_Z, far)
                    self.arrived(MATE_Z, far)

            self.each(distance, act)

    def steps(self):
        do = [lambda: self.column(0), lambda: self.column(1), lambda: self.sides(0), lambda: self.column(2), lambda: self.diagonal(0),
              lambda: self.sides(1), lambda: self.column(3), lambda: self.diagonal(1), lambda: self.sides(2), lambda: self.diagonal(2),
              lambda: self.sides(3), lambda: self.diagonal(3)]
        return do


def gather_sems(planes):
    return pltpu.SemaphoreType.DMA((2, 11, planes))


def gather_kernel(planes, in_ref, out_ref, in_full, out_full, in_sems, out_sems):
    at = lax.axis_index("seq")
    for ref, full in ((in_ref, in_full), (out_ref, out_full)):
        rows = ref.shape[0]
        full[pl.ds(pl.multiple_of(at * rows, 16), rows), :] = ref[...]
    first = Gather(in_full, in_ref.shape[0], "columns", in_sems, planes)
    second = Gather(out_full, out_ref.shape[0], "rows", out_sems, planes)
    meet_all(planes)
    for step in first.steps():
        step()
    for step in second.steps():
        step()
    first.finish()
    second.finish()


def gather_weights(w_in, w_out):
    count = lax.axis_size("seq")
    if count != 16:
        return tuple(lax.all_gather(w, "seq", axis=0, tiled=True) for w in (w_in, w_out))
    wide = jnp.pad(w_in, ((0, 0), (0, 3584 - w_in.shape[1])))
    whole = [jax.ShapeDtypeStruct((w.shape[0] * count, w.shape[1]), w.dtype) for w in (wide, w_out)]
    vmem = pl.BlockSpec(memory_space=pltpu.VMEM)
    full, out = pl.pallas_call(
        functools.partial(gather_kernel, count // 4),
        out_shape=whole,
        in_specs=[vmem, vmem],
        out_specs=[vmem, vmem],
        scratch_shapes=[gather_sems(count // 4), gather_sems(count // 4)],
        compiler_params=pltpu.CompilerParams(collective_id=0, has_side_effects=True, vmem_limit_bytes=40 << 20),
    )(wide, w_out)
    return full[:, : w_in.shape[1]], out


EPSILON = 1e-05
HIGHEST = lax.Precision.HIGHEST


def passed_along(array, axis, by):
    devices = lax.axis_size(axis)
    pairs = [(i, i + by) for i in range(devices) if 0 <= i + by < devices]
    return lax.ppermute(array, axis, pairs)


def prefix(array, axis, combine, identity, reverse):
    devices, place = (lax.axis_size(axis), lax.axis_index(axis))
    everything = jax.tree.map(lambda part: lax.all_gather(part, axis), array)
    start = jax.tree.map(
        lambda part, zero: jnp.broadcast_to(jnp.asarray(zero, part.dtype), part.shape),
        array,
        identity,
    )

    def lap(k, before):
        at = devices - 1 - k if reverse else k
        reached = at > place if reverse else at < place
        new = combine(before, jax.tree.map(lambda part: part[at], everything))
        return jax.tree.map(lambda a, b: jnp.where(reached, a, b), new, before)

    return lax.fori_loop(0, devices, lap, start)


def for_sending(array):
    return jax.tree.map(lambda a: a.astype(jnp.bfloat16) if a.dtype == jnp.float32 else a, array)


def rms_scale(values, gain_vec):
    return (
        values * lax.rsqrt(jnp.mean(values * values, axis=-1, keepdims=True) + EPSILON) * gain_vec
    )


def causal_conv(padded, seg_pad, seg_one, kernel, offset):
    length_t = seg_one.shape[0]
    total = jnp.zeros((length_t, padded.shape[1]), jnp.float32) + offset[None, :]
    for tap_index in range(KC):
        window = padded[tap_index : tap_index + length_t]
        same_doc = (seg_pad[tap_index : tap_index + length_t] == seg_one).astype(jnp.float32)
        total = total + kernel[tap_index][None, :] * window * same_doc[:, None]
    return total


def cumulative(step_size, rate):
    length_t = step_size.shape[0]
    lower = jnp.tril(jnp.ones((length_t, length_t), jnp.float32))
    return jnp.dot(lower, step_size * rate[None, :], precision=HIGHEST)


def block_state(inner, b_proj, step_size, rate, seg_one, previous):
    cum_decay = cumulative(step_size, rate)
    last_seg = seg_one[-1]
    to_end = (
        jnp.where((seg_one == last_seg)[:, None], jnp.exp(cum_decay[-1][None, :] - cum_decay), 0.0)
        * step_size
    )
    state_part = jnp.einsum("uhp,un->hpn", inner * to_end[:, :, None], b_proj, precision=HIGHEST)
    through = jnp.logical_and(seg_one[0] == last_seg, seg_one[0] == previous).astype(jnp.float32)
    return (state_part, jnp.exp(cum_decay[-1]) * through)


def block_output(inner, b_proj, c_proj, step_size, rate, state_in, seg_one, previous):
    cum_decay = cumulative(step_size, rate)
    length_t = seg_one.shape[0]
    row_index = lax.broadcasted_iota(jnp.int32, (length_t, length_t), 0)
    col_index = lax.broadcasted_iota(jnp.int32, (length_t, length_t), 1)
    allowed = jnp.logical_and(row_index >= col_index, seg_one[:, None] == seg_one[None, :])[
        :, :, None
    ]
    spread = cum_decay[:, None, :] - cum_decay[None, :, :]
    decays = jnp.where(allowed, jnp.exp(jnp.where(allowed, spread, 0.0)), 0.0)
    scores = jnp.dot(c_proj, b_proj.T, precision=HIGHEST)
    weights = decays * scores[:, :, None] * step_size[None, :, :]
    local_part = jnp.einsum("tuh,uhp->thp", weights, inner, precision=HIGHEST)
    carried = (seg_one == previous).astype(jnp.float32)[:, None] * jnp.exp(cum_decay)
    return local_part + carried[:, :, None] * jnp.einsum(
        "tn,hpn->thp", c_proj, state_in, precision=HIGHEST
    )


def prepare(proj_out, tail_rows, kernel, offset, step_bias, log_rate, tail_seg, seg_one):
    length_t = proj_out.shape[0]
    padded = jnp.concatenate([tail_rows, proj_out[:, DI : DI + CH]], axis=0)
    seg_pad = jnp.concatenate([tail_seg, seg_one])
    activated = jax.nn.silu(causal_conv(padded, seg_pad, seg_one, kernel, offset))
    inner = activated[:, :DI].reshape(length_t, H, P_SIZE)
    b_proj = activated[:, DI : DI + N]
    c_proj = activated[:, DI + N :]
    step_size = jax.nn.softplus(proj_out[:, DI + CH :] + step_bias[None, :])
    rate = -jnp.exp(log_rate)
    return (inner, b_proj, c_proj, step_size, rate, proj_out[:, :DI])


def finish(
    inner,
    b_proj,
    c_proj,
    step_size,
    rate,
    gate_in,
    state_in,
    skip_gain,
    gate_gain,
    seg_one,
    previous,
):
    length_t = inner.shape[0]
    mixed = block_output(inner, b_proj, c_proj, step_size, rate, state_in, seg_one, previous)
    mixed = mixed + skip_gain[None, :, None] * inner
    gated = mixed.reshape(length_t, DI) * jax.nn.silu(gate_in)
    return rms_scale(gated, gate_gain)


def chain_link(earlier, later):
    return (earlier[0] * later[0], later[0][:, None, None] * earlier[1] + later[1])


def body(
    tokens,
    cotangent,
    segments,
    norm_gain,
    w_in,
    conv_weight,
    conv_bias,
    step_bias,
    log_rate,
    skip_gain,
    gate_gain,
    w_out,
):
    batches = tokens.shape[0]
    length_t = tokens.shape[2]
    halo_rows = KC - 1
    identity = (jnp.ones((H,), jnp.float32), jnp.zeros((H, P_SIZE, N), jnp.float32))
    totals = None
    head_totals = (
        jnp.zeros((H,), jnp.float32),
        jnp.zeros((H,), jnp.float32),
        jnp.zeros((H,), jnp.float32),
    )
    act_list = []
    grad_list = []
    both = gather_weights(w_in, w_out)
    for micro in range(batches):
        gathered = (
            both[0],
            both[1],
            lax.all_gather(conv_weight, "seq", axis=1, tiled=True),
            lax.all_gather(conv_bias, "seq", axis=0, tiled=True),
            lax.all_gather(norm_gain, "seq", axis=0, tiled=True),
            lax.all_gather(gate_gain, "seq", axis=0, tiled=True),
        )
        in_full = gathered[0]
        out_full = gathered[1]
        kernel = gathered[2].astype(jnp.float32)
        offset = gathered[3].astype(jnp.float32)
        gain_one = gathered[4].astype(jnp.float32)
        gain_two = gathered[5].astype(jnp.float32)
        resid = tokens[micro, 0].astype(jnp.float32)
        seg_one = segments[micro, 0].astype(jnp.float32) + 1.0
        normed, norm_back = jax.vjp(rms_scale, resid, gain_one)
        normed_low = normed.astype(jnp.bfloat16)
        proj_out = jnp.dot(normed_low, in_full, preferred_element_type=jnp.float32)
        tail_rows, tail_seg = passed_along(
            (proj_out[length_t - halo_rows :, DI : DI + CH], seg_one[length_t - halo_rows :]),
            "seq",
            1,
        )
        previous = tail_seg[halo_rows - 1]
        prepared, prep_back = jax.vjp(
            partial(prepare, tail_seg=tail_seg, seg_one=seg_one),
            proj_out,
            tail_rows,
            kernel,
            offset,
            step_bias,
            log_rate,
        )
        inner, b_proj, c_proj, step_size, rate, gate_in = prepared
        state_out, state_back = jax.vjp(
            partial(block_state, seg_one=seg_one, previous=previous), inner, b_proj, step_size, rate
        )
        state_part, through = state_out
        state_in = prefix((through, state_part), "seq", chain_link, identity, False)[1]
        normed_two, finish_back = jax.vjp(
            partial(finish, seg_one=seg_one, previous=previous),
            inner,
            b_proj,
            c_proj,
            step_size,
            rate,
            gate_in,
            state_in,
            skip_gain,
            gain_two,
        )
        gate_low = normed_two.astype(jnp.bfloat16)
        branch = jnp.dot(gate_low, out_full, preferred_element_type=jnp.float32)
        act_list.append((resid + branch).astype(jnp.bfloat16))
        cot_low = cotangent[micro, 0]
        again = both
        in_back = again[0]
        out_back = again[1]
        out_term = lax.dot_general(
            gate_low, cot_low, (((0,), (0,)), ((), ())), preferred_element_type=jnp.float32
        )
        grad_gate = lax.dot_general(
            cot_low, out_back, (((1,), (1,)), ((), ())), preferred_element_type=jnp.float32
        )
        g_inner, g_bproj, g_cproj, g_step, g_rate, g_gate_in, g_state_in, g_skip, g_gain_two = (
            finish_back(grad_gate)
        )
        carried = prefix((through, g_state_in), "seq", chain_link, identity, True)[1]
        h_inner, h_bproj, h_step, h_rate = state_back(
            (carried, jnp.sum(carried * state_in, axis=(1, 2)))
        )
        g_proj, g_tail, g_kernel, g_offset, g_bias, g_log = prep_back(
            (
                g_inner + h_inner,
                g_bproj + h_bproj,
                g_cproj,
                g_step + h_step,
                g_rate + h_rate,
                g_gate_in,
            )
        )
        returned = passed_along(g_tail, "seq", -1)
        width_after = proj_out.shape[1] - DI - CH
        g_proj = g_proj + jnp.pad(returned, ((length_t - halo_rows, 0), (DI, width_after)))
        proj_grad_low = g_proj.astype(jnp.bfloat16)
        grad_normed = lax.dot_general(
            proj_grad_low, in_back, (((1,), (1,)), ((), ())), preferred_element_type=jnp.float32
        )
        grad_resid, g_gain_one = norm_back(grad_normed)
        grad_list.append((cot_low.astype(jnp.float32) + grad_resid).astype(jnp.bfloat16))
        in_shard = lax.psum_scatter(
            lax.dot_general(
                normed_low,
                proj_grad_low,
                (((0,), (0,)), ((), ())),
                preferred_element_type=jnp.float32,
            ),
            "seq",
            scatter_dimension=0,
            tiled=True,
        )
        shards = (
            lax.psum_scatter(out_term, "seq", scatter_dimension=0, tiled=True),
            lax.psum_scatter(g_kernel, "seq", scatter_dimension=1, tiled=True),
            lax.psum_scatter(g_offset, "seq", scatter_dimension=0, tiled=True),
            lax.psum_scatter(g_gain_one, "seq", scatter_dimension=0, tiled=True),
            lax.psum_scatter(g_gain_two, "seq", scatter_dimension=0, tiled=True),
        )
        this_round = (in_shard, shards[0], shards[1], shards[2], shards[3], shards[4])
        if totals is None:
            totals = this_round
        else:
            totals = tuple((prior + fresh for prior, fresh in zip(totals, this_round)))
        head_totals = (head_totals[0] + g_bias, head_totals[1] + g_log, head_totals[2] + g_skip)
    summed = jax.tree.map(
        lambda part: part.astype(jnp.float32), lax.psum(for_sending(totals), "dp")
    )
    heads = lax.psum((head_totals[0], head_totals[1], head_totals[2]), ("dp", "seq"))
    activations = jnp.stack(act_list)[:, None]
    grad_tokens = jnp.stack(grad_list)[:, None]
    return (
        activations,
        grad_tokens,
        summed[4],
        summed[0],
        summed[2],
        summed[3],
        heads[0],
        heads[1],
        heads[2],
        summed[5],
        summed[1],
    )


def solution(mesh):
    in_specs = (
        P(None, "dp", "seq", None),
        P(None, "dp", "seq", None),
        P(None, "dp", "seq"),
        P("seq"),
        P("seq", None),
        P(None, "seq"),
        P("seq"),
        P(),
        P(),
        P(),
        P("seq"),
        P("seq", None),
    )
    out_specs = (
        P(None, "dp", "seq", None),
        P(None, "dp", "seq", None),
        P("seq"),
        P("seq", None),
        P(None, "seq"),
        P("seq"),
        P(),
        P(),
        P(),
        P("seq"),
        P("seq", None),
    )
    return jax.shard_map(body, mesh=mesh, in_specs=in_specs, out_specs=out_specs, check_vma=False)
```

```python
import functools
from functools import partial

import jax
import jax.numpy as jnp
from jax import lax
from jax.experimental import pallas as pl
from jax.experimental.pallas import tpu as pltpu
from jax.sharding import PartitionSpec as P

DI = 1536
H = 24
P_SIZE = 64
N = 128
KC = 4
CH = 1792


EPSILON = 1e-05
HIGHEST = lax.Precision.HIGHEST


def passed_along(array, axis, by):
    devices = lax.axis_size(axis)
    pairs = [(i, i + by) for i in range(devices) if 0 <= i + by < devices]
    return lax.ppermute(array, axis, pairs)


def prefix(array, axis, combine, identity, reverse):
    devices, place = (lax.axis_size(axis), lax.axis_index(axis))
    everything = jax.tree.map(lambda part: lax.all_gather(part, axis), array)
    start = jax.tree.map(
        lambda part, zero: jnp.broadcast_to(jnp.asarray(zero, part.dtype), part.shape),
        array,
        identity,
    )

    def lap(k, before):
        at = devices - 1 - k if reverse else k
        reached = at > place if reverse else at < place
        new = combine(before, jax.tree.map(lambda part: part[at], everything))
        return jax.tree.map(lambda a, b: jnp.where(reached, a, b), new, before)

    return lax.fori_loop(0, devices, lap, start)


def for_sending(array):
    return jax.tree.map(lambda a: a.astype(jnp.bfloat16) if a.dtype == jnp.float32 else a, array)


def rms_scale(values, gain_vec):
    return (
        values * lax.rsqrt(jnp.mean(values * values, axis=-1, keepdims=True) + EPSILON) * gain_vec
    )


def causal_conv(padded, seg_pad, seg_one, kernel, offset):
    length_t = seg_one.shape[0]
    total = jnp.zeros((length_t, padded.shape[1]), jnp.float32) + offset[None, :]
    for tap_index in range(KC):
        window = padded[tap_index : tap_index + length_t]
        same_doc = (seg_pad[tap_index : tap_index + length_t] == seg_one).astype(jnp.float32)
        total = total + kernel[tap_index][None, :] * window * same_doc[:, None]
    return total


def cumulative(step_size, rate):
    length_t = step_size.shape[0]
    lower = jnp.tril(jnp.ones((length_t, length_t), jnp.float32))
    return jnp.dot(lower, step_size * rate[None, :], precision=HIGHEST)


def block_state(inner, b_proj, step_size, rate, seg_one, previous):
    cum_decay = cumulative(step_size, rate)
    last_seg = seg_one[-1]
    to_end = (
        jnp.where((seg_one == last_seg)[:, None], jnp.exp(cum_decay[-1][None, :] - cum_decay), 0.0)
        * step_size
    )
    state_part = jnp.einsum("uhp,un->hpn", inner * to_end[:, :, None], b_proj, precision=HIGHEST)
    through = jnp.logical_and(seg_one[0] == last_seg, seg_one[0] == previous).astype(jnp.float32)
    return (state_part, jnp.exp(cum_decay[-1]) * through)


def block_output(inner, b_proj, c_proj, step_size, rate, state_in, seg_one, previous):
    cum_decay = cumulative(step_size, rate)
    length_t = seg_one.shape[0]
    row_index = lax.broadcasted_iota(jnp.int32, (length_t, length_t), 0)
    col_index = lax.broadcasted_iota(jnp.int32, (length_t, length_t), 1)
    allowed = jnp.logical_and(row_index >= col_index, seg_one[:, None] == seg_one[None, :])[
        :, :, None
    ]
    spread = cum_decay[:, None, :] - cum_decay[None, :, :]
    decays = jnp.where(allowed, jnp.exp(jnp.where(allowed, spread, 0.0)), 0.0)
    scores = jnp.dot(c_proj, b_proj.T, precision=HIGHEST)
    weights = decays * scores[:, :, None] * step_size[None, :, :]
    local_part = jnp.einsum("tuh,uhp->thp", weights, inner, precision=HIGHEST)
    carried = (seg_one == previous).astype(jnp.float32)[:, None] * jnp.exp(cum_decay)
    return local_part + carried[:, :, None] * jnp.einsum(
        "tn,hpn->thp", c_proj, state_in, precision=HIGHEST
    )


def prepare(proj_out, tail_rows, kernel, offset, step_bias, log_rate, tail_seg, seg_one):
    length_t = proj_out.shape[0]
    padded = jnp.concatenate([tail_rows, proj_out[:, DI : DI + CH]], axis=0)
    seg_pad = jnp.concatenate([tail_seg, seg_one])
    activated = jax.nn.silu(causal_conv(padded, seg_pad, seg_one, kernel, offset))
    inner = activated[:, :DI].reshape(length_t, H, P_SIZE)
    b_proj = activated[:, DI : DI + N]
    c_proj = activated[:, DI + N :]
    step_size = jax.nn.softplus(proj_out[:, DI + CH :] + step_bias[None, :])
    rate = -jnp.exp(log_rate)
    return (inner, b_proj, c_proj, step_size, rate, proj_out[:, :DI])


def finish(
    inner,
    b_proj,
    c_proj,
    step_size,
    rate,
    gate_in,
    state_in,
    skip_gain,
    gate_gain,
    seg_one,
    previous,
):
    length_t = inner.shape[0]
    mixed = block_output(inner, b_proj, c_proj, step_size, rate, state_in, seg_one, previous)
    mixed = mixed + skip_gain[None, :, None] * inner
    gated = mixed.reshape(length_t, DI) * jax.nn.silu(gate_in)
    return rms_scale(gated, gate_gain)


def chain_link(earlier, later):
    return (earlier[0] * later[0], later[0][:, None, None] * earlier[1] + later[1])


def body(
    tokens,
    cotangent,
    segments,
    norm_gain,
    w_in,
    conv_weight,
    conv_bias,
    step_bias,
    log_rate,
    skip_gain,
    gate_gain,
    w_out,
):
    batches = tokens.shape[0]
    length_t = tokens.shape[2]
    halo_rows = KC - 1
    identity = (jnp.ones((H,), jnp.float32), jnp.zeros((H, P_SIZE, N), jnp.float32))
    totals = None
    head_totals = (
        jnp.zeros((H,), jnp.float32),
        jnp.zeros((H,), jnp.float32),
        jnp.zeros((H,), jnp.float32),
    )
    act_list = []
    grad_list = []
    for micro in range(batches):
        gathered = (
            lax.all_gather(w_in, "seq", axis=0, tiled=True),
            lax.all_gather(w_out, "seq", axis=0, tiled=True),
            lax.all_gather(conv_weight, "seq", axis=1, tiled=True),
            lax.all_gather(conv_bias, "seq", axis=0, tiled=True),
            lax.all_gather(norm_gain, "seq", axis=0, tiled=True),
            lax.all_gather(gate_gain, "seq", axis=0, tiled=True),
        )
        in_full = gathered[0]
        out_full = gathered[1]
        kernel = gathered[2].astype(jnp.float32)
        offset = gathered[3].astype(jnp.float32)
        gain_one = gathered[4].astype(jnp.float32)
        gain_two = gathered[5].astype(jnp.float32)
        resid = tokens[micro, 0].astype(jnp.float32)
        seg_one = segments[micro, 0].astype(jnp.float32) + 1.0
        normed, norm_back = jax.vjp(rms_scale, resid, gain_one)
        normed_low = normed.astype(jnp.bfloat16)
        proj_out = jnp.dot(normed_low, in_full, preferred_element_type=jnp.float32)
        tail_rows, tail_seg = passed_along(
            (proj_out[length_t - halo_rows :, DI : DI + CH], seg_one[length_t - halo_rows :]),
            "seq",
            1,
        )
        previous = tail_seg[halo_rows - 1]
        prepared, prep_back = jax.vjp(
            partial(prepare, tail_seg=tail_seg, seg_one=seg_one),
            proj_out,
            tail_rows,
            kernel,
            offset,
            step_bias,
            log_rate,
        )
        inner, b_proj, c_proj, step_size, rate, gate_in = prepared
        state_out, state_back = jax.vjp(
            partial(block_state, seg_one=seg_one, previous=previous), inner, b_proj, step_size, rate
        )
        state_part, through = state_out
        state_in = prefix((through, state_part), "seq", chain_link, identity, False)[1]
        normed_two, finish_back = jax.vjp(
            partial(finish, seg_one=seg_one, previous=previous),
            inner,
            b_proj,
            c_proj,
            step_size,
            rate,
            gate_in,
            state_in,
            skip_gain,
            gain_two,
        )
        gate_low = normed_two.astype(jnp.bfloat16)
        branch = jnp.dot(gate_low, out_full, preferred_element_type=jnp.float32)
        act_list.append((resid + branch).astype(jnp.bfloat16))
        cot_low = cotangent[micro, 0]
        again = (
            lax.all_gather(w_in, "seq", axis=0, tiled=True),
            lax.all_gather(w_out, "seq", axis=0, tiled=True),
        )
        in_back = again[0]
        out_back = again[1]
        out_term = lax.dot_general(
            gate_low, cot_low, (((0,), (0,)), ((), ())), preferred_element_type=jnp.float32
        )
        grad_gate = lax.dot_general(
            cot_low, out_back, (((1,), (1,)), ((), ())), preferred_element_type=jnp.float32
        )
        g_inner, g_bproj, g_cproj, g_step, g_rate, g_gate_in, g_state_in, g_skip, g_gain_two = (
            finish_back(grad_gate)
        )
        carried = prefix((through, g_state_in), "seq", chain_link, identity, True)[1]
        h_inner, h_bproj, h_step, h_rate = state_back(
            (carried, jnp.sum(carried * state_in, axis=(1, 2)))
        )
        g_proj, g_tail, g_kernel, g_offset, g_bias, g_log = prep_back(
            (
                g_inner + h_inner,
                g_bproj + h_bproj,
                g_cproj,
                g_step + h_step,
                g_rate + h_rate,
                g_gate_in,
            )
        )
        returned = passed_along(g_tail, "seq", -1)
        width_after = proj_out.shape[1] - DI - CH
        g_proj = g_proj + jnp.pad(returned, ((length_t - halo_rows, 0), (DI, width_after)))
        proj_grad_low = g_proj.astype(jnp.bfloat16)
        grad_normed = lax.dot_general(
            proj_grad_low, in_back, (((1,), (1,)), ((), ())), preferred_element_type=jnp.float32
        )
        grad_resid, g_gain_one = norm_back(grad_normed)
        grad_list.append((cot_low.astype(jnp.float32) + grad_resid).astype(jnp.bfloat16))
        in_shard = lax.psum_scatter(
            lax.dot_general(
                normed_low,
                proj_grad_low,
                (((0,), (0,)), ((), ())),
                preferred_element_type=jnp.float32,
            ),
            "seq",
            scatter_dimension=0,
            tiled=True,
        )
        shards = (
            lax.psum_scatter(out_term, "seq", scatter_dimension=0, tiled=True),
            lax.psum_scatter(g_kernel, "seq", scatter_dimension=1, tiled=True),
            lax.psum_scatter(g_offset, "seq", scatter_dimension=0, tiled=True),
            lax.psum_scatter(g_gain_one, "seq", scatter_dimension=0, tiled=True),
            lax.psum_scatter(g_gain_two, "seq", scatter_dimension=0, tiled=True),
        )
        this_round = (in_shard, shards[0], shards[1], shards[2], shards[3], shards[4])
        if totals is None:
            totals = this_round
        else:
            totals = tuple((prior + fresh for prior, fresh in zip(totals, this_round)))
        head_totals = (head_totals[0] + g_bias, head_totals[1] + g_log, head_totals[2] + g_skip)
    summed = jax.tree.map(
        lambda part: part.astype(jnp.float32), lax.psum(for_sending(totals), "dp")
    )
    heads = lax.psum((head_totals[0], head_totals[1], head_totals[2]), ("dp", "seq"))
    activations = jnp.stack(act_list)[:, None]
    grad_tokens = jnp.stack(grad_list)[:, None]
    return (
        activations,
        grad_tokens,
        summed[4],
        summed[0],
        summed[2],
        summed[3],
        heads[0],
        heads[1],
        heads[2],
        summed[5],
        summed[1],
    )


MESH = pl.DeviceIdType.MESH


def chip(x, y, z):
    return z * 4 + y * 2 + x


def place():
    core = lax.axis_index("dp")
    at = lax.axis_index("seq")
    return at % 2, (at // 2) % 2, at // 4, core


def meet_all(planes):
    barrier = pltpu.get_barrier_semaphore()
    me = lax.axis_index("seq")
    core = lax.axis_index("dp")
    count = planes * 4

    def greet(k, carry):
        other = lax.rem(me + k, count)
        for far in range(2):

            @pl.when(jnp.logical_or(k > 0, far != core))
            def _():
                pl.semaphore_signal(barrier, inc=1, device_id=(far, other), device_id_type=MESH)

        return carry

    lax.fori_loop(0, count, greet, 0)
    pl.semaphore_wait(barrier, 2 * count - 1)


UP, DOWN, SIDE_X, SIDE_Y, HALF_X, HALF_Y, MATE_Z, MATE_X, MATE_Y, MATE_HX, MATE_HY = range(11)


class Gather:
    def __init__(self, whole, rows, quarter, sems, planes):
        self.whole, self.rows, self.quarter, self.sems, self.planes = whole, rows, quarter, sems, planes
        self.x, self.y, self.z, self.core = place()

    def region(self, block, core, part=None):
        width = self.whole.shape[1] // 2
        start = pl.multiple_of(block * self.rows, 16)
        left = pl.multiple_of(core * width, 128)
        if part is None:
            return self.whole.at[pl.ds(start, self.rows), pl.ds(left, width)]
        if self.quarter == "rows":
            half = self.rows // 2
            return self.whole.at[pl.ds(pl.multiple_of(start + part * half, 16), half), pl.ds(left, width)]
        half = width // 2
        return self.whole.at[pl.ds(start, self.rows), pl.ds(pl.multiple_of(left + part * half, 128), half)]

    def copy(self, kind, far, block, core, part, device):
        region = self.region(block, core, part)
        return pltpu.make_async_remote_copy(
            src_ref=region,
            dst_ref=region,
            send_sem=self.sems.at[0, kind, far],
            recv_sem=self.sems.at[1, kind, far],
            device_id=device,
            device_id_type=MESH,
        )

    def transfers(self, far):
        x, y, z, c = self.x, self.y, self.z, self.core
        own = chip(x, y, far)
        by_x, by_y, across = chip(1 - x, y, far), chip(x, 1 - y, far), chip(1 - x, 1 - y, far)
        mate = (1 - c, chip(x, y, z))
        to_x, to_y = (c, chip(1 - x, y, z)), (c, chip(x, 1 - y, z))
        return {
            UP: (own, None, (c, chip(x, y, z + 1))),
            DOWN: (own, None, (c, chip(x, y, z - 1))),
            SIDE_X: (own, None, to_x),
            SIDE_Y: (own, None, to_y),
            HALF_X: (by_y, 1, to_x),
            HALF_Y: (by_x, 0, to_y),
            MATE_Z: (own, None, mate),
            MATE_X: (by_x, None, mate),
            MATE_Y: (by_y, None, mate),
            MATE_HX: (across, 1, mate),
            MATE_HY: (across, 0, mate),
        }

    def send(self, kind, far):
        block, part, device = self.transfers(far)[kind]
        self.copy(kind, far, block, self.core, part, device).start()

    def sent(self, kind, far):
        block, part, device = self.transfers(far)[kind]
        self.copy(kind, far, block, self.core, part, device).wait_send()

    def arrived(self, kind, far):
        x, y = self.x, self.y
        block, part, core = {
            UP: (chip(x, y, far), None, 0),
            DOWN: (chip(x, y, far), None, 0),
            SIDE_X: (chip(1 - x, y, far), None, 0),
            SIDE_Y: (chip(x, 1 - y, far), None, 0),
            HALF_X: (chip(1 - x, 1 - y, far), 1, 0),
            HALF_Y: (chip(1 - x, 1 - y, far), 0, 0),
            MATE_Z: (chip(x, y, far), None, 1),
            MATE_X: (chip(1 - x, y, far), None, 1),
            MATE_Y: (chip(x, 1 - y, far), None, 1),
            MATE_HX: (chip(1 - x, 1 - y, far), 1, 1),
            MATE_HY: (chip(1 - x, 1 - y, far), 0, 1),
        }[kind]
        owner = self.core if core == 0 else 1 - self.core
        self.copy(kind, far, block, owner, part, (1 - self.core, chip(x, y, self.z))).wait_recv()

    def each(self, distance, act):
        for sign in (-1, 1) if distance else (1,):
            far = self.z + sign * distance
            if distance:
                pl.when(jnp.logical_and(far >= 0, far < self.planes))(functools.partial(act, far, sign))
            else:
                act(far, sign)

    def column(self, distance):
        def act(far, sign):
            if distance:
                self.arrived(UP if sign < 0 else DOWN, far)
            if sign < 0 or not distance:
                pl.when(self.z < self.planes - 1)(lambda: self.send(UP, far))
            if sign > 0:
                pl.when(self.z > 0)(lambda: self.send(DOWN, far))
            self.send(SIDE_X, far)
            self.send(SIDE_Y, far)
            if distance:
                self.send(MATE_Z, far)

        self.each(distance, act)

    def sides(self, distance):
        def act(far, sign):
            self.arrived(SIDE_X, far)
            self.send(HALF_Y, far)
            self.send(MATE_X, far)
            self.arrived(SIDE_Y, far)
            self.send(HALF_X, far)
            self.send(MATE_Y, far)

        self.each(distance, act)

    def diagonal(self, distance):
        def act(far, sign):
            self.arrived(HALF_Y, far)
            self.send(MATE_HY, far)
            self.arrived(HALF_X, far)
            self.send(MATE_HX, far)

        self.each(distance, act)

    def finish(self):
        for distance in range(self.planes):

            def act(far, sign):
                if sign < 0 or not distance:
                    pl.when(self.z < self.planes - 1)(lambda: self.sent(UP, far))
                if sign > 0:
                    pl.when(self.z > 0)(lambda: self.sent(DOWN, far))
                for kind in (SIDE_X, SIDE_Y, HALF_X, HALF_Y, MATE_X, MATE_Y, MATE_HX, MATE_HY):
                    self.sent(kind, far)
                for kind in (MATE_X, MATE_Y, MATE_HX, MATE_HY):
                    self.arrived(kind, far)
                if distance:
                    self.sent(MATE_Z, far)
                    self.arrived(MATE_Z, far)

            self.each(distance, act)

    def steps(self):
        do = [lambda: self.column(0), lambda: self.column(1), lambda: self.sides(0), lambda: self.column(2), lambda: self.diagonal(0),
              lambda: self.sides(1), lambda: self.column(3), lambda: self.diagonal(1), lambda: self.sides(2), lambda: self.diagonal(2),
              lambda: self.sides(3), lambda: self.diagonal(3)]
        return do


def gather_sems(planes):
    return pltpu.SemaphoreType.DMA((2, 11, planes))


class Reduce:
    X, Y, HX, HY, RISE, FALL, MATE, LAST = range(8)

    @staticmethod
    def scratch(rows, width, quarter, planes):
        half = width // 2
        corner = (rows // 2, half) if quarter == "rows" else (rows, half // 2)
        bf16 = jnp.bfloat16
        return [
            pltpu.VMEM((4 * planes * rows, half), bf16),
            pltpu.VMEM((4, planes, rows, half), bf16),
            pltpu.VMEM((2, planes) + corner, bf16),
            pltpu.SemaphoreType.DMA((2, 8, planes)),
        ]

    def __init__(self, part, out, rows, quarter, scratch, planes):
        self.part, self.out, self.rows, self.quarter, self.planes = part, out, rows, quarter, planes
        self.mate_in, self.side_in, self.corner_in, self.sems = scratch
        self.x, self.y, self.z, self.core = place()
        self.half = part.shape[1] // 2

    def block(self, owner, part=None):
        start = pl.multiple_of(owner * self.rows, 16)
        left = pl.multiple_of(self.core * self.half, 128)
        if part is None:
            return pl.ds(start, self.rows), pl.ds(left, self.half)
        if self.quarter == "rows":
            return pl.ds(pl.multiple_of(start + part * (self.rows // 2), 16), self.rows // 2), pl.ds(left, self.half)
        quarter = self.half // 2
        return pl.ds(start, self.rows), pl.ds(pl.multiple_of(left + part * quarter, 128), quarter)

    def copy(self, kind, far, source, target, device):
        return pltpu.make_async_remote_copy(
            src_ref=source,
            dst_ref=target,
            send_sem=self.sems.at[0, kind, far],
            recv_sem=self.sems.at[1, kind, far],
            device_id=device,
            device_id_type=MESH,
        )

    def move(self, kind, far):
        x, y, z, c = self.x, self.y, self.z, self.core
        part = self.part
        to_x, to_y, mate = (c, chip(1 - x, y, z)), (c, chip(x, 1 - y, z)), (1 - c, chip(x, y, z))
        if kind == self.X:
            return self.copy(kind, far, part.at[self.block(chip(1 - x, y, far))], self.side_in.at[0, far], to_x)
        if kind == self.Y:
            return self.copy(kind, far, part.at[self.block(chip(x, 1 - y, far))], self.side_in.at[1, far], to_y)
        if kind == self.HX:
            return self.copy(kind, far, part.at[self.block(chip(1 - x, 1 - y, far), 0)], self.corner_in.at[0, far], to_x)
        if kind == self.HY:
            return self.copy(kind, far, part.at[self.block(chip(1 - x, 1 - y, far), 1)], self.corner_in.at[1, far], to_y)
        if kind == self.RISE:
            return self.copy(kind, far, part.at[self.block(chip(x, y, far))], self.side_in.at[2, far], (c, chip(x, y, z + 1)))
        if kind == self.FALL:
            return self.copy(kind, far, part.at[self.block(chip(x, y, far))], self.side_in.at[3, far], (c, chip(x, y, z - 1)))
        if kind == self.MATE:
            rows = pl.ds(pl.multiple_of(far * 4 * self.rows, 16), 4 * self.rows)
            left = pl.multiple_of((1 - c) * self.half, 128)
            return self.copy(kind, far, part.at[rows, pl.ds(left, self.half)], self.mate_in.at[rows], mate)
        left = pl.multiple_of(c * self.half, 128)
        region = self.out.at[:, pl.ds(left, self.half)]
        return self.copy(kind, 0, region, region, mate)

    def add(self, at, *refs):
        total = self.part[at].astype(jnp.float32)
        for ref in refs:
            total = total + ref[...].astype(jnp.float32)
        self.part[at] = low(total)

    def each(self, distance, act):
        for sign in (-1, 1) if distance else (1,):
            far = self.z + sign * distance
            if distance:
                pl.when(jnp.logical_and(far >= 0, far < self.planes))(functools.partial(act, far, sign))
            else:
                act(far, sign)

    def start(self, distance):
        self.each(distance, lambda far, sign: self.move(self.MATE, far).start())

    def fold(self, distance):
        def act(far, sign):
            self.move(self.MATE, far).wait_recv()

            def rows(k, carry):
                start = pl.multiple_of((far * 4 + k) * self.rows, 16)
                left = pl.multiple_of(self.core * self.half, 128)
                self.add((pl.ds(start, self.rows), pl.ds(left, self.half)), self.mate_in.at[pl.ds(start, self.rows)])
                return carry

            lax.fori_loop(0, 4, rows, 0)
            self.move(self.HX, far).start()
            self.move(self.HY, far).start()

        self.each(distance, act)

    def sides(self, distance):
        x, y = self.x, self.y

        def act(far, sign):
            self.move(self.HX, far).wait_recv()
            self.add(self.block(chip(x, 1 - y, far), 0), self.corner_in.at[0, far])
            self.move(self.Y, far).start()
            self.move(self.HY, far).wait_recv()
            self.add(self.block(chip(1 - x, y, far), 1), self.corner_in.at[1, far])
            self.move(self.X, far).start()

        self.each(distance, act)

    def column(self, distance):
        x, y, z = self.x, self.y, self.z

        def act(far, sign):
            self.move(self.X, far).wait_recv()
            self.move(self.Y, far).wait_recv()
            at = self.block(chip(x, y, far))
            if distance:
                self.add(at, self.side_in.at[0, far], self.side_in.at[1, far])
                if sign > 0:

                    @pl.when(z > 0)
                    def _():
                        self.move(self.RISE, far).wait_recv()
                        self.add(at, self.side_in.at[2, far])

                    self.move(self.RISE, far).start()
                else:

                    @pl.when(z < self.planes - 1)
                    def _():
                        self.move(self.FALL, far).wait_recv()
                        self.add(at, self.side_in.at[3, far])

                    self.move(self.FALL, far).start()
                return
            total = self.part[at].astype(jnp.float32)
            total = total + self.side_in[0, far].astype(jnp.float32) + self.side_in[1, far].astype(jnp.float32)
            left = pl.multiple_of(self.core * self.half, 128)
            here = (slice(None), pl.ds(left, self.half))
            self.out[here] = total

            @pl.when(z > 0)
            def _():
                self.move(self.RISE, far).wait_recv()
                self.out[here] = self.out[here] + self.side_in[2, far].astype(jnp.float32)

            @pl.when(z < self.planes - 1)
            def _():
                self.move(self.FALL, far).wait_recv()
                self.out[here] = self.out[here] + self.side_in[3, far].astype(jnp.float32)

            self.move(self.LAST, 0).start()

        self.each(distance, act)

    def finish(self):
        last = self.move(self.LAST, 0)
        left = pl.multiple_of((1 - self.core) * self.half, 128)
        region = self.out.at[:, pl.ds(left, self.half)]
        self.copy(self.LAST, 0, region, region, (1 - self.core, chip(self.x, self.y, self.z))).wait_recv()
        last.wait_send()
        for distance in range(self.planes):

            def act(far, sign):
                for kind in (self.MATE, self.HX, self.HY, self.X, self.Y):
                    self.move(kind, far).wait_send()
                if distance:
                    self.move(self.RISE if sign > 0 else self.FALL, far).wait_send()

            self.each(distance, act)

    def steps(self):
        top = self.planes - 1
        do = [functools.partial(self.start, d) for d in range(top, -1, -1)]
        do += [functools.partial(self.fold, d) for d in range(top, -1, -1)]
        for d in range(top, -1, -1):
            do += [functools.partial(self.sides, d)]
            if d < top:
                do += [functools.partial(self.column, d + 1)]
        return do + [functools.partial(self.column, 0)]


class Chain:
    CUT = 3

    @staticmethod
    def scratch():
        half = pltpu.VMEM((N, DI // 2), jnp.bfloat16)
        wide = pltpu.VMEM((N, DI // 2), jnp.float32)
        return [half, half, half, half, half, half, wide, wide, pltpu.SemaphoreType.DMA((2, 2 + Chain.CUT))]

    def __init__(self, part, result, factors, scratch, lead, planes):
        self.part, self.result, self.factors, self.lead, self.planes = part, result, factors, lead, planes
        self.give, self.take, self.leave, self.come, self.back, self.again, self.total, self.front, self.sems = scratch
        self.x, self.y, self.z, self.core = place()
        self.half = DI // 2
        self.leads = self.core == lead
        self.ahead = 1 if lead == 0 else -1
        self.first = self.z == (0 if lead == 0 else planes - 1)
        self.last = self.z == (planes - 1 if lead == 0 else 0)

    def own(self):
        return pl.ds(pl.multiple_of(self.core * self.half, 128), self.half)

    def other(self):
        return pl.ds(pl.multiple_of((1 - self.core) * self.half, 128), self.half)

    def copy(self, k, source, target, device):
        return pltpu.make_async_remote_copy(
            src_ref=source,
            dst_ref=target,
            send_sem=self.sems.at[0, k],
            recv_sem=self.sems.at[1, k],
            device_id=device,
            device_id_type=MESH,
        )

    def mate(self):
        return (1 - self.core, chip(self.x, self.y, self.z))

    def trade(self):
        return self.copy(0, self.give, self.take, self.mate())

    def returned(self):
        return self.copy(1, self.back, self.again, self.mate())

    def hop(self, k):
        cut = self.half // self.CUT
        at = (slice(None), pl.ds(k * cut, cut))
        return self.copy(
            2 + k, self.leave.at[at], self.come.at[at], (self.core, chip(self.x, self.y, self.z + self.ahead))
        )

    def start(self):
        self.give[...] = low(self.part[:, self.other()])
        self.trade().start()

    def rows(self):
        return self.factors[self.lead, 0:1, self.own()], self.factors[1 - self.lead, 0:1, self.own()]

    def merge(self):
        self.trade().wait_recv()
        own = self.part[:, self.own()]
        got = self.take[...].astype(jnp.float32)
        ahead, behind = jnp.where(self.leads, own, got), jnp.where(self.leads, got, own)
        _, following = self.rows()
        self.front[...] = ahead
        self.total[...] = following * ahead + behind

        @pl.when(self.first)
        def _():
            self.come[...] = jnp.zeros(self.come.shape, self.come.dtype)
            self.leave[...] = low(self.total[...])
            for k in range(self.CUT):
                self.hop(k).start()

    def pass_on(self):
        leading, following = self.rows()
        cut = self.half // self.CUT

        @pl.when(jnp.logical_not(self.first))
        def _():
            for k in range(self.CUT):
                self.hop(k).wait_recv()

                @pl.when(jnp.logical_not(self.last))
                def _():
                    at = (slice(None), slice(k * cut, (k + 1) * cut))
                    both = (leading * following)[:, k * cut : (k + 1) * cut]
                    self.leave[at] = low(both * self.come[at].astype(jnp.float32) + self.total[at])
                    self.hop(k).start()

        came = self.come[...].astype(jnp.float32)
        later = low(leading * came + self.front[...])
        self.back[...] = jnp.where(self.leads, later.astype(jnp.float32), came).astype(jnp.bfloat16)
        self.returned().start()
        self.result[:, self.own()] = jnp.where(self.leads, came, later.astype(jnp.float32)).astype(jnp.bfloat16)

    def close(self):
        self.returned().wait_recv()
        self.result[:, self.other()] = self.again[...]

    def finish(self):
        self.trade().wait_send()
        self.returned().wait_send()

        @pl.when(jnp.logical_not(self.last))
        def _():
            for k in range(self.CUT):
                self.hop(k).wait_send()


VMEM = pl.BlockSpec(memory_space=pltpu.VMEM)
ROWS = 256
HALO = 16
WIDE = 2048
TRANS = (((0,), (0,)), ((), ()))
TRANS_B = (((1,), (1,)), ((), ()))


def dot(a, b, dims=(((1,), (0,)), ((), ()))):
    return lax.dot_general(a, b, dims, preferred_element_type=jnp.float32)


def low(a):
    return a.astype(jnp.bfloat16)


class Shuffle:
    def __init__(self, source, target, sems, offset=0, back=False):
        self.source, self.target, self.sems, self.offset, self.back = source, target, sems, offset, back
        self.x, self.y, self.z, self.core = place()

    def piece(self, k):
        x, y, z, c = self.x, self.y, self.z, self.core
        rows = 128
        if self.back:
            source = self.source.at[pl.ds(rows * k, rows)]
            target = self.target.at[x]
        else:
            source = self.source.at[k]
            if len(self.target.shape) == len(self.source.shape):
                target = self.target.at[self.offset + x]
            else:
                target = self.target.at[pl.ds(pl.multiple_of(self.offset + rows * x, 16), rows)]
        stays = jnp.logical_and(x == k, y == c)
        local = pltpu.make_async_copy(source, target, self.sems.at[1, x])
        remote = pltpu.make_async_remote_copy(
            src_ref=source,
            dst_ref=target,
            send_sem=self.sems.at[0, k],
            recv_sem=self.sems.at[1, x],
            device_id=(y, chip(k, c, z)),
            device_id_type=MESH,
        )
        return stays, local, remote

    def start(self):
        for k in range(2):
            stays, local, remote = self.piece(k)
            pl.when(stays)(local.start)
            pl.when(jnp.logical_not(stays))(remote.start)

    def arrived(self):
        x, y, z, c = self.x, self.y, self.z, self.core
        for k in range(2):
            if self.back:
                target = self.target.at[k]
            elif len(self.target.shape) == len(self.source.shape):
                target = self.target.at[self.offset + k]
            else:
                target = self.target.at[pl.ds(self.offset + 128 * k, 128)]
            stays = jnp.logical_and(x == k, y == c)
            local = pltpu.make_async_copy(target, target, self.sems.at[1, k])
            remote = pltpu.make_async_remote_copy(
                src_ref=target,
                dst_ref=target,
                send_sem=self.sems.at[0, k],
                recv_sem=self.sems.at[1, k],
                device_id=(y, chip(k, c, z)),
                device_id_type=MESH,
            )
            pl.when(stays)(local.wait)
            pl.when(jnp.logical_not(stays))(remote.wait_recv)

    def finish(self):
        for k in range(2):
            stays, local, remote = self.piece(k)
            pl.when(jnp.logical_not(stays))(remote.wait_send)


class Before:
    def __init__(self, source, target, sems, planes):
        self.source, self.target, self.sems, self.planes = source, target, sems, planes
        self.x, self.y, self.z, self.core = place()

    def piece(self, m):
        x, y, z, c = self.x, self.y, self.z, self.core
        source = self.source(m)
        return pltpu.make_async_remote_copy(
            src_ref=source,
            dst_ref=self.target,
            send_sem=self.sems.at[0, m],
            recv_sem=self.sems.at[1, 0],
            device_id=(1 - y, chip(m, c, z + y)),
            device_id_type=MESH,
        )

    def when_sending(self):
        return jnp.logical_and(self.x == 1, jnp.logical_or(self.y == 0, self.z < self.planes - 1))

    def start(self):
        @pl.when(self.when_sending())
        def _():
            for m in range(2):
                self.piece(m).start()

    def arrived(self):
        pl.when(self.z + self.core > 0)(self.piece(0).wait_recv)

    def finish(self):
        @pl.when(self.when_sending())
        def _():
            for m in range(2):
                self.piece(m).wait_send()


class ToAll:
    def __init__(self, table, sems, planes):
        self.table, self.sems, self.count = table, sems, planes * 4
        self.me, self.core = lax.axis_index("seq"), lax.axis_index("dp")

    def copy(self, block, other):
        return pltpu.make_async_remote_copy(
            src_ref=self.table.at[block],
            dst_ref=self.table.at[block],
            send_sem=self.sems.at[0, other],
            recv_sem=self.sems.at[1, block],
            device_id=(self.core, other),
            device_id_type=MESH,
        )

    def over(self, act):
        def one(k, carry):
            act(lax.rem(self.me + k, self.count))
            return carry

        lax.fori_loop(1, self.count, one, 0)

    def start(self):
        self.over(lambda other: self.copy(self.me, other).start())

    def arrived(self):
        self.over(lambda other: self.copy(other, self.me).wait_recv())

    def finish(self):
        self.over(lambda other: self.copy(self.me, other).wait_send())


def enter_kernel(
    planes, tok_ref, seg_ref, small_ref, wa_ref,
    whole, table, tok, seg, normed_ref, proj_ref, conv_ref, gain_ref, ngain_ref,
    normed_all, gather_sem, tok_sem, seg_sem, end_sem, segend_sem, small_sem,
):
    at = lax.axis_index("seq")
    x, y, z, c = place()
    whole[pl.ds(pl.multiple_of(at * 48, 16), 48), :] = wa_ref[...]
    table[at] = small_ref[...]

    @pl.when(z + c == 0)
    def _():
        tok[0:HALO, :] = jnp.zeros((HALO, tok.shape[1]), tok.dtype)
        seg[0] = jnp.full((8, 128), -1.0, jnp.float32)

    gather = Gather(whole, 48, "columns", gather_sem, planes)
    tokens = Shuffle(tok_ref, tok, tok_sem, HALO)
    numbers = Shuffle(seg_ref, seg, seg_sem, 1)
    ends = Before(lambda m: tok_ref.at[m, pl.ds(128 - HALO, HALO)], tok.at[pl.ds(0, HALO)], end_sem, planes)
    segends = Before(lambda m: seg_ref.at[m], seg.at[0], segend_sem, planes)
    small = ToAll(table, small_sem, planes)
    meet_all(planes)
    moves = [tokens, ends, numbers, segends, small]
    for move in moves:
        move.start()
    steps = gather.steps()
    for step in steps[:3]:
        step()
    for move in moves:
        move.arrived()
    conv_ref[...] = jnp.concatenate([table[k, :, 0:112] for k in range(16)], axis=1)
    gate = jnp.concatenate([table[k, :, 0:96] for k in range(16)], axis=1)
    gain_ref[...] = gate
    ngain_ref[...] = jnp.concatenate([table[k, :, 0:48] for k in range(16)], axis=1)
    gain = ngain_ref[5:6, :]
    u = tok[...].astype(jnp.float32)
    r = lax.rsqrt(jnp.mean(u * u, axis=-1, keepdims=True) + EPSILON)
    normed_all[...] = low(u * r * gain)
    normed_ref[...] = normed_all[HALO:, :]
    for step in steps[3:]:
        step()
    gather.finish()
    for move in moves:
        move.finish()

    def columns(k, carry):
        at_k = pl.ds(pl.multiple_of(k * 512, 512), 512)
        proj_ref[:, at_k] = dot(normed_all[...], whole[:, at_k])
        return carry

    lax.fori_loop(0, WIDE // 512, columns, 0)


def enter(tokens, segf, small, wa, planes):
    f32, bf16 = jnp.float32, jnp.bfloat16
    shape = jax.ShapeDtypeStruct
    two = pltpu.SemaphoreType.DMA((2, 2))
    return pl.pallas_call(
        functools.partial(enter_kernel, planes),
        out_shape=[
            shape((768, WIDE), bf16),
            shape((16, 8, 128), f32),
            shape((HALO + ROWS, 768), bf16),
            shape((3, 8, 128), f32),
            shape((ROWS, 768), bf16),
            shape((HALO + ROWS, WIDE), f32),
            shape((8, CH), f32),
            shape((8, DI), f32),
            shape((8, 768), f32),
        ],
        in_specs=[VMEM] * 4,
        out_specs=[VMEM] * 9,
        scratch_shapes=[
            pltpu.VMEM((HALO + ROWS, 768), bf16),
            gather_sems(planes), two, two, two, two,
            pltpu.SemaphoreType.DMA((2, 16)),
        ],
        compiler_params=pltpu.CompilerParams(collective_id=0, has_side_effects=True, vmem_limit_bytes=48 << 20),
    )(tokens, segf, small, wa)


TILE = 128
TILES = DI // TILE


class Names:
    def __init__(self, names, refs):
        for name, ref in zip(names, refs, strict=True):
            setattr(self, name, ref)


def at_tile(j):
    return pl.ds(pl.multiple_of(j * TILE, TILE), TILE)


def at_rows(k, rows):
    return pl.ds(pl.multiple_of(k * rows, rows), rows)


def loop(low_end, high_end, act):
    def one(k, carry):
        act(k)
        return carry

    lax.fori_loop(low_end, high_end, one, 0)


def iota(shape, dim):
    return lax.broadcasted_iota(jnp.int32, shape, dim)


def pieces(a):
    high = low(a)
    rest = a - high.astype(jnp.float32)
    middle = low(rest)
    return high, middle, low(rest - middle.astype(jnp.float32))


def packed(a):
    a = jnp.where(iota(a.shape, 1) < H, a, 0.0)
    high, middle, rest = (part.astype(jnp.float32) for part in pieces(a))
    return low(high + pltpu.roll(middle, 32, 1) + pltpu.roll(rest, 64, 1))


def spread_matrix(width, first=0):
    row, col = iota((128, width), 0), iota((128, width), 1) + first
    return low(jnp.where(jnp.logical_and(row % 32 == col // P_SIZE, row < 96), 1.0, 0.0))


def head_sums(a, j):
    row, col = iota((TILE, 128), 0), iota((TILE, 128), 1)
    pick = low(jnp.where(row // P_SIZE + 2 * j == col, 1.0, 0.0))
    high, middle, rest = pieces(a)
    return dot(high, pick) + dot(middle, pick) + dot(rest, pick)


def sigmoid(v):
    return 1.0 / (1.0 + jnp.exp(-v))


REST_IN = ["wa", "tok", "seg", "normed", "proj", "conv", "gain", "ngain", "heads", "wz", "wout", "cot"]
REST_OUT = ["act_out", "tokens_out", "grad_a", "grad_z", "grad_out", "small_out"]


def rest_scratch(planes):
    f32, bf16 = jnp.float32, jnp.bfloat16
    v = pltpu.VMEM
    dma = pltpu.SemaphoreType.DMA
    two = dma((2, 2))
    return {
        "wz_full": v((768, DI), bf16), "wout_full": v((DI, 768), bf16), "wz_sem": gather_sems(planes), "wout_sem": gather_sems(planes),
        "cot_own": v((ROWS, 768), bf16), "cot_sem": two, "act_sem": two, "back_sem": two,
        "segcol": v((384, 128), f32), "same": v((KC, ROWS + HALO, 128), f32),
        "pre": v((ROWS, CH), f32), "inner": v((ROWS, DI), f32), "bproj": v((ROWS, N), bf16), "cproj": v((ROWS, N), bf16),
        "cumt": v((H, 8, ROWS), f32), "bar": v((ROWS, ROWS), f32), "scores": v((ROWS, ROWS), f32),
        "step": v((ROWS, 128), f32), "cum": v((ROWS, 128), f32), "ein": v((ROWS, 128), f32), "eout": v((ROWS, 128), f32),
        "stepx": v((ROWS, DI), f32), "einx": v((ROWS, DI), f32), "eoutx": v((ROWS, DI), f32), "cumx": v((ROWS, DI), f32),
        "xs": v((ROWS, DI), bf16), "xso": v((ROWS, DI), bf16),
        "part": v((N, DI), f32), "factors": v((2, 8, DI), f32), "factor_sem": dma((2,)), "skipx": v((8, DI), f32),
        "state": v((N, DI), bf16), "dstate": v((N, DI), bf16),
        "y": v((ROWS, DI), f32), "z": v((ROWS, DI), f32), "gated": v((ROWS, DI), bf16), "act_own": v((ROWS, 768), bf16),
        "dz": v((ROWS, DI), bf16), "dy": v((ROWS, DI), bf16), "dyin": v((ROWS, DI), bf16),
        "ggain": v((8, DI), f32), "gskip": v((8, DI), f32),
        "dscores": v((ROWS, ROWS), f32), "dxs": v((ROWS, DI), f32), "sums": v((3, ROWS, 128), f32),
        "dpre": v((ROWS + HALO, CH), f32), "dx": v((ROWS, WIDE), bf16), "tail": v((8, CH), f32), "tail_in": v((8, CH), f32), "tail_sem": dma((2,)),
        "gconv": v((8, CH), f32), "gtok": v((ROWS, 768), bf16),
        "table": v((16, 8, 128), f32), "inbox": v((2, 16, 8, 128), f32), "table_sem": dma((2, 2, 16)),
        "part_a": v((768, WIDE), bf16), "part_z": v((768, DI), bf16), "part_out": v((DI, 768), bf16),
    }


def rest_kernel(planes, names, *refs):
    r = Names(REST_IN + REST_OUT + names, refs[: len(REST_IN) + len(REST_OUT) + len(names)])
    extra = list(refs[len(REST_IN) + len(REST_OUT) + len(names) :])
    chain_f, chain_b = extra[0:9], extra[9:18]
    red_a, red_z, red_out = extra[18:22], extra[22:26], extra[26:30]
    x, y, z, c = place()
    me = chip(x, y, z)
    mate = (1 - c, me)
    f32 = jnp.float32
    r.wz_full[pl.ds(pl.multiple_of(me * 48, 16), 48), :] = r.wz[...]
    r.wout_full[pl.ds(pl.multiple_of(me * 96, 16), 96), :] = r.wout[...]
    gather_z = Gather(r.wz_full, 48, "columns", r.wz_sem, planes)
    gather_out = Gather(r.wout_full, 96, "rows", r.wout_sem, planes)
    cots = Shuffle(r.cot, r.cot_own, r.cot_sem)
    meet_all(planes)
    cots.start()
    waiting = [step for pair in zip(gather_z.steps(), gather_out.steps()) for step in pair]

    def background(count):
        for _ in range(min(count, len(waiting))):
            waiting.pop(0)()

    background(2)

    for k in range(3):
        r.segcol[128 * k : 128 * k + 128, :] = jnp.transpose(jnp.broadcast_to(r.seg[k, 0:1, :], (128, 128)))
    seg = r.segcol[128:384, :]
    for k in range(KC):
        r.same[k] = jnp.zeros((ROWS + HALO, 128), f32)
        r.same[k, 8 : 8 + ROWS, :] = jnp.where(r.segcol[125 + k : 125 + k + ROWS, :] == seg, 1.0, 0.0)

    def convolve(j):
        at = at_tile(j)
        total = jnp.broadcast_to(r.conv[4:5, at], (ROWS, TILE))
        for k in range(KC):
            total = total + r.conv[k : k + 1, at] * r.proj[13 + k : 13 + k + ROWS, at] * r.same[k, 8 : 8 + ROWS, :]
        r.pre[:, at] = total
        return total * sigmoid(total)

    def inner(j):
        r.inner[:, at_tile(j)] = convolve(j)

    loop(0, TILES, inner)
    r.bproj[...] = low(convolve(TILES))
    r.cproj[...] = low(convolve(TILES + 1))
    background(4)

    raw = r.proj[HALO:, CH : CH + 128] + r.heads[0:1, :]
    step = jnp.maximum(raw, 0.0) + jnp.log1p(jnp.exp(-jnp.abs(raw)))
    rate = -jnp.exp(r.heads[1:2, :])
    lower = jnp.where(iota((ROWS, ROWS), 0) >= iota((ROWS, ROWS), 1), 1.0, 0.0)
    cum = jnp.dot(lower, step * rate, precision=HIGHEST, preferred_element_type=f32)
    r.step[...] = step
    r.cum[...] = cum
    across = jnp.transpose(cum)
    for h in range(H):
        r.cumt[h] = jnp.broadcast_to(across[h : h + 1, :], (8, ROWS))
    last = cum[ROWS - 1 : ROWS, :]
    before = r.segcol[127:128, :]
    first_seg, last_seg = seg[0:1, :], seg[ROWS - 1 : ROWS, :]
    r.ein[...] = jnp.where(seg == before, jnp.exp(cum), 0.0)
    r.eout[...] = jnp.where(seg == last_seg, jnp.exp(last - cum), 0.0)
    through = jnp.logical_and(first_seg == last_seg, first_seg == before)
    factor = jnp.where(through, jnp.exp(last), 0.0)
    segrow = jnp.concatenate([r.seg[1, 0:1, :], r.seg[2, 0:1, :]], axis=1)
    allowed = jnp.logical_and(jnp.concatenate([seg, seg], axis=1) == segrow, iota((ROWS, ROWS), 0) >= iota((ROWS, ROWS), 1))
    r.bar[...] = jnp.where(allowed, 0.0, -1e30)
    rows = packed(jnp.concatenate([jnp.broadcast_to(factor, (8, 128)), jnp.broadcast_to(r.heads[2:3, :], (8, 128))], axis=0))
    both = dot(rows, spread_matrix(DI))
    r.factors[c] = both[0:8, :]
    r.skipx[...] = both[8:16, :]
    share = pltpu.make_async_remote_copy(
        src_ref=r.factors.at[c], dst_ref=r.factors.at[c], send_sem=r.factor_sem.at[0], recv_sem=r.factor_sem.at[1],
        device_id=mate, device_id_type=MESH,
    )
    share.start()
    spreads = [(r.stepx, packed(step)), (r.einx, packed(r.ein[...])), (r.eoutx, packed(r.eout[...])), (r.cumx, packed(cum))]
    r.stepx[...] = dot(spreads[0][1], spread_matrix(DI))
    r.einx[...] = dot(spreads[1][1], spread_matrix(DI))
    r.eoutx[...] = dot(spreads[2][1], spread_matrix(DI))
    r.cumx[...] = dot(spreads[3][1], spread_matrix(DI))

    def outgoing(j):
        at = at_tile(j)
        scaled = r.stepx[:, at] * r.inner[:, at]
        r.xs[:, at] = low(scaled)
        xso = low(scaled * r.eoutx[:, at])
        r.xso[:, at] = xso
        r.part[:, at] = dot(r.bproj[...], xso, TRANS)

    loop(0, TILES, outgoing)
    forward = Chain(r.part, r.state, r.factors, chain_f, 0, planes)
    forward.start()
    r.scores[...] = dot(r.cproj[...], r.bproj[...], TRANS_B)
    background(4)

    first_half = iota((1, TILE), 1) < P_SIZE

    def decays(j, band):
        size = 128 * (band + 1)
        rows = slice(128 * band, 128 * band + 128)
        tile = r.cumx[rows, at_tile(j)]
        turned = pltpu.roll(tile, P_SIZE, 1)
        out = []
        for k in range(2):
            column = jnp.where(first_half, tile, turned) if k == 0 else jnp.where(first_half, turned, tile)
            wide = column if band == 0 else jnp.concatenate([column, column], axis=1)
            out.append(jnp.exp(wide - r.cumt[2 * j + k, 0:1, 0:size] + r.bar[rows, 0:size]))
        return out

    def halves(tile):
        zero = jnp.zeros_like(tile)
        return jnp.where(first_half, tile, zero), jnp.where(first_half, zero, tile)

    def within(j):
        at = at_tile(j)
        for band in range(2):
            size = 128 * (band + 1)
            rows = slice(128 * band, 128 * band + 128)
            inside = halves(r.xs[0:size, at])
            total = 0.0
            for decay, xs in zip(decays(j, band), inside):
                total = total + dot(low(decay * r.scores[rows, 0:size]), xs)
            r.y[rows, at] = total

    def turn(chain, when):
        for k in range(planes):
            if when[k]:
                position = k if chain.lead == 0 else planes - 1 - k
                pl.when(z == position)(chain.pass_on)

    loop(0, 2, within)
    share.wait_recv()
    forward.merge()
    turn(forward, [1, 0, 0, 0])
    loop(2, 5, within)
    background(2)
    turn(forward, [0, 1, 0, 0])
    loop(5, 8, within)
    background(4)
    turn(forward, [0, 0, 1, 0])
    loop(8, 12, within)
    background(4)
    turn(forward, [0, 0, 0, 1])
    forward.close()

    def carried(j):
        at = at_tile(j)
        r.y[:, at] = r.y[:, at] + r.einx[:, at] * dot(r.cproj[...], r.state[:, at])

    loop(0, TILES, carried)
    background(100)
    gather_z.finish()
    gather_out.finish()
    cots.arrived()

    def projections(j):
        at = pl.ds(pl.multiple_of(j * 512, 512), 512)
        r.z[:, at] = dot(r.normed[...], r.wz_full[:, at])
        r.dxs[:, at] = dot(r.cot_own[...], r.wout_full[at, :], TRANS_B)

    loop(0, 3, projections)
    r.ggain[...] = jnp.zeros((8, DI), f32)
    r.gskip[...] = jnp.zeros((8, DI), f32)

    def gate(k):
        rows = at_rows(k, 16)
        inner, gate_in = r.inner[rows, :], r.z[rows, :]
        mixed = r.y[rows, :] + r.skipx[0:1, :] * inner
        sig = sigmoid(gate_in)
        silu = gate_in * sig
        v = mixed * silu
        scale = lax.rsqrt(jnp.mean(v * v, axis=-1, keepdims=True) + EPSILON)
        gain = r.gain[6:7, :]
        r.gated[rows, :] = low(v * scale * gain)
        dgated = r.dxs[rows, :]
        weighed = dgated * (v * scale)
        r.ggain[...] = r.ggain[...] + weighed[0:8, :] + weighed[8:16, :]
        a = gain * dgated
        dv = scale * (a - v * (scale * scale) * jnp.mean(v * a, axis=-1, keepdims=True))
        dmixed = dv * silu
        r.z[rows, :] = dmixed
        r.dy[rows, :] = low(dmixed)
        r.dyin[rows, :] = low(dmixed * r.einx[rows, :])
        r.dz[rows, :] = low(dv * mixed * (sig * (1.0 + gate_in * (1.0 - sig))))
        skip = dmixed * inner
        r.gskip[...] = r.gskip[...] + skip[0:8, :] + skip[8:16, :]

    loop(0, ROWS // 16, gate)

    def incoming(j):
        at = at_tile(j)
        r.part[:, at] = dot(r.cproj[...], r.dyin[:, at], TRANS)

    loop(0, TILES, incoming)
    backward = Chain(r.part, r.dstate, r.factors, chain_b, 1, planes)
    backward.start()

    def weights(j):
        at = at_rows(j, 256)
        r.part_out[at, :] = low(dot(r.gated[:, at], r.cot_own[...], TRANS))
        r.part_z[:, at] = low(dot(r.normed[...], r.dz[:, at], TRANS))

    loop(0, 2, weights)
    backward.merge()
    turn(backward, [1, 0, 0, 0])
    loop(2, 6, weights)
    turn(backward, [0, 1, 0, 0])
    reduce_out = Reduce(r.part_out, r.grad_out, 96, "rows", red_out, planes)
    reduce_z = Reduce(r.part_z, r.grad_z, 48, "columns", red_z, planes)
    waiting.extend(step for pair in zip(reduce_out.steps(), reduce_z.steps()) for step in pair)
    background(8)

    def project_out(k):
        rows = at_rows(k, 64)
        branch = dot(r.gated[rows, :], r.wout_full[...])
        r.act_own[rows, :] = low(r.tok[pl.ds(pl.multiple_of(HALO + k * 64, 16), 64), :].astype(f32) + branch)

    loop(0, 4, project_out)
    acts = Shuffle(r.act_own, r.act_out, r.act_sem, back=True)
    acts.start()
    turn(backward, [0, 0, 1, 0])

    r.dscores[...] = jnp.zeros((ROWS, ROWS), f32)
    r.sums[...] = jnp.zeros((3, ROWS, 128), f32)

    def within_back(j):
        at = at_tile(j)
        upper = lower = 0.0
        for band in range(2):
            size = 128 * (band + 1)
            rows = slice(128 * band, 128 * band + 128)
            xs = r.xs[0:size, at]
            grads = 0.0
            for decay, dy in zip(decays(j, band), halves(r.dy[rows, at])):
                weight = low(decay * r.scores[rows, 0:size])
                grads = grads + decay * dot(dy, xs, TRANS_B)
                upper = upper + dot(weight[:, 0:128], dy, TRANS)
                if band:
                    lower = lower + dot(weight[:, 128:256], dy, TRANS)
            r.dscores[rows, 0:size] = r.dscores[rows, 0:size] + grads
        r.dxs[0:128, at] = upper
        r.dxs[128:256, at] = lower
        gain = r.dy[:, at].astype(f32) * r.y[:, at] - r.xs[:, at].astype(f32) * r.dxs[:, at]
        r.sums[0] = r.sums[0] + head_sums(gain, j)

    loop(0, 3, within_back)
    turn(backward, [0, 0, 0, 1])
    background(6)
    loop(3, 6, within_back)
    backward.close()
    background(6)
    loop(6, 9, within_back)
    background(4)
    loop(9, 12, within_back)
    background(4)

    def last_sums(j):
        at = at_tile(j)
        xs = r.xs[:, at].astype(f32)
        far = r.eoutx[:, at] * dot(r.bproj[...], r.dstate[:, at])
        total = r.dxs[:, at] + far
        r.sums[1] = r.sums[1] + head_sums(xs * far, j)
        inner = r.inner[:, at]
        r.sums[2] = r.sums[2] + head_sums(inner * total, j)
        r.dxs[:, at] = r.skipx[0:1, at] * r.z[:, at] + r.stepx[:, at] * total

    loop(0, TILES, last_sums)
    dscores = low(r.dscores[...])
    dbproj = dot(dscores, r.cproj[...], TRANS) + dot(r.xso[...], r.dstate[...], TRANS_B)
    dcproj = dot(dscores, r.bproj[...]) + dot(r.dyin[...], r.state[...], TRANS_B)
    pick = jnp.where(iota((DI, 128), 0) // P_SIZE == iota((DI, 128), 1), 1.0, 0.0)
    crossing = jnp.sum(r.dstate[...].astype(f32) * r.state[...].astype(f32), axis=0, keepdims=True) * r.factors[c, 0:1, :]
    rows = jnp.concatenate([jnp.broadcast_to(crossing, (8, DI)), r.gskip[...]], axis=0)
    rows = jnp.dot(rows, pick, precision=HIGHEST, preferred_element_type=f32)
    at_end, gskip = rows[0:1, :], jnp.sum(rows[8:16, :], axis=0, keepdims=True)
    upper = jnp.where(iota((ROWS, ROWS), 0) <= iota((ROWS, ROWS), 1), 1.0, 0.0)
    strict = jnp.where(iota((ROWS, ROWS), 0) > iota((ROWS, ROWS), 1), 1.0, 0.0)
    dlog = (
        jnp.dot(upper, r.sums[0], precision=HIGHEST, preferred_element_type=f32)
        + jnp.dot(strict, r.sums[1], precision=HIGHEST, preferred_element_type=f32)
        + at_end
    )
    step = r.step[...]
    dstep = r.sums[2] + rate * dlog
    draw = dstep * sigmoid(r.proj[HALO:, CH : CH + 128] + r.heads[0:1, :])
    lanes = iota((1, 128), 1) < H
    draw = jnp.where(lanes, draw, 0.0)
    gbias = jnp.sum(draw, axis=0, keepdims=True)
    glog = jnp.where(lanes, jnp.sum(step * dlog, axis=0, keepdims=True) * rate, 0.0)
    r.dx[:, CH : CH + 128] = low(draw)
    r.dx[:, CH + 128 :] = jnp.zeros((ROWS, WIDE - CH - 128), jnp.bfloat16)

    def unconvolve(j, grad):
        at = at_tile(j)
        pre = r.pre[:, at]
        sig = sigmoid(pre)
        grad = grad * (sig * (1.0 + pre * (1.0 - sig)))
        r.dpre[0:8, at] = jnp.zeros((8, TILE), f32)
        r.dpre[8 + ROWS :, at] = jnp.zeros((8, TILE), f32)
        r.dpre[8 : 8 + ROWS, at] = grad
        taps = [
            jnp.sum(grad * r.same[k, 8 : 8 + ROWS, :] * r.proj[13 + k : 13 + k + ROWS, at], axis=0, keepdims=True) for k in range(KC)
        ]
        taps += [jnp.sum(grad, axis=0, keepdims=True), jnp.zeros((3, TILE), f32)]
        r.gconv[:, at] = jnp.concatenate(taps, axis=0)
        total = 0.0
        for k in range(KC):
            rows = slice(3 - k, 3 - k + 8 + ROWS)
            total = total + r.conv[k : k + 1, at] * (r.same[k, rows, :] * r.dpre[rows, at])
        r.tail[:, at] = total[0:8, :]
        r.dx[:, at] = low(total[8:, :])
        r.dpre[0:8, at] = total[ROWS : ROWS + 8, :]

    loop(0, TILES, lambda j: unconvolve(j, r.dxs[:, at_tile(j)]))
    unconvolve(TILES, dbproj)
    unconvolve(TILES + 1, dcproj)
    tails = [
        pltpu.make_async_remote_copy(
            src_ref=r.tail, dst_ref=r.tail_in, send_sem=r.tail_sem.at[0], recv_sem=r.tail_sem.at[1],
            device_id=(1 - c, chip(x, y, z - 1 + c)), device_id_type=MESH,
        )
    ]
    pl.when(z + c > 0)(tails[0].start)

    @pl.when(z + c == planes)
    def _():
        r.tail_in[...] = jnp.zeros((8, CH), f32)

    pl.when(z + c < planes)(tails[0].wait_recv)
    r.dx[ROWS - 16 :, 0:CH] = low(
        jnp.concatenate([r.dx[ROWS - 16 : ROWS - 8, 0:CH].astype(f32), r.dpre[0:8, :] + r.tail_in[...]], axis=0)
    )

    def weights_a(j):
        at = at_rows(j, 512)
        r.part_a[:, at] = low(dot(r.normed[...], r.dx[:, at], TRANS))

    loop(0, 4, weights_a)
    background(100)
    reduce_a = Reduce(r.part_a, r.grad_a, 48, "columns", red_a, planes)
    last_steps = reduce_a.steps()
    for step in last_steps[:8]:
        step()
    ngain = jnp.zeros((8, 768), f32)
    for k in range(8):
        rows = slice(32 * k, 32 * k + 32)
        dnormed = dot(r.dz[rows, :], r.wz_full[...], TRANS_B) + dot(r.dx[rows, :], r.wa[...], TRANS_B)
        u = r.tok[HALO + 32 * k : HALO + 32 * k + 32, :].astype(f32)
        scale = lax.rsqrt(jnp.mean(u * u, axis=-1, keepdims=True) + EPSILON)
        weighed = dnormed * u * scale
        ngain = ngain + weighed[0:8] + weighed[8:16] + weighed[16:24] + weighed[24:32]
        a = r.ngain[5:6, :] * dnormed
        grad = scale * (a - u * (scale * scale) * jnp.mean(u * a, axis=-1, keepdims=True))
        r.gtok[rows, :] = low(r.cot_own[rows, :].astype(f32) + grad)
    grads = Shuffle(r.gtok, r.tokens_out, r.back_sem, back=True)
    grads.start()
    ngain = jnp.sum(ngain, axis=0, keepdims=True)
    ggain = jnp.sum(r.ggain[...], axis=0, keepdims=True)
    lane_heads = jnp.concatenate([gbias[:, 0:H], glog[:, 0:H], gskip[:, 0:H], jnp.zeros((1, 128 - 3 * H), f32)], axis=1)
    for k in range(16):
        convs = jnp.concatenate([r.gconv[0:5, 112 * k : 112 * k + 112], jnp.zeros((5, 16), f32)], axis=1)
        first = jnp.concatenate([ngain[:, 48 * k : 48 * k + 48], jnp.zeros((1, 80), f32)], axis=1)
        second = jnp.concatenate([ggain[:, 96 * k : 96 * k + 96], jnp.zeros((1, 32), f32)], axis=1)
        r.table[k] = jnp.concatenate([convs, first, second, lane_heads], axis=0)

    def to_all(k, act):
        other = lax.rem(me + k, 16)
        for far in range(2):
            copy = pltpu.make_async_remote_copy(
                src_ref=r.table.at[other], dst_ref=r.inbox.at[c, me], send_sem=r.table_sem.at[0, far, other],
                recv_sem=r.table_sem.at[1, c, me], device_id=(far, other), device_id_type=MESH,
            )
            pl.when(jnp.logical_or(k > 0, far != c))(functools.partial(act, copy))

    def from_all(k):
        other = lax.rem(me + k, 16)
        for far in range(2):
            copy = pltpu.make_async_remote_copy(
                src_ref=r.table.at[other], dst_ref=r.inbox.at[far, other], send_sem=r.table_sem.at[0, far, other],
                recv_sem=r.table_sem.at[1, far, other], device_id=(far, other), device_id_type=MESH,
            )
            pl.when(jnp.logical_or(k > 0, far != c))(copy.wait_recv)

    loop(0, 16, lambda k: to_all(k, lambda copy: copy.start()))
    r.inbox[c, me] = r.table[me]
    for step in last_steps[8:]:
        step()
    loop(0, 16, from_all)
    r.small_out[...] = jnp.sum(jnp.sum(r.inbox[...], axis=0), axis=0)
    loop(0, 16, lambda k: to_all(k, lambda copy: copy.wait_send()))
    for item in (reduce_out, reduce_z, reduce_a, forward, backward, cots, acts, grads):
        item.finish()
    acts.arrived()
    grads.arrived()
    share.wait_send()
    pl.when(z + c > 0)(tails[0].wait_send)


def rest(given, planes):
    f32, bf16 = jnp.float32, jnp.bfloat16
    shape = jax.ShapeDtypeStruct
    named = rest_scratch(planes)
    extra = Chain.scratch() + Chain.scratch()
    extra += Reduce.scratch(48, WIDE, "columns", planes) + Reduce.scratch(48, DI, "columns", planes) + Reduce.scratch(96, 768, "rows", planes)
    return pl.pallas_call(
        functools.partial(rest_kernel, planes, list(named)),
        out_shape=[
            shape((2, 128, 768), bf16), shape((2, 128, 768), bf16), shape((48, WIDE), f32),
            shape((48, DI), f32), shape((96, 768), f32), shape((8, 128), f32),
        ],
        in_specs=[VMEM] * len(REST_IN),
        out_specs=[VMEM] * len(REST_OUT),
        scratch_shapes=list(named.values()) + extra,
        compiler_params=pltpu.CompilerParams(collective_id=1, has_side_effects=True, vmem_limit_bytes=62 << 20),
    )(*given)


def fast_body(
    planes, tokens, cotangent, segments, norm_gain, w_in, conv_weight, conv_bias, step_bias, log_rate, skip_gain, gate_gain, w_out
):
    f32 = jnp.float32
    segf = jnp.broadcast_to((segments.astype(f32) + 1.0)[:, 0, None, :], (2, 8, 128))

    def padded(rows):
        return jnp.pad(rows.astype(f32), ((0, 0), (0, 128 - rows.shape[1])))

    nothing = jnp.zeros((1, 128), f32)
    small = jnp.concatenate(
        [padded(conv_weight), padded(conv_bias[None]), padded(norm_gain[None]), padded(gate_gain[None]), nothing], axis=0
    )
    heads = jnp.concatenate([padded(jnp.stack([step_bias, log_rate, skip_gain])), jnp.zeros((5, 128), f32)], axis=0)
    wa = jnp.pad(w_in[:, DI:], ((0, 0), (0, WIDE - (w_in.shape[1] - DI))))
    wa_full, table, tok, seg, normed, proj, conv, gain, ngain = enter(tokens[:, 0], segf, small, wa, planes)
    acts, grad_tokens, grad_a, grad_z, grad_out, sums = rest(
        (wa_full, tok, seg, normed, proj, conv, gain, ngain, heads, w_in[:, :DI], w_out, cotangent[:, 0]), planes
    )
    return (
        acts[:, None],
        grad_tokens[:, None],
        sums[5, 0:48],
        jnp.concatenate([grad_z, grad_a[:, : w_in.shape[1] - DI]], axis=1),
        sums[0:4, 0:112],
        sums[4, 0:112],
        sums[7, 0:H],
        sums[7, H : 2 * H],
        sums[7, 2 * H : 3 * H],
        sums[6, 0:96],
        grad_out,
    )


def solution(mesh):
    in_specs = (
        P(None, "dp", "seq", None),
        P(None, "dp", "seq", None),
        P(None, "dp", "seq"),
        P("seq"),
        P("seq", None),
        P(None, "seq"),
        P("seq"),
        P(),
        P(),
        P(),
        P("seq"),
        P("seq", None),
    )
    out_specs = (
        P(None, "dp", "seq", None),
        P(None, "dp", "seq", None),
        P("seq"),
        P("seq", None),
        P(None, "seq"),
        P("seq"),
        P(),
        P(),
        P(),
        P("seq"),
        P("seq", None),
    )
    work = partial(fast_body, mesh.shape["seq"] // 4) if mesh.shape["seq"] == 16 else body
    return jax.shard_map(work, mesh=mesh, in_specs=in_specs, out_specs=out_specs, check_vma=False)
```

```python
import functools
from functools import partial

import jax
import jax.numpy as jnp
from jax import lax
from jax.experimental import pallas as pl
from jax.experimental.pallas import tpu as pltpu
from jax.sharding import PartitionSpec as P

DI = 1536
H = 24
P_SIZE = 64
N = 128
KC = 4
CH = 1792


EPSILON = 1e-05
HIGHEST = lax.Precision.HIGHEST


def passed_along(array, axis, by):
    devices = lax.axis_size(axis)
    pairs = [(i, i + by) for i in range(devices) if 0 <= i + by < devices]
    return lax.ppermute(array, axis, pairs)


def prefix(array, axis, combine, identity, reverse):
    devices, place = (lax.axis_size(axis), lax.axis_index(axis))
    everything = jax.tree.map(lambda part: lax.all_gather(part, axis), array)
    start = jax.tree.map(
        lambda part, zero: jnp.broadcast_to(jnp.asarray(zero, part.dtype), part.shape),
        array,
        identity,
    )

    def lap(k, before):
        at = devices - 1 - k if reverse else k
        reached = at > place if reverse else at < place
        new = combine(before, jax.tree.map(lambda part: part[at], everything))
        return jax.tree.map(lambda a, b: jnp.where(reached, a, b), new, before)

    return lax.fori_loop(0, devices, lap, start)


def for_sending(array):
    return jax.tree.map(lambda a: a.astype(jnp.bfloat16) if a.dtype == jnp.float32 else a, array)


def rms_scale(values, gain_vec):
    return (
        values * lax.rsqrt(jnp.mean(values * values, axis=-1, keepdims=True) + EPSILON) * gain_vec
    )


def causal_conv(padded, seg_pad, seg_one, kernel, offset):
    length_t = seg_one.shape[0]
    total = jnp.zeros((length_t, padded.shape[1]), jnp.float32) + offset[None, :]
    for tap_index in range(KC):
        window = padded[tap_index : tap_index + length_t]
        same_doc = (seg_pad[tap_index : tap_index + length_t] == seg_one).astype(jnp.float32)
        total = total + kernel[tap_index][None, :] * window * same_doc[:, None]
    return total


def cumulative(step_size, rate):
    length_t = step_size.shape[0]
    lower = jnp.tril(jnp.ones((length_t, length_t), jnp.float32))
    return jnp.dot(lower, step_size * rate[None, :], precision=HIGHEST)


def block_state(inner, b_proj, step_size, rate, seg_one, previous):
    cum_decay = cumulative(step_size, rate)
    last_seg = seg_one[-1]
    to_end = (
        jnp.where((seg_one == last_seg)[:, None], jnp.exp(cum_decay[-1][None, :] - cum_decay), 0.0)
        * step_size
    )
    state_part = jnp.einsum("uhp,un->hpn", inner * to_end[:, :, None], b_proj, precision=HIGHEST)
    through = jnp.logical_and(seg_one[0] == last_seg, seg_one[0] == previous).astype(jnp.float32)
    return (state_part, jnp.exp(cum_decay[-1]) * through)


def block_output(inner, b_proj, c_proj, step_size, rate, state_in, seg_one, previous):
    cum_decay = cumulative(step_size, rate)
    length_t = seg_one.shape[0]
    row_index = lax.broadcasted_iota(jnp.int32, (length_t, length_t), 0)
    col_index = lax.broadcasted_iota(jnp.int32, (length_t, length_t), 1)
    allowed = jnp.logical_and(row_index >= col_index, seg_one[:, None] == seg_one[None, :])[
        :, :, None
    ]
    spread = cum_decay[:, None, :] - cum_decay[None, :, :]
    decays = jnp.where(allowed, jnp.exp(jnp.where(allowed, spread, 0.0)), 0.0)
    scores = jnp.dot(c_proj, b_proj.T, precision=HIGHEST)
    weights = decays * scores[:, :, None] * step_size[None, :, :]
    local_part = jnp.einsum("tuh,uhp->thp", weights, inner, precision=HIGHEST)
    carried = (seg_one == previous).astype(jnp.float32)[:, None] * jnp.exp(cum_decay)
    return local_part + carried[:, :, None] * jnp.einsum(
        "tn,hpn->thp", c_proj, state_in, precision=HIGHEST
    )


def prepare(proj_out, tail_rows, kernel, offset, step_bias, log_rate, tail_seg, seg_one):
    length_t = proj_out.shape[0]
    padded = jnp.concatenate([tail_rows, proj_out[:, DI : DI + CH]], axis=0)
    seg_pad = jnp.concatenate([tail_seg, seg_one])
    activated = jax.nn.silu(causal_conv(padded, seg_pad, seg_one, kernel, offset))
    inner = activated[:, :DI].reshape(length_t, H, P_SIZE)
    b_proj = activated[:, DI : DI + N]
    c_proj = activated[:, DI + N :]
    step_size = jax.nn.softplus(proj_out[:, DI + CH :] + step_bias[None, :])
    rate = -jnp.exp(log_rate)
    return (inner, b_proj, c_proj, step_size, rate, proj_out[:, :DI])


def finish(
    inner,
    b_proj,
    c_proj,
    step_size,
    rate,
    gate_in,
    state_in,
    skip_gain,
    gate_gain,
    seg_one,
    previous,
):
    length_t = inner.shape[0]
    mixed = block_output(inner, b_proj, c_proj, step_size, rate, state_in, seg_one, previous)
    mixed = mixed + skip_gain[None, :, None] * inner
    gated = mixed.reshape(length_t, DI) * jax.nn.silu(gate_in)
    return rms_scale(gated, gate_gain)


def chain_link(earlier, later):
    return (earlier[0] * later[0], later[0][:, None, None] * earlier[1] + later[1])


def body(
    tokens,
    cotangent,
    segments,
    norm_gain,
    w_in,
    conv_weight,
    conv_bias,
    step_bias,
    log_rate,
    skip_gain,
    gate_gain,
    w_out,
):
    batches = tokens.shape[0]
    length_t = tokens.shape[2]
    halo_rows = KC - 1
    identity = (jnp.ones((H,), jnp.float32), jnp.zeros((H, P_SIZE, N), jnp.float32))
    totals = None
    head_totals = (
        jnp.zeros((H,), jnp.float32),
        jnp.zeros((H,), jnp.float32),
        jnp.zeros((H,), jnp.float32),
    )
    act_list = []
    grad_list = []
    for micro in range(batches):
        gathered = (
            lax.all_gather(w_in, "seq", axis=0, tiled=True),
            lax.all_gather(w_out, "seq", axis=0, tiled=True),
            lax.all_gather(conv_weight, "seq", axis=1, tiled=True),
            lax.all_gather(conv_bias, "seq", axis=0, tiled=True),
            lax.all_gather(norm_gain, "seq", axis=0, tiled=True),
            lax.all_gather(gate_gain, "seq", axis=0, tiled=True),
        )
        in_full = gathered[0]
        out_full = gathered[1]
        kernel = gathered[2].astype(jnp.float32)
        offset = gathered[3].astype(jnp.float32)
        gain_one = gathered[4].astype(jnp.float32)
        gain_two = gathered[5].astype(jnp.float32)
        resid = tokens[micro, 0].astype(jnp.float32)
        seg_one = segments[micro, 0].astype(jnp.float32) + 1.0
        normed, norm_back = jax.vjp(rms_scale, resid, gain_one)
        normed_low = normed.astype(jnp.bfloat16)
        proj_out = jnp.dot(normed_low, in_full, preferred_element_type=jnp.float32)
        tail_rows, tail_seg = passed_along(
            (proj_out[length_t - halo_rows :, DI : DI + CH], seg_one[length_t - halo_rows :]),
            "seq",
            1,
        )
        previous = tail_seg[halo_rows - 1]
        prepared, prep_back = jax.vjp(
            partial(prepare, tail_seg=tail_seg, seg_one=seg_one),
            proj_out,
            tail_rows,
            kernel,
            offset,
            step_bias,
            log_rate,
        )
        inner, b_proj, c_proj, step_size, rate, gate_in = prepared
        state_out, state_back = jax.vjp(
            partial(block_state, seg_one=seg_one, previous=previous), inner, b_proj, step_size, rate
        )
        state_part, through = state_out
        state_in = prefix((through, state_part), "seq", chain_link, identity, False)[1]
        normed_two, finish_back = jax.vjp(
            partial(finish, seg_one=seg_one, previous=previous),
            inner,
            b_proj,
            c_proj,
            step_size,
            rate,
            gate_in,
            state_in,
            skip_gain,
            gain_two,
        )
        gate_low = normed_two.astype(jnp.bfloat16)
        branch = jnp.dot(gate_low, out_full, preferred_element_type=jnp.float32)
        act_list.append((resid + branch).astype(jnp.bfloat16))
        cot_low = cotangent[micro, 0]
        again = (
            lax.all_gather(w_in, "seq", axis=0, tiled=True),
            lax.all_gather(w_out, "seq", axis=0, tiled=True),
        )
        in_back = again[0]
        out_back = again[1]
        out_term = lax.dot_general(
            gate_low, cot_low, (((0,), (0,)), ((), ())), preferred_element_type=jnp.float32
        )
        grad_gate = lax.dot_general(
            cot_low, out_back, (((1,), (1,)), ((), ())), preferred_element_type=jnp.float32
        )
        g_inner, g_bproj, g_cproj, g_step, g_rate, g_gate_in, g_state_in, g_skip, g_gain_two = (
            finish_back(grad_gate)
        )
        carried = prefix((through, g_state_in), "seq", chain_link, identity, True)[1]
        h_inner, h_bproj, h_step, h_rate = state_back(
            (carried, jnp.sum(carried * state_in, axis=(1, 2)))
        )
        g_proj, g_tail, g_kernel, g_offset, g_bias, g_log = prep_back(
            (
                g_inner + h_inner,
                g_bproj + h_bproj,
                g_cproj,
                g_step + h_step,
                g_rate + h_rate,
                g_gate_in,
            )
        )
        returned = passed_along(g_tail, "seq", -1)
        width_after = proj_out.shape[1] - DI - CH
        g_proj = g_proj + jnp.pad(returned, ((length_t - halo_rows, 0), (DI, width_after)))
        proj_grad_low = g_proj.astype(jnp.bfloat16)
        grad_normed = lax.dot_general(
            proj_grad_low, in_back, (((1,), (1,)), ((), ())), preferred_element_type=jnp.float32
        )
        grad_resid, g_gain_one = norm_back(grad_normed)
        grad_list.append((cot_low.astype(jnp.float32) + grad_resid).astype(jnp.bfloat16))
        in_shard = lax.psum_scatter(
            lax.dot_general(
                normed_low,
                proj_grad_low,
                (((0,), (0,)), ((), ())),
                preferred_element_type=jnp.float32,
            ),
            "seq",
            scatter_dimension=0,
            tiled=True,
        )
        shards = (
            lax.psum_scatter(out_term, "seq", scatter_dimension=0, tiled=True),
            lax.psum_scatter(g_kernel, "seq", scatter_dimension=1, tiled=True),
            lax.psum_scatter(g_offset, "seq", scatter_dimension=0, tiled=True),
            lax.psum_scatter(g_gain_one, "seq", scatter_dimension=0, tiled=True),
            lax.psum_scatter(g_gain_two, "seq", scatter_dimension=0, tiled=True),
        )
        this_round = (in_shard, shards[0], shards[1], shards[2], shards[3], shards[4])
        if totals is None:
            totals = this_round
        else:
            totals = tuple((prior + fresh for prior, fresh in zip(totals, this_round)))
        head_totals = (head_totals[0] + g_bias, head_totals[1] + g_log, head_totals[2] + g_skip)
    summed = jax.tree.map(
        lambda part: part.astype(jnp.float32), lax.psum(for_sending(totals), "dp")
    )
    heads = lax.psum((head_totals[0], head_totals[1], head_totals[2]), ("dp", "seq"))
    activations = jnp.stack(act_list)[:, None]
    grad_tokens = jnp.stack(grad_list)[:, None]
    return (
        activations,
        grad_tokens,
        summed[4],
        summed[0],
        summed[2],
        summed[3],
        heads[0],
        heads[1],
        heads[2],
        summed[5],
        summed[1],
    )


MESH = pl.DeviceIdType.MESH


def chip(x, y, z):
    return z * 4 + y * 2 + x


def place():
    core = lax.axis_index("dp")
    at = lax.axis_index("seq")
    return at % 2, (at // 2) % 2, at // 4, core


def meet_all(planes):
    barrier = pltpu.get_barrier_semaphore()
    me = lax.axis_index("seq")
    core = lax.axis_index("dp")
    count = planes * 4

    def greet(k, carry):
        other = lax.rem(me + k, count)
        for far in range(2):

            @pl.when(jnp.logical_or(k > 0, far != core))
            def _():
                pl.semaphore_signal(barrier, inc=1, device_id=(far, other), device_id_type=MESH)

        return carry

    lax.fori_loop(0, count, greet, 0)
    pl.semaphore_wait(barrier, 2 * count - 1)


COLUMN, SIDE_X, SIDE_Y, HALF_X, HALF_Y, MATE_Z, MATE_X, MATE_Y, MATE_HX, MATE_HY = range(10)


class Gather:
    def __init__(self, whole, rows, quarter, sems, planes):
        self.whole, self.rows, self.quarter, self.sems, self.planes = whole, rows, quarter, sems, planes
        self.x, self.y, self.z, self.core = place()

    def region(self, block, core, part=None):
        width = self.whole.shape[1] // 2
        start = pl.multiple_of(block * self.rows, 16)
        left = pl.multiple_of(core * width, 128)
        if part is None:
            return self.whole.at[pl.ds(start, self.rows), pl.ds(left, width)]
        if self.quarter == "rows":
            half = self.rows // 2
            return self.whole.at[pl.ds(pl.multiple_of(start + part * half, 16), half), pl.ds(left, width)]
        half = width // 2
        return self.whole.at[pl.ds(start, self.rows), pl.ds(pl.multiple_of(left + part * half, 128), half)]

    def copy(self, kind, leaves, lands, block, core, part, device):
        region = self.region(block, core, part)
        return pltpu.make_async_remote_copy(
            src_ref=region,
            dst_ref=region,
            send_sem=self.sems.at[0, kind, leaves],
            recv_sem=self.sems.at[1, kind, lands],
            device_id=device,
            device_id_type=MESH,
        )

    def out(self, kind, far):
        x, y, z, c = self.x, self.y, self.z, self.core
        if kind == COLUMN:
            return self.copy(kind, far, z, chip(x, y, z), c, None, (c, chip(x, y, far)))
        own, by_x, by_y, across = chip(x, y, far), chip(1 - x, y, far), chip(x, 1 - y, far), chip(1 - x, 1 - y, far)
        mate = (1 - c, chip(x, y, z))
        to_x, to_y = (c, chip(1 - x, y, z)), (c, chip(x, 1 - y, z))
        block, part, device = {
            SIDE_X: (own, None, to_x),
            SIDE_Y: (own, None, to_y),
            HALF_X: (by_y, 1, to_x),
            HALF_Y: (by_x, 0, to_y),
            MATE_Z: (own, None, mate),
            MATE_X: (by_x, None, mate),
            MATE_Y: (by_y, None, mate),
            MATE_HX: (across, 1, mate),
            MATE_HY: (across, 0, mate),
        }[kind]
        return self.copy(kind, far, far, block, c, part, device)

    def send(self, kind, far):
        self.out(kind, far).start()

    def arrived(self, kind, far):
        x, y = self.x, self.y
        own, by_x, by_y, across = chip(x, y, far), chip(1 - x, y, far), chip(x, 1 - y, far), chip(1 - x, 1 - y, far)
        block, part, mine = {
            COLUMN: (own, None, True),
            SIDE_X: (by_x, None, True),
            SIDE_Y: (by_y, None, True),
            HALF_X: (across, 1, True),
            HALF_Y: (across, 0, True),
            MATE_Z: (own, None, False),
            MATE_X: (by_x, None, False),
            MATE_Y: (by_y, None, False),
            MATE_HX: (across, 1, False),
            MATE_HY: (across, 0, False),
        }[kind]
        core = self.core if mine else 1 - self.core
        self.copy(kind, far, far, block, core, part, (1 - self.core, chip(x, y, self.z))).wait_recv()

    def each(self, distance, act):
        for sign in (-1, 1) if distance else (1,):
            far = self.z + sign * distance
            if distance:
                pl.when(jnp.logical_and(far >= 0, far < self.planes))(functools.partial(act, far))
            else:
                act(far)

    def begin_sides(self):
        self.send(SIDE_X, self.z)
        self.send(SIDE_Y, self.z)

    def begin_column(self):
        for distance in range(1, self.planes):
            self.each(distance, lambda far: self.send(COLUMN, far))

    def begin(self):
        self.begin_sides()
        self.begin_column()

    def column(self, distance):
        def act(far):
            self.arrived(COLUMN, far)
            self.send(SIDE_X, far)
            self.send(SIDE_Y, far)
            self.send(MATE_Z, far)

        self.each(distance, act)

    def sides(self, distance):
        def act(far):
            self.arrived(SIDE_X, far)
            self.send(HALF_Y, far)
            self.send(MATE_X, far)
            self.arrived(SIDE_Y, far)
            self.send(HALF_X, far)
            self.send(MATE_Y, far)

        self.each(distance, act)

    def diagonal(self, distance):
        def act(far):
            self.arrived(HALF_Y, far)
            self.send(MATE_HY, far)
            self.arrived(HALF_X, far)
            self.send(MATE_HX, far)

        self.each(distance, act)

    def whole_here(self):
        for distance in range(self.planes):

            def act(far):
                for kind in (MATE_X, MATE_Y, MATE_HX, MATE_HY) + ((MATE_Z,) if distance else ()):
                    self.arrived(kind, far)

            self.each(distance, act)

    def finish(self):
        for distance in range(self.planes):

            def act(far):
                kinds = (SIDE_X, SIDE_Y, HALF_X, HALF_Y, MATE_X, MATE_Y, MATE_HX, MATE_HY)
                for kind in kinds + ((MATE_Z, COLUMN) if distance else ()):
                    self.out(kind, far).wait_send()

            self.each(distance, act)


def gather_sems(planes):
    return pltpu.SemaphoreType.DMA((2, 10, planes))


class Reduce:
    X, Y, HX, HY, COLUMN, MATE, LAST = range(7)

    @staticmethod
    def scratch(rows, width, quarter, planes):
        half = width // 2
        corner = (rows // 2, half) if quarter == "rows" else (rows, half // 2)
        bf16 = jnp.bfloat16
        return [
            pltpu.VMEM((4 * planes * rows, half), bf16),
            pltpu.VMEM((3, planes, rows, half), bf16),
            pltpu.VMEM((2, planes) + corner, bf16),
            pltpu.SemaphoreType.DMA((2, 7, planes)),
        ]

    def __init__(self, part, out, rows, quarter, scratch, planes):
        self.part, self.out, self.rows, self.quarter, self.planes = part, out, rows, quarter, planes
        self.mate_in, self.side_in, self.corner_in, self.sems = scratch
        self.x, self.y, self.z, self.core = place()
        self.half = part.shape[1] // 2

    def block(self, owner, part=None):
        start = pl.multiple_of(owner * self.rows, 16)
        left = pl.multiple_of(self.core * self.half, 128)
        if part is None:
            return pl.ds(start, self.rows), pl.ds(left, self.half)
        if self.quarter == "rows":
            return pl.ds(pl.multiple_of(start + part * (self.rows // 2), 16), self.rows // 2), pl.ds(left, self.half)
        quarter = self.half // 2
        return pl.ds(start, self.rows), pl.ds(pl.multiple_of(left + part * quarter, 128), quarter)

    def copy(self, kind, far, source, target, device):
        return pltpu.make_async_remote_copy(
            src_ref=source,
            dst_ref=target,
            send_sem=self.sems.at[0, kind, far],
            recv_sem=self.sems.at[1, kind, far],
            device_id=device,
            device_id_type=MESH,
        )

    def move(self, kind, far):
        x, y, z, c = self.x, self.y, self.z, self.core
        part = self.part
        to_x, to_y, mate = (c, chip(1 - x, y, z)), (c, chip(x, 1 - y, z)), (1 - c, chip(x, y, z))
        if kind == self.X:
            return self.copy(kind, far, part.at[self.block(chip(1 - x, y, far))], self.side_in.at[0, far], to_x)
        if kind == self.Y:
            return self.copy(kind, far, part.at[self.block(chip(x, 1 - y, far))], self.side_in.at[1, far], to_y)
        if kind == self.HX:
            return self.copy(kind, far, part.at[self.block(chip(1 - x, 1 - y, far), 0)], self.corner_in.at[0, far], to_x)
        if kind == self.HY:
            return self.copy(kind, far, part.at[self.block(chip(1 - x, 1 - y, far), 1)], self.corner_in.at[1, far], to_y)
        if kind == self.COLUMN:
            return pltpu.make_async_remote_copy(
                src_ref=part.at[self.block(chip(x, y, far))],
                dst_ref=self.side_in.at[2, z],
                send_sem=self.sems.at[0, kind, far],
                recv_sem=self.sems.at[1, kind, z],
                device_id=(c, chip(x, y, far)),
                device_id_type=MESH,
            )
        if kind == self.MATE:
            rows = pl.ds(pl.multiple_of(far * 4 * self.rows, 16), 4 * self.rows)
            left = pl.multiple_of((1 - c) * self.half, 128)
            return self.copy(kind, far, part.at[rows, pl.ds(left, self.half)], self.mate_in.at[rows], mate)
        left = pl.multiple_of(c * self.half, 128)
        region = self.out.at[:, pl.ds(left, self.half)]
        return self.copy(kind, 0, region, region, mate)

    def add(self, at, *refs):
        total = self.part[at].astype(jnp.float32)
        for ref in refs:
            total = total + ref[...].astype(jnp.float32)
        self.part[at] = low(total)

    def each(self, distance, act):
        for sign in (-1, 1) if distance else (1,):
            far = self.z + sign * distance
            if distance:
                pl.when(jnp.logical_and(far >= 0, far < self.planes))(functools.partial(act, far, sign))
            else:
                act(far, sign)

    def start(self, distance):
        self.each(distance, lambda far, sign: self.move(self.MATE, far).start())

    def fold(self, distance):
        def act(far, sign):
            self.move(self.MATE, far).wait_recv()

            def rows(k, carry):
                start = pl.multiple_of((far * 4 + k) * self.rows, 16)
                left = pl.multiple_of(self.core * self.half, 128)
                self.add((pl.ds(start, self.rows), pl.ds(left, self.half)), self.mate_in.at[pl.ds(start, self.rows)])
                return carry

            lax.fori_loop(0, 4, rows, 0)
            self.move(self.HX, far).start()
            self.move(self.HY, far).start()

        self.each(distance, act)

    def sides(self, distance):
        x, y = self.x, self.y

        def act(far, sign):
            self.move(self.HX, far).wait_recv()
            self.add(self.block(chip(x, 1 - y, far), 0), self.corner_in.at[0, far])
            self.move(self.Y, far).start()
            self.move(self.HY, far).wait_recv()
            self.add(self.block(chip(1 - x, y, far), 1), self.corner_in.at[1, far])
            self.move(self.X, far).start()

        self.each(distance, act)

    def column(self, distance):
        x, y, z = self.x, self.y, self.z

        def act(far, sign):
            self.move(self.X, far).wait_recv()
            self.move(self.Y, far).wait_recv()
            if distance:
                self.add(self.block(chip(x, y, far)), self.side_in.at[0, far], self.side_in.at[1, far])
                self.move(self.COLUMN, far).start()

        self.each(distance, act)

    def close(self):
        z = self.z
        at = self.block(chip(self.x, self.y, z))
        left = pl.multiple_of(self.core * self.half, 128)
        here = (slice(None), pl.ds(left, self.half))
        total = self.part[at].astype(jnp.float32)
        self.out[here] = total + self.side_in[0, z].astype(jnp.float32) + self.side_in[1, z].astype(jnp.float32)
        for distance in range(self.planes - 1, 0, -1):

            def act(far, sign):
                self.copy(self.COLUMN, far, self.side_in.at[2, far], self.side_in.at[2, far], (self.core, chip(self.x, self.y, far))).wait_recv()
                self.out[here] = self.out[here] + self.side_in[2, far].astype(jnp.float32)

            self.each(distance, act)
        self.move(self.LAST, 0).start()

    def finish(self):
        last = self.move(self.LAST, 0)
        left = pl.multiple_of((1 - self.core) * self.half, 128)
        region = self.out.at[:, pl.ds(left, self.half)]
        self.copy(self.LAST, 0, region, region, (1 - self.core, chip(self.x, self.y, self.z))).wait_recv()
        last.wait_send()
        for distance in range(self.planes):

            def act(far, sign):
                for kind in (self.MATE, self.HX, self.HY, self.X, self.Y):
                    self.move(kind, far).wait_send()
                if distance:
                    self.move(self.COLUMN, far).wait_send()

            self.each(distance, act)


class Chain:
    CUT = 6

    @staticmethod
    def scratch():
        half = pltpu.VMEM((N, DI // 2), jnp.bfloat16)
        wide = pltpu.VMEM((N, DI // 2), jnp.float32)
        return [half, half, half, half, half, half, wide, wide, pltpu.SemaphoreType.DMA((2, 2 + Chain.CUT))]

    def __init__(self, part, result, factors, scratch, lead, planes):
        self.part, self.result, self.factors, self.lead, self.planes = part, result, factors, lead, planes
        self.give, self.take, self.leave, self.come, self.back, self.again, self.total, self.front, self.sems = scratch
        self.x, self.y, self.z, self.core = place()
        self.half = DI // 2
        self.leads = self.core == lead
        self.ahead = 1 if lead == 0 else -1
        self.first = self.z == (0 if lead == 0 else planes - 1)
        self.last = self.z == (planes - 1 if lead == 0 else 0)

    def own(self):
        return pl.ds(pl.multiple_of(self.core * self.half, 128), self.half)

    def other(self):
        return pl.ds(pl.multiple_of((1 - self.core) * self.half, 128), self.half)

    def copy(self, k, source, target, device):
        return pltpu.make_async_remote_copy(
            src_ref=source,
            dst_ref=target,
            send_sem=self.sems.at[0, k],
            recv_sem=self.sems.at[1, k],
            device_id=device,
            device_id_type=MESH,
        )

    def mate(self):
        return (1 - self.core, chip(self.x, self.y, self.z))

    def trade(self):
        return self.copy(0, self.give, self.take, self.mate())

    def returned(self):
        return self.copy(1, self.back, self.again, self.mate())

    def hop(self, k):
        cut = self.half // self.CUT
        at = (slice(None), pl.ds(k * cut, cut))
        return self.copy(
            2 + k, self.leave.at[at], self.come.at[at], (self.core, chip(self.x, self.y, self.z + self.ahead))
        )

    def start(self):
        self.give[...] = low(self.part[:, self.other()])
        self.trade().start()

    def rows(self):
        return self.factors[self.lead, 0:1, self.own()], self.factors[1 - self.lead, 0:1, self.own()]

    def merge(self):
        self.trade().wait_recv()
        own = self.part[:, self.own()]
        got = self.take[...].astype(jnp.float32)
        ahead, behind = jnp.where(self.leads, own, got), jnp.where(self.leads, got, own)
        _, following = self.rows()
        self.front[...] = ahead
        self.total[...] = following * ahead + behind

        @pl.when(self.first)
        def _():
            self.come[...] = jnp.zeros(self.come.shape, self.come.dtype)
            self.leave[...] = low(self.total[...])
            for k in range(self.CUT):
                self.hop(k).start()

    def pass_on(self):
        leading, following = self.rows()
        cut = self.half // self.CUT

        @pl.when(jnp.logical_not(self.first))
        def _():
            for k in range(self.CUT):
                self.hop(k).wait_recv()

                @pl.when(jnp.logical_not(self.last))
                def _():
                    at = (slice(None), slice(k * cut, (k + 1) * cut))
                    both = (leading * following)[:, k * cut : (k + 1) * cut]
                    self.leave[at] = low(both * self.come[at].astype(jnp.float32) + self.total[at])
                    self.hop(k).start()

        came = self.come[...].astype(jnp.float32)
        later = low(leading * came + self.front[...])
        self.back[...] = jnp.where(self.leads, later.astype(jnp.float32), came).astype(jnp.bfloat16)
        self.returned().start()
        self.result[:, self.own()] = jnp.where(self.leads, came, later.astype(jnp.float32)).astype(jnp.bfloat16)

    def close(self):
        self.returned().wait_recv()
        self.result[:, self.other()] = self.again[...]

    def finish(self):
        self.trade().wait_send()
        self.returned().wait_send()

        @pl.when(jnp.logical_not(self.last))
        def _():
            for k in range(self.CUT):
                self.hop(k).wait_send()


VMEM = pl.BlockSpec(memory_space=pltpu.VMEM)
ROWS = 256
HALO = 16
WIDE = 2048
TRANS = (((0,), (0,)), ((), ()))
TRANS_B = (((1,), (1,)), ((), ()))


def dot(a, b, dims=(((1,), (0,)), ((), ()))):
    return lax.dot_general(a, b, dims, preferred_element_type=jnp.float32)


def low(a):
    return a.astype(jnp.bfloat16)


class Shuffle:
    def __init__(self, source, target, sems, offset=0, back=False):
        self.source, self.target, self.sems, self.offset, self.back = source, target, sems, offset, back
        self.x, self.y, self.z, self.core = place()

    def piece(self, k):
        x, y, z, c = self.x, self.y, self.z, self.core
        rows = 128
        if self.back:
            source = self.source.at[pl.ds(rows * k, rows)]
            target = self.target.at[x]
        else:
            source = self.source.at[k]
            if len(self.target.shape) == len(self.source.shape):
                target = self.target.at[self.offset + x]
            else:
                target = self.target.at[pl.ds(pl.multiple_of(self.offset + rows * x, 16), rows)]
        stays = jnp.logical_and(x == k, y == c)
        local = pltpu.make_async_copy(source, target, self.sems.at[1, x])
        remote = pltpu.make_async_remote_copy(
            src_ref=source,
            dst_ref=target,
            send_sem=self.sems.at[0, k],
            recv_sem=self.sems.at[1, x],
            device_id=(y, chip(k, c, z)),
            device_id_type=MESH,
        )
        return stays, local, remote

    def start(self):
        for k in range(2):
            stays, local, remote = self.piece(k)
            pl.when(stays)(local.start)
            pl.when(jnp.logical_not(stays))(remote.start)

    def arrived(self):
        x, y, z, c = self.x, self.y, self.z, self.core
        for k in range(2):
            if self.back:
                target = self.target.at[k]
            elif len(self.target.shape) == len(self.source.shape):
                target = self.target.at[self.offset + k]
            else:
                target = self.target.at[pl.ds(self.offset + 128 * k, 128)]
            stays = jnp.logical_and(x == k, y == c)
            local = pltpu.make_async_copy(target, target, self.sems.at[1, k])
            remote = pltpu.make_async_remote_copy(
                src_ref=target,
                dst_ref=target,
                send_sem=self.sems.at[0, k],
                recv_sem=self.sems.at[1, k],
                device_id=(y, chip(k, c, z)),
                device_id_type=MESH,
            )
            pl.when(stays)(local.wait)
            pl.when(jnp.logical_not(stays))(remote.wait_recv)

    def finish(self):
        for k in range(2):
            stays, local, remote = self.piece(k)
            pl.when(jnp.logical_not(stays))(remote.wait_send)


class Before:
    def __init__(self, source, target, sems, planes):
        self.source, self.target, self.sems, self.planes = source, target, sems, planes
        self.x, self.y, self.z, self.core = place()

    def piece(self, m):
        x, y, z, c = self.x, self.y, self.z, self.core
        source = self.source(m)
        return pltpu.make_async_remote_copy(
            src_ref=source,
            dst_ref=self.target,
            send_sem=self.sems.at[0, m],
            recv_sem=self.sems.at[1, 0],
            device_id=(1 - y, chip(m, c, z + y)),
            device_id_type=MESH,
        )

    def when_sending(self):
        return jnp.logical_and(self.x == 1, jnp.logical_or(self.y == 0, self.z < self.planes - 1))

    def start(self):
        @pl.when(self.when_sending())
        def _():
            for m in range(2):
                self.piece(m).start()

    def arrived(self):
        pl.when(self.z + self.core > 0)(self.piece(0).wait_recv)

    def finish(self):
        @pl.when(self.when_sending())
        def _():
            for m in range(2):
                self.piece(m).wait_send()


class ToAll:
    def __init__(self, table, sems, planes):
        self.table, self.sems, self.count = table, sems, planes * 4
        self.me, self.core = lax.axis_index("seq"), lax.axis_index("dp")

    def copy(self, block, other):
        return pltpu.make_async_remote_copy(
            src_ref=self.table.at[block],
            dst_ref=self.table.at[block],
            send_sem=self.sems.at[0, other],
            recv_sem=self.sems.at[1, block],
            device_id=(self.core, other),
            device_id_type=MESH,
        )

    def over(self, act):
        def one(k, carry):
            act(lax.rem(self.me + k, self.count))
            return carry

        lax.fori_loop(1, self.count, one, 0)

    def start(self):
        self.over(lambda other: self.copy(self.me, other).start())

    def arrived(self):
        self.over(lambda other: self.copy(other, self.me).wait_recv())

    def finish(self):
        self.over(lambda other: self.copy(self.me, other).wait_send())


TILE = 128
TILES = DI // TILE


class Names:
    def __init__(self, names, refs):
        for name, ref in zip(names, refs, strict=True):
            setattr(self, name, ref)


def at_tile(j):
    return pl.ds(pl.multiple_of(j * TILE, TILE), TILE)


def at_rows(k, rows):
    return pl.ds(pl.multiple_of(k * rows, rows), rows)


def loop(low_end, high_end, act):
    def one(k, carry):
        act(k)
        return carry

    lax.fori_loop(low_end, high_end, one, 0)


def iota(shape, dim):
    return lax.broadcasted_iota(jnp.int32, shape, dim)


def pieces(a):
    high = low(a)
    rest = a - high.astype(jnp.float32)
    middle = low(rest)
    return high, middle, low(rest - middle.astype(jnp.float32))


def packed(a):
    a = jnp.where(iota(a.shape, 1) < H, a, 0.0)
    high, middle, rest = (part.astype(jnp.float32) for part in pieces(a))
    return low(high + pltpu.roll(middle, 32, 1) + pltpu.roll(rest, 64, 1))


def spread_matrix(width, first=0):
    row, col = iota((128, width), 0), iota((128, width), 1) + first
    return low(jnp.where(jnp.logical_and(row % 32 == col // P_SIZE, row < 96), 1.0, 0.0))


def head_sums(a, j):
    row, col = iota((TILE, 128), 0), iota((TILE, 128), 1)
    pick = low(jnp.where(row // P_SIZE + 2 * j == col, 1.0, 0.0))
    high, middle, _ = pieces(a)
    return dot(jnp.concatenate([high, middle], axis=1), jnp.concatenate([pick, pick], axis=0))


def sigmoid(v):
    return 1.0 / (1.0 + jnp.exp(-v))


GIVEN = ["tok_in", "cot", "seg_in", "small_in", "w_in", "wout"]
MADE = ["act_out", "tokens_out", "grad_a", "grad_z", "grad_out", "small_out"]


def block_scratch(planes):
    f32, bf16 = jnp.float32, jnp.bfloat16
    v = pltpu.VMEM
    dma = pltpu.SemaphoreType.DMA
    two = dma((2, 2))
    return {
        "wa": v((768, WIDE), bf16), "wa_sem": gather_sems(planes), "tok": v((HALO + ROWS, 768), bf16), "seg": v((3, 8, 128), f32),
        "normed": v((HALO + ROWS, 768), bf16), "proj": v((HALO + ROWS, WIDE), f32), "conv": v((8, CH), f32), "gain": v((8, DI), f32),
        "ngain": v((8, 768), f32), "ngrad": v((8, 768), f32), "given": v((16, 8, 128), f32), "numbers": v((2, 8, 128), f32),
        "tok_sem": two, "end_sem": two, "seg_sem": two, "segend_sem": two, "given_sem": dma((2, 16)),
        "wz_full": v((768, DI), bf16), "wout_full": v((DI, 768), bf16), "wz_sem": gather_sems(planes), "wout_sem": gather_sems(planes),
        "cot_own": v((ROWS, 768), bf16), "cot_sem": two, "act_sem": two, "back_sem": two,
        "segcol": v((384, 128), f32), "same": v((KC, ROWS + HALO, 128), f32),
        "pre": v((ROWS, CH), f32), "inner": v((ROWS, DI), f32), "bproj": v((ROWS, N), bf16), "cproj": v((ROWS, N), bf16),
        "cumt": v((H, 8, ROWS), f32), "bar": v((ROWS, ROWS), f32), "scores": v((ROWS, ROWS), f32),
        "step": v((ROWS, 128), f32), "cum": v((ROWS, 128), f32), "ein": v((ROWS, 128), f32), "eout": v((ROWS, 128), f32),
        "stepx": v((ROWS, DI), f32), "einx": v((ROWS, DI), f32), "eoutx": v((ROWS, DI), f32), "cumx": v((ROWS, DI), f32),
        "xs": v((ROWS, DI), bf16), "xso": v((ROWS, DI), bf16),
        "part": v((N, DI), f32), "factors": v((2, 8, DI), f32), "factor_sem": dma((2,)), "skipx": v((8, DI), f32),
        "state": v((N, DI), bf16), "dstate": v((N, DI), bf16),
        "y": v((ROWS, DI), f32), "z": v((ROWS, DI), f32), "gated": v((ROWS, DI), bf16), "act_own": v((ROWS, 768), bf16),
        "dz": v((ROWS, DI), bf16), "dy": v((ROWS, DI), bf16), "dyin": v((ROWS, DI), bf16),
        "ggain": v((8, DI), f32), "gskip": v((8, DI), f32),
        "dscores": v((ROWS, ROWS), f32), "dxs": v((ROWS, DI), f32), "sums": v((3, ROWS, 128), f32),
        "dpre": v((2, ROWS + HALO, TILE), f32), "late": v((8, CH), f32), "dx": v((HALO + ROWS, WIDE), bf16), "tail": v((8, CH), f32), "tail_in": v((8, CH), f32), "tail_sem": dma((2,)),
        "gconv": v((8, CH), f32), "gtok": v((ROWS, 768), bf16),
        "table": v((16, 8, 128), f32), "inbox": v((2, 16, 8, 128), f32), "table_sem": dma((2, 2, 16)),
        "part_a": v((2, 768, WIDE // 2), bf16), "part_z": v((768, DI), bf16), "part_out": v((DI, 768), bf16),
    }


def block_kernel(planes, names, *refs):
    r = Names(GIVEN + MADE + names, refs[: len(GIVEN) + len(MADE) + len(names)])
    extra = list(refs[len(GIVEN) + len(MADE) + len(names) :])
    chain_f, chain_b = extra[0:9], extra[9:15] + extra[6:8] + extra[15:16]
    red_a, red_b, red_z, red_out = extra[16:20], extra[20:24], extra[24:28], extra[28:32]
    x, y, z, c = place()
    me = chip(x, y, z)
    mate = (1 - c, me)
    f32 = jnp.float32
    r.wa[pl.ds(pl.multiple_of(me * 48, 16), 48), 0:CH] = r.w_in[:, DI : DI + CH]
    step_columns = r.w_in[:, DI + CH :]
    fill = jnp.zeros((48, WIDE - CH - H), step_columns.dtype)
    r.wa[pl.ds(pl.multiple_of(me * 48, 16), 48), CH:] = jnp.concatenate([step_columns, fill], axis=1)
    r.wz_full[pl.ds(pl.multiple_of(me * 48, 16), 48), :] = r.w_in[:, 0:DI]
    r.wout_full[pl.ds(pl.multiple_of(me * 96, 16), 96), :] = r.wout[...]
    r.given[me] = r.small_in[0:8, :]
    for m in range(2):
        r.numbers[m] = jnp.broadcast_to(r.seg_in[m : m + 1, :].astype(f32) + 1.0, (8, 128))

    @pl.when(z + c == 0)
    def _():
        r.tok[0:HALO, :] = jnp.zeros((HALO, 768), r.tok.dtype)
        r.seg[0] = jnp.full((8, 128), -1.0, f32)

    gather_a = Gather(r.wa, 48, "columns", r.wa_sem, planes)
    gather_z = Gather(r.wz_full, 48, "columns", r.wz_sem, planes)
    gather_out = Gather(r.wout_full, 96, "rows", r.wout_sem, planes)
    cots = Shuffle(r.cot, r.cot_own, r.cot_sem)
    moves = [
        Shuffle(r.tok_in, r.tok, r.tok_sem, HALO),
        Before(lambda m: r.tok_in.at[m, pl.ds(128 - HALO, HALO)], r.tok.at[pl.ds(0, HALO)], r.end_sem, planes),
        Shuffle(r.numbers, r.seg, r.seg_sem, 1),
        Before(lambda m: r.numbers.at[m], r.seg.at[0], r.segend_sem, planes),
        ToAll(r.given, r.given_sem, planes),
    ]
    meet_all(planes)
    gather_a.begin()
    for item in moves:
        item.start()
    gather_a.column(1)
    gather_a.sides(0)
    for item in moves:
        item.arrived()
    r.conv[...] = jnp.concatenate([r.given[k, :, 0:112] for k in range(16)], axis=1)
    r.gain[...] = jnp.concatenate([r.given[k, :, 0:96] for k in range(16)], axis=1)
    r.ngain[...] = jnp.concatenate([r.given[k, :, 0:48] for k in range(16)], axis=1)
    gather_a.column(2)
    gather_a.column(3)
    gather_z.begin_column()
    gather_out.begin_column()
    gather_a.sides(1)
    gather_a.diagonal(0)
    u = r.tok[...].astype(f32)
    r.normed[...] = low(u * lax.rsqrt(jnp.mean(u * u, axis=-1, keepdims=True) + EPSILON) * r.ngain[5:6, :])
    gather_a.sides(2)
    for gather in (gather_z, gather_out):
        gather.begin_sides()
    gather_a.diagonal(1)

    for k in range(3):
        r.segcol[128 * k : 128 * k + 128, :] = jnp.transpose(jnp.broadcast_to(r.seg[k, 0:1, :], (128, 128)))
    seg = r.segcol[128:384, :]
    for k in range(KC):
        r.same[k] = jnp.zeros((ROWS + HALO, 128), f32)
        r.same[k, 8 : 8 + ROWS, :] = jnp.where(r.segcol[125 + k : 125 + k + ROWS, :] == seg, 1.0, 0.0)
    gather_a.sides(3)
    gather_a.diagonal(2)
    for gather in (gather_z, gather_out):
        for d in range(1, planes):
            gather.column(d)
    cots.start()
    gather_a.diagonal(3)
    gather_a.whole_here()

    def sides(d):
        gather_z.sides(d)
        gather_out.sides(d)

    def diagonal(d):
        gather_z.diagonal(d)
        gather_out.diagonal(d)

    def project(k):
        at_k = pl.ds(pl.multiple_of(k * 512, 512), 512)
        r.proj[:, at_k] = dot(r.normed[...], r.wa[:, at_k])

    project(WIDE // 512 - 1)

    def convolve(j):
        at = at_tile(j)
        total = jnp.broadcast_to(r.conv[4:5, at], (ROWS, TILE))
        for k in range(KC):
            total = total + r.conv[k : k + 1, at] * r.proj[13 + k : 13 + k + ROWS, at] * r.same[k, 8 : 8 + ROWS, :]
        r.pre[:, at] = total
        return total * sigmoid(total)

    r.bproj[...] = low(convolve(TILES))
    r.cproj[...] = low(convolve(TILES + 1))

    raw = r.proj[HALO:, CH : CH + 128] + r.small_in[8:9, :]
    step = jnp.maximum(raw, 0.0) + jnp.log1p(jnp.exp(-jnp.abs(raw)))
    rate = -jnp.exp(r.small_in[9:10, :])
    lower = jnp.where(iota((ROWS, ROWS), 0) >= iota((ROWS, ROWS), 1), 1.0, 0.0)
    cum = jnp.dot(lower, step * rate, precision=HIGHEST, preferred_element_type=f32)
    r.step[...] = step
    r.cum[...] = cum
    across = jnp.transpose(cum)
    for h in range(H):
        r.cumt[h] = jnp.broadcast_to(across[h : h + 1, :], (8, ROWS))
    last = cum[ROWS - 1 : ROWS, :]
    before = r.segcol[127:128, :]
    first_seg, last_seg = seg[0:1, :], seg[ROWS - 1 : ROWS, :]
    r.ein[...] = jnp.where(seg == before, jnp.exp(cum), 0.0)
    r.eout[...] = jnp.where(seg == last_seg, jnp.exp(last - cum), 0.0)
    through = jnp.logical_and(first_seg == last_seg, first_seg == before)
    factor = jnp.where(through, jnp.exp(last), 0.0)
    segrow = jnp.concatenate([r.seg[1, 0:1, :], r.seg[2, 0:1, :]], axis=1)
    allowed = jnp.logical_and(jnp.concatenate([seg, seg], axis=1) == segrow, iota((ROWS, ROWS), 0) >= iota((ROWS, ROWS), 1))
    r.bar[...] = jnp.where(allowed, 0.0, -1e30)
    rows = packed(jnp.concatenate([jnp.broadcast_to(factor, (8, 128)), jnp.broadcast_to(r.small_in[10:11, :], (8, 128))], axis=0))
    both = dot(rows, spread_matrix(DI))
    r.factors[c] = both[0:8, :]
    r.skipx[...] = both[8:16, :]
    share = pltpu.make_async_remote_copy(
        src_ref=r.factors.at[c], dst_ref=r.factors.at[c], send_sem=r.factor_sem.at[0], recv_sem=r.factor_sem.at[1],
        device_id=mate, device_id_type=MESH,
    )
    share.start()
    spreads = [(r.stepx, packed(step)), (r.einx, packed(r.ein[...])), (r.eoutx, packed(r.eout[...])), (r.cumx, packed(cum))]
    r.stepx[...] = dot(spreads[0][1], spread_matrix(DI))
    r.eoutx[...] = dot(spreads[2][1], spread_matrix(DI))
    loop(0, WIDE // 512 - 1, project)

    def trade_order(k):
        return lax.rem(k + TILES // 2 * (1 - c), TILES)

    def outgoing(k):
        j = trade_order(k)
        at = at_tile(j)
        inner = convolve(j)
        r.inner[:, at] = inner
        scaled = r.stepx[:, at] * inner
        r.xs[:, at] = low(scaled)
        xso = low(scaled * r.eoutx[:, at])
        r.xso[:, at] = xso
        r.part[:, at] = dot(r.bproj[...], xso, TRANS)

    loop(0, TILES // 2, outgoing)
    forward = Chain(r.part, r.state, r.factors, chain_f, 0, planes)
    forward.start()
    loop(TILES // 2, TILES, outgoing)
    share.wait_recv()
    forward.merge()
    r.scores[...] = dot(r.cproj[...], r.bproj[...], TRANS_B)
    r.einx[...] = dot(spreads[1][1], spread_matrix(DI))
    r.cumx[...] = dot(spreads[3][1], spread_matrix(DI))
    sides(0)

    first_half = iota((1, TILE), 1) < P_SIZE

    def decays(j, band):
        size = 128 * (band + 1)
        rows = slice(128 * band, 128 * band + 128)
        tile = r.cumx[rows, at_tile(j)]
        turned = pltpu.roll(tile, P_SIZE, 1)
        out = []
        for k in range(2):
            column = jnp.where(first_half, tile, turned) if k == 0 else jnp.where(first_half, turned, tile)
            wide = column if band == 0 else jnp.concatenate([column, column], axis=1)
            out.append(jnp.exp(wide - r.cumt[2 * j + k, 0:1, 0:size] + r.bar[rows, 0:size]))
        return out

    def halves(tile):
        zero = jnp.zeros_like(tile)
        return jnp.where(first_half, tile, zero), jnp.where(first_half, zero, tile)

    def within(j):
        at = at_tile(j)
        for band in range(2):
            size = 128 * (band + 1)
            rows = slice(128 * band, 128 * band + 128)
            inside = halves(r.xs[0:size, at])
            total = 0.0
            for decay, xs in zip(decays(j, band), inside):
                total = total + dot(low(decay * r.scores[rows, 0:size]), xs)
            r.y[rows, at] = total

    def turn(chain, when):
        for k in range(planes):
            if when[k]:
                position = k if chain.lead == 0 else planes - 1 - k
                pl.when(z == position)(chain.pass_on)

    turn(forward, [1, 0, 0, 0])
    loop(0, 4, within)
    turn(forward, [0, 1, 0, 0])
    sides(1)
    diagonal(0)
    loop(4, 8, within)
    turn(forward, [0, 0, 1, 0])
    sides(2)
    diagonal(1)
    loop(8, 12, within)
    sides(3)
    turn(forward, [0, 0, 0, 1])
    diagonal(2)
    forward.close()

    def carried(j):
        at = at_tile(j)
        r.y[:, at] = r.y[:, at] + r.einx[:, at] * dot(r.cproj[...], r.state[:, at])

    loop(0, TILES, carried)
    diagonal(3)
    gather_z.whole_here()
    gather_out.whole_here()
    cots.arrived()

    def projections(j):
        at = pl.ds(pl.multiple_of(j * 512, 512), 512)
        r.z[:, at] = dot(r.normed[HALO:, :], r.wz_full[:, at])
        r.dxs[:, at] = dot(r.cot_own[...], r.wout_full[at, :], TRANS_B)

    loop(0, 3, projections)
    r.ggain[...] = jnp.zeros((8, DI), f32)
    r.gskip[...] = jnp.zeros((8, DI), f32)

    def gate(k):
        rows = at_rows(k, 16)
        inner, gate_in = r.inner[rows, :], r.z[rows, :]
        mixed = r.y[rows, :] + r.skipx[0:1, :] * inner
        sig = sigmoid(gate_in)
        silu = gate_in * sig
        v = mixed * silu
        scale = lax.rsqrt(jnp.mean(v * v, axis=-1, keepdims=True) + EPSILON)
        gain = r.gain[6:7, :]
        r.gated[rows, :] = low(v * scale * gain)
        dgated = r.dxs[rows, :]
        weighed = dgated * (v * scale)
        r.ggain[...] = r.ggain[...] + weighed[0:8, :] + weighed[8:16, :]
        a = gain * dgated
        dv = scale * (a - v * (scale * scale) * jnp.mean(v * a, axis=-1, keepdims=True))
        dmixed = dv * silu
        r.z[rows, :] = dmixed
        r.dy[rows, :] = low(dmixed)
        r.dyin[rows, :] = low(dmixed * r.einx[rows, :])
        r.dz[rows, :] = low(dv * mixed * (sig * (1.0 + gate_in * (1.0 - sig))))
        skip = dmixed * inner
        r.gskip[...] = r.gskip[...] + skip[0:8, :] + skip[8:16, :]

    loop(0, ROWS // 16, gate)

    def incoming(j):
        at = at_tile(j)
        r.part[:, at] = dot(r.cproj[...], r.dyin[:, at], TRANS)

    loop(0, TILES // 2, lambda k: incoming(trade_order(k)))
    backward = Chain(r.part, r.dstate, r.factors, chain_b, 1, planes)
    backward.start()
    loop(TILES // 2, TILES, lambda k: incoming(trade_order(k)))
    reduce_out = Reduce(r.part_out, r.grad_out, 96, "rows", red_out, planes)
    reduce_z = Reduce(r.part_z, r.grad_z, 48, "columns", red_z, planes)
    every = range(planes - 1, -1, -1)

    def weights_out(j):
        at = at_rows(j, 256)
        r.part_out[at, :] = low(dot(r.gated[:, at], r.cot_own[...], TRANS))

    loop(0, 2, weights_out)
    backward.merge()
    turn(backward, [1, 0, 0, 0])
    loop(2, 6, weights_out)
    for d in every:
        reduce_out.start(d)

    def weights_z(k):
        half = lax.rem(k // 3 + 1 + c, 2)
        at = pl.ds(pl.multiple_of(half * (DI // 2) + k % 3 * 256, 256), 256)
        r.part_z[:, at] = low(dot(r.normed[HALO:, :], r.dz[:, at], TRANS))

    loop(0, 3, weights_z)
    for d in every:
        reduce_z.start(d)
    loop(3, 6, weights_z)
    for d in every:
        reduce_out.fold(d)
    turn(backward, [0, 1, 0, 0])
    for d in every:
        reduce_z.fold(d)

    def project_out(k):
        at = at_rows(k, 256)
        r.act_own[:, at] = low(r.tok[HALO:, at].astype(f32) + dot(r.gated[...], r.wout_full[:, at]))

    loop(0, 3, project_out)
    acts = Shuffle(r.act_own, r.act_out, r.act_sem, back=True)
    acts.start()

    def reduce_sides(d):
        reduce_out.sides(d)
        reduce_z.sides(d)

    def reduce_column(d):
        reduce_out.column(d)
        reduce_z.column(d)

    r.dscores[...] = jnp.zeros((ROWS, ROWS), f32)
    r.sums[...] = jnp.zeros((3, ROWS, 128), f32)

    def within_back(j):
        at = at_tile(j)
        upper = lower = 0.0
        for band in range(2):
            size = 128 * (band + 1)
            rows = slice(128 * band, 128 * band + 128)
            xs = r.xs[0:size, at]
            grads = 0.0
            for decay, dy in zip(decays(j, band), halves(r.dy[rows, at])):
                weight = low(decay * r.scores[rows, 0:size])
                grads = grads + decay * dot(dy, xs, TRANS_B)
                upper = upper + dot(weight[:, 0:128], dy, TRANS)
                if band:
                    lower = lower + dot(weight[:, 128:256], dy, TRANS)
            r.dscores[rows, 0:size] = r.dscores[rows, 0:size] + grads
        r.dxs[0:128, at] = upper
        r.dxs[128:256, at] = lower
        gain = r.dy[:, at].astype(f32) * r.y[:, at] - r.xs[:, at].astype(f32) * r.dxs[:, at]
        r.sums[0] = r.sums[0] + head_sums(gain, j)

    loop(0, 2, within_back)
    turn(backward, [0, 0, 1, 0])
    reduce_sides(3)
    loop(2, 5, within_back)
    reduce_sides(2)
    reduce_column(3)
    loop(5, 8, within_back)
    reduce_sides(1)
    reduce_column(2)
    turn(backward, [0, 0, 0, 1])
    loop(8, 12, within_back)
    backward.close()
    reduce_sides(0)

    def last_sums(j):
        at = at_tile(j)
        xs = r.xs[:, at].astype(f32)
        far = r.eoutx[:, at] * dot(r.bproj[...], r.dstate[:, at])
        total = r.dxs[:, at] + far
        r.sums[1] = r.sums[1] + head_sums(xs * far, j)
        inner = r.inner[:, at]
        r.sums[2] = r.sums[2] + head_sums(inner * total, j)
        r.dxs[:, at] = r.skipx[0:1, at] * r.z[:, at] + r.stepx[:, at] * total

    def unconvolve(j, grad):
        at = at_tile(j)
        pre = r.pre[:, at]
        sig = sigmoid(pre)
        grad = grad * (sig * (1.0 + pre * (1.0 - sig)))
        slot = j % 2
        r.dpre[slot, 0:8, :] = jnp.zeros((8, TILE), f32)
        r.dpre[slot, 8 + ROWS :, :] = jnp.zeros((8, TILE), f32)
        r.dpre[slot, 8 : 8 + ROWS, :] = grad
        taps = [
            jnp.sum(grad * r.same[k, 8 : 8 + ROWS, :] * r.proj[13 + k : 13 + k + ROWS, at], axis=0, keepdims=True) for k in range(KC)
        ]
        taps += [jnp.sum(grad, axis=0, keepdims=True), jnp.zeros((3, TILE), f32)]
        r.gconv[:, at] = jnp.concatenate(taps, axis=0)
        total = 0.0
        for k in range(KC):
            rows = slice(3 - k, 3 - k + 8 + ROWS)
            total = total + r.conv[k : k + 1, at] * (r.same[k, rows, :] * r.dpre[slot, rows, :])
        r.tail[:, at] = total[0:8, :]
        r.dx[0:HALO, at] = low(jnp.concatenate([jnp.zeros((8, TILE), f32), total[0:8, :]], axis=0))
        r.dx[HALO:, at] = low(total[8:, :])
        r.late[:, at] = total[ROWS : ROWS + 8, :]

    reduce_first = Reduce(r.part_a.at[0], r.grad_a.at[0], 48, "columns", red_a, planes)
    reduce_second = Reduce(r.part_a.at[1], r.grad_a.at[1], 48, "columns", red_b, planes)

    def weights_a(group, k):
        half = lax.rem(k + 1 + c, 2)
        at = pl.ds(pl.multiple_of(half * (WIDE // 4), 512), 512)
        from_ = pl.ds(pl.multiple_of(group * (WIDE // 2) + half * (WIDE // 4), 512), 512)
        r.part_a[group, :, at] = low(dot(r.normed[...], r.dx[:, from_], TRANS))

    def columns_back(j):
        last_sums(j)
        unconvolve(j, r.dxs[:, at_tile(j)])

    r.dx[0:HALO, CH:] = jnp.zeros((HALO, WIDE - CH), jnp.bfloat16)
    r.dx[HALO:, CH + 128 :] = jnp.zeros((ROWS, WIDE - CH - 128), jnp.bfloat16)
    loop(0, 8, columns_back)
    weights_a(0, 0)
    for d in every:
        reduce_first.start(d)
    weights_a(0, 1)
    reduce_column(1)
    loop(8, 12, columns_back)
    for d in every:
        reduce_first.fold(d)
    dscores = low(r.dscores[...])
    dbproj = dot(dscores, r.cproj[...], TRANS) + dot(r.xso[...], r.dstate[...], TRANS_B)
    dcproj = dot(dscores, r.bproj[...]) + dot(r.dyin[...], r.state[...], TRANS_B)
    pick = jnp.where(iota((DI, 128), 0) // P_SIZE == iota((DI, 128), 1), 1.0, 0.0)
    crossing = jnp.sum(r.dstate[...].astype(f32) * r.state[...].astype(f32), axis=0, keepdims=True) * r.factors[c, 0:1, :]
    rows = jnp.concatenate([jnp.broadcast_to(crossing, (8, DI)), r.gskip[...]], axis=0)
    rows = jnp.dot(rows, pick, precision=HIGHEST, preferred_element_type=f32)
    at_end, gskip = rows[0:1, :], jnp.sum(rows[8:16, :], axis=0, keepdims=True)
    upper = jnp.where(iota((ROWS, ROWS), 0) <= iota((ROWS, ROWS), 1), 1.0, 0.0)
    strict = jnp.where(iota((ROWS, ROWS), 0) > iota((ROWS, ROWS), 1), 1.0, 0.0)
    dlog = (
        jnp.dot(upper, r.sums[0], precision=HIGHEST, preferred_element_type=f32)
        + jnp.dot(strict, r.sums[1], precision=HIGHEST, preferred_element_type=f32)
        + at_end
    )
    step = r.step[...]
    dstep = r.sums[2] + rate * dlog
    draw = dstep * sigmoid(r.proj[HALO:, CH : CH + 128] + r.small_in[8:9, :])
    lanes = iota((1, 128), 1) < H
    draw = jnp.where(lanes, draw, 0.0)
    gbias = jnp.sum(draw, axis=0, keepdims=True)
    glog = jnp.where(lanes, jnp.sum(step * dlog, axis=0, keepdims=True) * rate, 0.0)
    r.dx[HALO:, CH : CH + 128] = low(draw)
    unconvolve(TILES, dbproj)
    unconvolve(TILES + 1, dcproj)
    tails = [
        pltpu.make_async_remote_copy(
            src_ref=r.tail, dst_ref=r.tail_in, send_sem=r.tail_sem.at[0], recv_sem=r.tail_sem.at[1],
            device_id=(1 - c, chip(x, y, z - 1 + c)), device_id_type=MESH,
        )
    ]
    pl.when(z + c > 0)(tails[0].start)

    @pl.when(z + c == planes)
    def _():
        r.tail_in[...] = jnp.zeros((8, CH), f32)

    weights_a(1, 0)
    for d in every:
        reduce_second.start(d)
    weights_a(1, 1)
    reduce_first.sides(3)
    reduce_column(0)
    for d in every:
        reduce_second.fold(d)
    reduce_first.sides(2)
    reduce_out.close()
    reduce_z.close()
    pl.when(z + c < planes)(tails[0].wait_recv)
    r.dx[HALO + ROWS - 16 :, 0:CH] = low(
        jnp.concatenate([r.dx[HALO + ROWS - 16 : HALO + ROWS - 8, 0:CH].astype(f32), r.late[...] + r.tail_in[...]], axis=0)
    )

    def back_in(k):
        at = at_rows(k, 256)
        r.y[:, at] = dot(r.dz[...], r.wz_full[at, :], TRANS_B) + dot(r.dx[HALO:, :], r.wa[at, :], TRANS_B)

    loop(0, 3, back_in)
    reduce_first.sides(1)
    reduce_first.column(3)
    reduce_second.sides(3)
    r.ngrad[...] = jnp.zeros((8, 768), f32)

    def norm_back(k):
        rows = at_rows(k, 16)
        dnormed = r.y[rows, 0:768]
        u = r.tok[pl.ds(pl.multiple_of(HALO + 16 * k, 16), 16), :].astype(f32)
        scale = lax.rsqrt(jnp.mean(u * u, axis=-1, keepdims=True) + EPSILON)
        weighed = dnormed * u * scale
        r.ngrad[...] = r.ngrad[...] + weighed[0:8] + weighed[8:16]
        a = r.ngain[5:6, :] * dnormed
        grad = scale * (a - u * (scale * scale) * jnp.mean(u * a, axis=-1, keepdims=True))
        r.gtok[rows, :] = low(r.cot_own[rows, :].astype(f32) + grad)

    loop(0, 8, norm_back)
    reduce_first.sides(0)
    reduce_first.column(2)
    reduce_second.sides(2)
    reduce_second.column(3)
    loop(8, 16, norm_back)
    grads = Shuffle(r.gtok, r.tokens_out, r.back_sem, back=True)
    grads.start()
    reduce_first.column(1)
    reduce_second.sides(1)
    reduce_second.column(2)
    ngain = jnp.sum(r.ngrad[...], axis=0, keepdims=True)
    ggain = jnp.sum(r.ggain[...], axis=0, keepdims=True)
    lane_heads = jnp.concatenate([gbias[:, 0:H], glog[:, 0:H], gskip[:, 0:H], jnp.zeros((1, 128 - 3 * H), f32)], axis=1)
    for k in range(16):
        convs = jnp.concatenate([r.gconv[0:5, 112 * k : 112 * k + 112], jnp.zeros((5, 16), f32)], axis=1)
        first = jnp.concatenate([ngain[:, 48 * k : 48 * k + 48], jnp.zeros((1, 80), f32)], axis=1)
        second = jnp.concatenate([ggain[:, 96 * k : 96 * k + 96], jnp.zeros((1, 32), f32)], axis=1)
        r.table[k] = jnp.concatenate([convs, first, second, lane_heads], axis=0)

    def to_all(k, act):
        other = lax.rem(me + k, 16)
        for far in range(2):
            copy = pltpu.make_async_remote_copy(
                src_ref=r.table.at[other], dst_ref=r.inbox.at[c, me], send_sem=r.table_sem.at[0, far, other],
                recv_sem=r.table_sem.at[1, c, me], device_id=(far, other), device_id_type=MESH,
            )
            pl.when(jnp.logical_or(k > 0, far != c))(functools.partial(act, copy))

    def from_all(k):
        other = lax.rem(me + k, 16)
        for far in range(2):
            copy = pltpu.make_async_remote_copy(
                src_ref=r.table.at[other], dst_ref=r.inbox.at[far, other], send_sem=r.table_sem.at[0, far, other],
                recv_sem=r.table_sem.at[1, far, other], device_id=(far, other), device_id_type=MESH,
            )
            pl.when(jnp.logical_or(k > 0, far != c))(copy.wait_recv)

    loop(0, 16, lambda k: to_all(k, lambda copy: copy.start()))
    r.inbox[c, me] = r.table[me]
    reduce_second.sides(0)
    reduce_first.column(0)
    reduce_second.column(1)
    reduce_first.close()
    reduce_second.column(0)
    reduce_second.close()
    loop(0, 16, from_all)
    r.small_out[...] = jnp.sum(jnp.sum(r.inbox[...], axis=0), axis=0)
    loop(0, 16, lambda k: to_all(k, lambda copy: copy.wait_send()))
    for item in moves + [gather_a, gather_z, gather_out, reduce_out, reduce_z, reduce_first, reduce_second, forward, backward, cots, acts, grads]:
        item.finish()
    acts.arrived()
    grads.arrived()
    share.wait_send()
    pl.when(z + c > 0)(tails[0].wait_send)


def block(given, planes):
    f32, bf16 = jnp.float32, jnp.bfloat16
    shape = jax.ShapeDtypeStruct
    named = block_scratch(planes)
    extra = Chain.scratch() + Chain.scratch()[:6] + Chain.scratch()[8:]
    extra += Reduce.scratch(48, WIDE // 2, "columns", planes) + Reduce.scratch(48, WIDE // 2, "columns", planes) + Reduce.scratch(48, DI, "columns", planes)
    extra += Reduce.scratch(96, 768, "rows", planes)
    return pl.pallas_call(
        functools.partial(block_kernel, planes, list(named)),
        out_shape=[
            shape((2, 128, 768), bf16), shape((2, 128, 768), bf16), shape((2, 48, WIDE // 2), f32),
            shape((48, DI), f32), shape((96, 768), f32), shape((8, 128), f32),
        ],
        in_specs=[VMEM] * len(GIVEN),
        out_specs=[VMEM] * len(MADE),
        scratch_shapes=list(named.values()) + extra,
        compiler_params=pltpu.CompilerParams(collective_id=0, has_side_effects=True, vmem_limit_bytes=62 << 20),
    )(*given)


def deliver_kernel(acts, tokens, grad_a, grad_z, grad_out, sums, *out):
    out[0][...] = acts[...]
    out[1][...] = tokens[...]
    out[2][...] = sums[5:6, 0:48]
    out[3][:, 0:DI] = grad_z[...]
    out[3][:, DI : DI + WIDE // 2] = grad_a[0]
    out[3][:, DI + WIDE // 2 :] = grad_a[1, :, 0 : CH + H - WIDE // 2]
    out[4][...] = sums[0:4, 0:112]
    out[5][...] = sums[4:5, 0:112]
    out[6][...] = sums[7:8, 0:H]
    out[7][...] = sums[7:8, H : 2 * H]
    out[8][...] = sums[7:8, 2 * H : 3 * H]
    out[9][...] = sums[6:7, 0:96]
    out[10][...] = grad_out[...]


def deliver(made):
    f32, bf16 = jnp.float32, jnp.bfloat16
    shapes = [
        ((2, 128, 768), bf16), ((2, 128, 768), bf16), ((1, 48), f32), ((48, DI + CH + H), f32), ((4, 112), f32), ((1, 112), f32),
        ((1, H), f32), ((1, H), f32), ((1, H), f32), ((1, 96), f32), ((96, 768), f32),
    ]
    return pl.pallas_call(
        deliver_kernel,
        out_shape=[jax.ShapeDtypeStruct(*s) for s in shapes],
        in_specs=[VMEM] * len(made),
        out_specs=[VMEM] * len(shapes),
    )(*made)


def fast_body(
    planes, tokens, cotangent, segments, norm_gain, w_in, conv_weight, conv_bias, step_bias, log_rate, skip_gain, gate_gain, w_out
):
    def at_row(row, values):
        values = values.astype(jnp.float32).reshape(-1, values.shape[-1])
        return jnp.pad(values, ((row, 16 - row - values.shape[0]), (0, 128 - values.shape[1])))

    rows = ((0, conv_weight), (4, conv_bias), (5, norm_gain), (6, gate_gain), (8, step_bias), (9, log_rate), (10, skip_gain))
    small = sum(at_row(row, values) for row, values in rows)
    made = block((tokens[:, 0], cotangent[:, 0], segments[:, 0], small, w_in, w_out), planes)
    out = deliver(made)
    return (
        out[0][:, None], out[1][:, None], out[2][0], out[3], out[4], out[5][0], out[6][0], out[7][0], out[8][0], out[9][0], out[10],
    )


def solution(mesh):
    in_specs = (
        P(None, "dp", "seq", None),
        P(None, "dp", "seq", None),
        P(None, "dp", "seq"),
        P("seq"),
        P("seq", None),
        P(None, "seq"),
        P("seq"),
        P(),
        P(),
        P(),
        P("seq"),
        P("seq", None),
    )
    out_specs = (
        P(None, "dp", "seq", None),
        P(None, "dp", "seq", None),
        P("seq"),
        P("seq", None),
        P(None, "seq"),
        P("seq"),
        P(),
        P(),
        P(),
        P("seq"),
        P("seq", None),
    )
    work = partial(fast_body, mesh.shape["seq"] // 4) if mesh.shape["seq"] == 16 else body
    return jax.shard_map(work, mesh=mesh, in_specs=in_specs, out_specs=out_specs, check_vma=False)
```

```python
import functools
from functools import partial

import jax
import jax.numpy as jnp
from jax import lax
from jax.experimental import pallas as pl
from jax.experimental.pallas import tpu as pltpu
from jax.sharding import PartitionSpec as P

DI = 1536
H = 24
P_SIZE = 64
N = 128
KC = 4
CH = 1792


EPSILON = 1e-05
HIGHEST = lax.Precision.HIGHEST


def passed_along(array, axis, by):
    devices = lax.axis_size(axis)
    pairs = [(i, i + by) for i in range(devices) if 0 <= i + by < devices]
    return lax.ppermute(array, axis, pairs)


def prefix(array, axis, combine, identity, reverse):
    devices, place = (lax.axis_size(axis), lax.axis_index(axis))
    everything = jax.tree.map(lambda part: lax.all_gather(part, axis), array)
    start = jax.tree.map(
        lambda part, zero: jnp.broadcast_to(jnp.asarray(zero, part.dtype), part.shape),
        array,
        identity,
    )

    def lap(k, before):
        at = devices - 1 - k if reverse else k
        reached = at > place if reverse else at < place
        new = combine(before, jax.tree.map(lambda part: part[at], everything))
        return jax.tree.map(lambda a, b: jnp.where(reached, a, b), new, before)

    return lax.fori_loop(0, devices, lap, start)


def for_sending(array):
    return jax.tree.map(lambda a: a.astype(jnp.bfloat16) if a.dtype == jnp.float32 else a, array)


def rms_scale(values, gain_vec):
    return (
        values * lax.rsqrt(jnp.mean(values * values, axis=-1, keepdims=True) + EPSILON) * gain_vec
    )


def causal_conv(padded, seg_pad, seg_one, kernel, offset):
    length_t = seg_one.shape[0]
    total = jnp.zeros((length_t, padded.shape[1]), jnp.float32) + offset[None, :]
    for tap_index in range(KC):
        window = padded[tap_index : tap_index + length_t]
        same_doc = (seg_pad[tap_index : tap_index + length_t] == seg_one).astype(jnp.float32)
        total = total + kernel[tap_index][None, :] * window * same_doc[:, None]
    return total


def cumulative(step_size, rate):
    length_t = step_size.shape[0]
    lower = jnp.tril(jnp.ones((length_t, length_t), jnp.float32))
    return jnp.dot(lower, step_size * rate[None, :], precision=HIGHEST)


def block_state(inner, b_proj, step_size, rate, seg_one, previous):
    cum_decay = cumulative(step_size, rate)
    last_seg = seg_one[-1]
    to_end = (
        jnp.where((seg_one == last_seg)[:, None], jnp.exp(cum_decay[-1][None, :] - cum_decay), 0.0)
        * step_size
    )
    state_part = jnp.einsum("uhp,un->hpn", inner * to_end[:, :, None], b_proj, precision=HIGHEST)
    through = jnp.logical_and(seg_one[0] == last_seg, seg_one[0] == previous).astype(jnp.float32)
    return (state_part, jnp.exp(cum_decay[-1]) * through)


def block_output(inner, b_proj, c_proj, step_size, rate, state_in, seg_one, previous):
    cum_decay = cumulative(step_size, rate)
    length_t = seg_one.shape[0]
    row_index = lax.broadcasted_iota(jnp.int32, (length_t, length_t), 0)
    col_index = lax.broadcasted_iota(jnp.int32, (length_t, length_t), 1)
    allowed = jnp.logical_and(row_index >= col_index, seg_one[:, None] == seg_one[None, :])[
        :, :, None
    ]
    spread = cum_decay[:, None, :] - cum_decay[None, :, :]
    decays = jnp.where(allowed, jnp.exp(jnp.where(allowed, spread, 0.0)), 0.0)
    scores = jnp.dot(c_proj, b_proj.T, precision=HIGHEST)
    weights = decays * scores[:, :, None] * step_size[None, :, :]
    local_part = jnp.einsum("tuh,uhp->thp", weights, inner, precision=HIGHEST)
    carried = (seg_one == previous).astype(jnp.float32)[:, None] * jnp.exp(cum_decay)
    return local_part + carried[:, :, None] * jnp.einsum(
        "tn,hpn->thp", c_proj, state_in, precision=HIGHEST
    )


def prepare(proj_out, tail_rows, kernel, offset, step_bias, log_rate, tail_seg, seg_one):
    length_t = proj_out.shape[0]
    padded = jnp.concatenate([tail_rows, proj_out[:, DI : DI + CH]], axis=0)
    seg_pad = jnp.concatenate([tail_seg, seg_one])
    activated = jax.nn.silu(causal_conv(padded, seg_pad, seg_one, kernel, offset))
    inner = activated[:, :DI].reshape(length_t, H, P_SIZE)
    b_proj = activated[:, DI : DI + N]
    c_proj = activated[:, DI + N :]
    step_size = jax.nn.softplus(proj_out[:, DI + CH :] + step_bias[None, :])
    rate = -jnp.exp(log_rate)
    return (inner, b_proj, c_proj, step_size, rate, proj_out[:, :DI])


def finish(
    inner,
    b_proj,
    c_proj,
    step_size,
    rate,
    gate_in,
    state_in,
    skip_gain,
    gate_gain,
    seg_one,
    previous,
):
    length_t = inner.shape[0]
    mixed = block_output(inner, b_proj, c_proj, step_size, rate, state_in, seg_one, previous)
    mixed = mixed + skip_gain[None, :, None] * inner
    gated = mixed.reshape(length_t, DI) * jax.nn.silu(gate_in)
    return rms_scale(gated, gate_gain)


def chain_link(earlier, later):
    return (earlier[0] * later[0], later[0][:, None, None] * earlier[1] + later[1])


def body(
    tokens,
    cotangent,
    segments,
    norm_gain,
    w_in,
    conv_weight,
    conv_bias,
    step_bias,
    log_rate,
    skip_gain,
    gate_gain,
    w_out,
):
    batches = tokens.shape[0]
    length_t = tokens.shape[2]
    halo_rows = KC - 1
    identity = (jnp.ones((H,), jnp.float32), jnp.zeros((H, P_SIZE, N), jnp.float32))
    totals = None
    head_totals = (
        jnp.zeros((H,), jnp.float32),
        jnp.zeros((H,), jnp.float32),
        jnp.zeros((H,), jnp.float32),
    )
    act_list = []
    grad_list = []
    for micro in range(batches):
        gathered = (
            lax.all_gather(w_in, "seq", axis=0, tiled=True),
            lax.all_gather(w_out, "seq", axis=0, tiled=True),
            lax.all_gather(conv_weight, "seq", axis=1, tiled=True),
            lax.all_gather(conv_bias, "seq", axis=0, tiled=True),
            lax.all_gather(norm_gain, "seq", axis=0, tiled=True),
            lax.all_gather(gate_gain, "seq", axis=0, tiled=True),
        )
        in_full = gathered[0]
        out_full = gathered[1]
        kernel = gathered[2].astype(jnp.float32)
        offset = gathered[3].astype(jnp.float32)
        gain_one = gathered[4].astype(jnp.float32)
        gain_two = gathered[5].astype(jnp.float32)
        resid = tokens[micro, 0].astype(jnp.float32)
        seg_one = segments[micro, 0].astype(jnp.float32) + 1.0
        normed, norm_back = jax.vjp(rms_scale, resid, gain_one)
        normed_low = normed.astype(jnp.bfloat16)
        proj_out = jnp.dot(normed_low, in_full, preferred_element_type=jnp.float32)
        tail_rows, tail_seg = passed_along(
            (proj_out[length_t - halo_rows :, DI : DI + CH], seg_one[length_t - halo_rows :]),
            "seq",
            1,
        )
        previous = tail_seg[halo_rows - 1]
        prepared, prep_back = jax.vjp(
            partial(prepare, tail_seg=tail_seg, seg_one=seg_one),
            proj_out,
            tail_rows,
            kernel,
            offset,
            step_bias,
            log_rate,
        )
        inner, b_proj, c_proj, step_size, rate, gate_in = prepared
        state_out, state_back = jax.vjp(
            partial(block_state, seg_one=seg_one, previous=previous), inner, b_proj, step_size, rate
        )
        state_part, through = state_out
        state_in = prefix((through, state_part), "seq", chain_link, identity, False)[1]
        normed_two, finish_back = jax.vjp(
            partial(finish, seg_one=seg_one, previous=previous),
            inner,
            b_proj,
            c_proj,
            step_size,
            rate,
            gate_in,
            state_in,
            skip_gain,
            gain_two,
        )
        gate_low = normed_two.astype(jnp.bfloat16)
        branch = jnp.dot(gate_low, out_full, preferred_element_type=jnp.float32)
        act_list.append((resid + branch).astype(jnp.bfloat16))
        cot_low = cotangent[micro, 0]
        again = (
            lax.all_gather(w_in, "seq", axis=0, tiled=True),
            lax.all_gather(w_out, "seq", axis=0, tiled=True),
        )
        in_back = again[0]
        out_back = again[1]
        out_term = lax.dot_general(
            gate_low, cot_low, (((0,), (0,)), ((), ())), preferred_element_type=jnp.float32
        )
        grad_gate = lax.dot_general(
            cot_low, out_back, (((1,), (1,)), ((), ())), preferred_element_type=jnp.float32
        )
        g_inner, g_bproj, g_cproj, g_step, g_rate, g_gate_in, g_state_in, g_skip, g_gain_two = (
            finish_back(grad_gate)
        )
        carried = prefix((through, g_state_in), "seq", chain_link, identity, True)[1]
        h_inner, h_bproj, h_step, h_rate = state_back(
            (carried, jnp.sum(carried * state_in, axis=(1, 2)))
        )
        g_proj, g_tail, g_kernel, g_offset, g_bias, g_log = prep_back(
            (
                g_inner + h_inner,
                g_bproj + h_bproj,
                g_cproj,
                g_step + h_step,
                g_rate + h_rate,
                g_gate_in,
            )
        )
        returned = passed_along(g_tail, "seq", -1)
        width_after = proj_out.shape[1] - DI - CH
        g_proj = g_proj + jnp.pad(returned, ((length_t - halo_rows, 0), (DI, width_after)))
        proj_grad_low = g_proj.astype(jnp.bfloat16)
        grad_normed = lax.dot_general(
            proj_grad_low, in_back, (((1,), (1,)), ((), ())), preferred_element_type=jnp.float32
        )
        grad_resid, g_gain_one = norm_back(grad_normed)
        grad_list.append((cot_low.astype(jnp.float32) + grad_resid).astype(jnp.bfloat16))
        in_shard = lax.psum_scatter(
            lax.dot_general(
                normed_low,
                proj_grad_low,
                (((0,), (0,)), ((), ())),
                preferred_element_type=jnp.float32,
            ),
            "seq",
            scatter_dimension=0,
            tiled=True,
        )
        shards = (
            lax.psum_scatter(out_term, "seq", scatter_dimension=0, tiled=True),
            lax.psum_scatter(g_kernel, "seq", scatter_dimension=1, tiled=True),
            lax.psum_scatter(g_offset, "seq", scatter_dimension=0, tiled=True),
            lax.psum_scatter(g_gain_one, "seq", scatter_dimension=0, tiled=True),
            lax.psum_scatter(g_gain_two, "seq", scatter_dimension=0, tiled=True),
        )
        this_round = (in_shard, shards[0], shards[1], shards[2], shards[3], shards[4])
        if totals is None:
            totals = this_round
        else:
            totals = tuple((prior + fresh for prior, fresh in zip(totals, this_round)))
        head_totals = (head_totals[0] + g_bias, head_totals[1] + g_log, head_totals[2] + g_skip)
    summed = jax.tree.map(
        lambda part: part.astype(jnp.float32), lax.psum(for_sending(totals), "dp")
    )
    heads = lax.psum((head_totals[0], head_totals[1], head_totals[2]), ("dp", "seq"))
    activations = jnp.stack(act_list)[:, None]
    grad_tokens = jnp.stack(grad_list)[:, None]
    return (
        activations,
        grad_tokens,
        summed[4],
        summed[0],
        summed[2],
        summed[3],
        heads[0],
        heads[1],
        heads[2],
        summed[5],
        summed[1],
    )


MESH = pl.DeviceIdType.MESH


def chip(x, y, z):
    return z * 4 + y * 2 + x


def place():
    core = lax.axis_index("dp")
    at = lax.axis_index("seq")
    return at % 2, (at // 2) % 2, at // 4, core


def greet_all(planes):
    barrier = pltpu.get_barrier_semaphore()
    me = lax.axis_index("seq")
    core = lax.axis_index("dp")
    count = planes * 4

    def greet(k, carry):
        other = lax.rem(me + k, count)
        for far in range(2):

            @pl.when(jnp.logical_or(k > 0, far != core))
            def _():
                pl.semaphore_signal(barrier, inc=1, device_id=(far, other), device_id_type=MESH)

        return carry

    lax.fori_loop(0, count, greet, 0)


def meet_all(planes):
    pl.semaphore_wait(pltpu.get_barrier_semaphore(), 8 * planes - 1)


COLUMN, SIDE_X, SIDE_Y, HALF_X, HALF_Y, MATE_Z, MATE_X, MATE_Y, MATE_HX, MATE_HY = range(10)


class Gather:
    def __init__(self, whole, rows, quarter, sems, planes):
        self.whole, self.rows, self.quarter, self.sems, self.planes = whole, rows, quarter, sems, planes
        self.x, self.y, self.z, self.core = place()

    def region(self, block, core, part=None):
        width = self.whole.shape[1] // 2
        start = pl.multiple_of(block * self.rows, 16)
        left = pl.multiple_of(core * width, 128)
        if part is None:
            return self.whole.at[pl.ds(start, self.rows), pl.ds(left, width)]
        if self.quarter == "rows":
            half = self.rows // 2
            return self.whole.at[pl.ds(pl.multiple_of(start + part * half, 16), half), pl.ds(left, width)]
        half = width // 2
        return self.whole.at[pl.ds(start, self.rows), pl.ds(pl.multiple_of(left + part * half, 128), half)]

    def copy(self, kind, leaves, lands, block, core, part, device):
        region = self.region(block, core, part)
        return pltpu.make_async_remote_copy(
            src_ref=region,
            dst_ref=region,
            send_sem=self.sems.at[0, kind, leaves],
            recv_sem=self.sems.at[1, kind, lands],
            device_id=device,
            device_id_type=MESH,
        )

    def out(self, kind, far):
        x, y, z, c = self.x, self.y, self.z, self.core
        if kind == COLUMN:
            return self.copy(kind, far, z, chip(x, y, z), c, None, (c, chip(x, y, far)))
        own, by_x, by_y, across = chip(x, y, far), chip(1 - x, y, far), chip(x, 1 - y, far), chip(1 - x, 1 - y, far)
        mate = (1 - c, chip(x, y, z))
        to_x, to_y = (c, chip(1 - x, y, z)), (c, chip(x, 1 - y, z))
        block, part, device = {
            SIDE_X: (own, None, to_x),
            SIDE_Y: (own, None, to_y),
            HALF_X: (by_y, 1, to_x),
            HALF_Y: (by_x, 0, to_y),
            MATE_Z: (own, None, mate),
            MATE_X: (by_x, None, mate),
            MATE_Y: (by_y, None, mate),
            MATE_HX: (across, 1, mate),
            MATE_HY: (across, 0, mate),
        }[kind]
        return self.copy(kind, far, far, block, c, part, device)

    def send(self, kind, far):
        self.out(kind, far).start()

    def arrived(self, kind, far):
        x, y = self.x, self.y
        own, by_x, by_y, across = chip(x, y, far), chip(1 - x, y, far), chip(x, 1 - y, far), chip(1 - x, 1 - y, far)
        block, part, mine = {
            COLUMN: (own, None, True),
            SIDE_X: (by_x, None, True),
            SIDE_Y: (by_y, None, True),
            HALF_X: (across, 1, True),
            HALF_Y: (across, 0, True),
            MATE_Z: (own, None, False),
            MATE_X: (by_x, None, False),
            MATE_Y: (by_y, None, False),
            MATE_HX: (across, 1, False),
            MATE_HY: (across, 0, False),
        }[kind]
        core = self.core if mine else 1 - self.core
        self.copy(kind, far, far, block, core, part, (1 - self.core, chip(x, y, self.z))).wait_recv()

    def each(self, distance, act):
        for sign in (-1, 1) if distance else (1,):
            far = self.z + sign * distance
            if distance:
                pl.when(jnp.logical_and(far >= 0, far < self.planes))(functools.partial(act, far))
            else:
                act(far)

    def begin_sides(self):
        self.send(SIDE_X, self.z)
        self.send(SIDE_Y, self.z)

    def begin_column(self):
        for distance in range(1, self.planes):
            self.each(distance, lambda far: self.send(COLUMN, far))

    def begin(self):
        self.begin_sides()
        self.begin_column()

    def column(self, distance):
        def act(far):
            self.arrived(COLUMN, far)
            self.send(SIDE_X, far)
            self.send(SIDE_Y, far)
            self.send(MATE_Z, far)

        self.each(distance, act)

    def sides(self, distance):
        def act(far):
            self.arrived(SIDE_X, far)
            self.send(HALF_Y, far)
            self.send(MATE_X, far)
            self.arrived(SIDE_Y, far)
            self.send(HALF_X, far)
            self.send(MATE_Y, far)

        self.each(distance, act)

    def diagonal(self, distance):
        def act(far):
            self.arrived(HALF_Y, far)
            self.send(MATE_HY, far)
            self.arrived(HALF_X, far)
            self.send(MATE_HX, far)

        self.each(distance, act)

    def whole_here(self):
        for distance in range(self.planes):

            def act(far):
                for kind in (MATE_X, MATE_Y, MATE_HX, MATE_HY) + ((MATE_Z,) if distance else ()):
                    self.arrived(kind, far)

            self.each(distance, act)

    def finish(self):
        for distance in range(self.planes):

            def act(far):
                kinds = (SIDE_X, SIDE_Y, HALF_X, HALF_Y, MATE_X, MATE_Y, MATE_HX, MATE_HY)
                for kind in kinds + ((MATE_Z, COLUMN) if distance else ()):
                    self.out(kind, far).wait_send()

            self.each(distance, act)


def gather_sems(planes):
    return pltpu.SemaphoreType.DMA((2, 10, planes))


class Reduce:
    X, Y, HX, HY, COLUMN, MATE, LAST = range(7)

    @staticmethod
    def scratch(rows, width, quarter, planes):
        half = width // 2
        corner = (rows // 2, half) if quarter == "rows" else (rows, half // 2)
        bf16 = jnp.bfloat16
        return [
            pltpu.VMEM((4 * planes * rows, half), bf16),
            pltpu.VMEM((3, planes, rows, half), bf16),
            pltpu.VMEM((2, planes) + corner, bf16),
            pltpu.SemaphoreType.DMA((2, 7, planes)),
        ]

    def __init__(self, part, out, rows, quarter, scratch, planes):
        self.part, self.out, self.rows, self.quarter, self.planes = part, out, rows, quarter, planes
        self.mate_in, self.side_in, self.corner_in, self.sems = scratch
        self.x, self.y, self.z, self.core = place()
        self.half = part.shape[1] // 2

    def block(self, owner, part=None):
        start = pl.multiple_of(owner * self.rows, 16)
        left = pl.multiple_of(self.core * self.half, 128)
        if part is None:
            return pl.ds(start, self.rows), pl.ds(left, self.half)
        if self.quarter == "rows":
            return pl.ds(pl.multiple_of(start + part * (self.rows // 2), 16), self.rows // 2), pl.ds(left, self.half)
        quarter = self.half // 2
        return pl.ds(start, self.rows), pl.ds(pl.multiple_of(left + part * quarter, 128), quarter)

    def copy(self, kind, far, source, target, device):
        return pltpu.make_async_remote_copy(
            src_ref=source,
            dst_ref=target,
            send_sem=self.sems.at[0, kind, far],
            recv_sem=self.sems.at[1, kind, far],
            device_id=device,
            device_id_type=MESH,
        )

    def move(self, kind, far):
        x, y, z, c = self.x, self.y, self.z, self.core
        part = self.part
        to_x, to_y, mate = (c, chip(1 - x, y, z)), (c, chip(x, 1 - y, z)), (1 - c, chip(x, y, z))
        if kind == self.X:
            return self.copy(kind, far, part.at[self.block(chip(1 - x, y, far))], self.side_in.at[0, far], to_x)
        if kind == self.Y:
            return self.copy(kind, far, part.at[self.block(chip(x, 1 - y, far))], self.side_in.at[1, far], to_y)
        if kind == self.HX:
            return self.copy(kind, far, part.at[self.block(chip(1 - x, 1 - y, far), 0)], self.corner_in.at[0, far], to_x)
        if kind == self.HY:
            return self.copy(kind, far, part.at[self.block(chip(1 - x, 1 - y, far), 1)], self.corner_in.at[1, far], to_y)
        if kind == self.COLUMN:
            return pltpu.make_async_remote_copy(
                src_ref=part.at[self.block(chip(x, y, far))],
                dst_ref=self.side_in.at[2, z],
                send_sem=self.sems.at[0, kind, far],
                recv_sem=self.sems.at[1, kind, z],
                device_id=(c, chip(x, y, far)),
                device_id_type=MESH,
            )
        if kind == self.MATE:
            rows = pl.ds(pl.multiple_of(far * 4 * self.rows, 16), 4 * self.rows)
            left = pl.multiple_of((1 - c) * self.half, 128)
            return self.copy(kind, far, part.at[rows, pl.ds(left, self.half)], self.mate_in.at[rows], mate)
        left = pl.multiple_of(c * self.half, 128)
        region = self.out.at[:, pl.ds(left, self.half)]
        return self.copy(kind, 0, region, region, mate)

    def add(self, at, *refs):
        total = self.part[at].astype(jnp.float32)
        for ref in refs:
            total = total + ref[...].astype(jnp.float32)
        self.part[at] = low(total)

    def each(self, distance, act):
        for sign in (-1, 1) if distance else (1,):
            far = self.z + sign * distance
            if distance:
                pl.when(jnp.logical_and(far >= 0, far < self.planes))(functools.partial(act, far, sign))
            else:
                act(far, sign)

    def start(self, distance):
        self.each(distance, lambda far, sign: self.move(self.MATE, far).start())

    def fold(self, distance):
        def act(far, sign):
            self.move(self.MATE, far).wait_recv()

            def rows(k, carry):
                start = pl.multiple_of((far * 4 + k) * self.rows, 16)
                left = pl.multiple_of(self.core * self.half, 128)
                self.add((pl.ds(start, self.rows), pl.ds(left, self.half)), self.mate_in.at[pl.ds(start, self.rows)])
                return carry

            lax.fori_loop(0, 4, rows, 0)
            self.move(self.HX, far).start()
            self.move(self.HY, far).start()

        self.each(distance, act)

    def sides(self, distance):
        x, y = self.x, self.y

        def act(far, sign):
            self.move(self.HX, far).wait_recv()
            self.add(self.block(chip(x, 1 - y, far), 0), self.corner_in.at[0, far])
            self.move(self.Y, far).start()
            self.move(self.HY, far).wait_recv()
            self.add(self.block(chip(1 - x, y, far), 1), self.corner_in.at[1, far])
            self.move(self.X, far).start()

        self.each(distance, act)

    def column(self, distance):
        x, y, z = self.x, self.y, self.z

        def act(far, sign):
            self.move(self.X, far).wait_recv()
            self.move(self.Y, far).wait_recv()
            if distance:
                self.add(self.block(chip(x, y, far)), self.side_in.at[0, far], self.side_in.at[1, far])
                self.move(self.COLUMN, far).start()

        self.each(distance, act)

    def close(self):
        z = self.z
        at = self.block(chip(self.x, self.y, z))
        left = pl.multiple_of(self.core * self.half, 128)
        here = (slice(None), pl.ds(left, self.half))
        total = self.part[at].astype(jnp.float32)
        self.out[here] = total + self.side_in[0, z].astype(jnp.float32) + self.side_in[1, z].astype(jnp.float32)
        for distance in range(self.planes - 1, 0, -1):

            def act(far, sign):
                self.copy(self.COLUMN, far, self.side_in.at[2, far], self.side_in.at[2, far], (self.core, chip(self.x, self.y, far))).wait_recv()
                self.out[here] = self.out[here] + self.side_in[2, far].astype(jnp.float32)

            self.each(distance, act)
        self.move(self.LAST, 0).start()

    def finish(self):
        last = self.move(self.LAST, 0)
        left = pl.multiple_of((1 - self.core) * self.half, 128)
        region = self.out.at[:, pl.ds(left, self.half)]
        self.copy(self.LAST, 0, region, region, (1 - self.core, chip(self.x, self.y, self.z))).wait_recv()
        last.wait_send()

    def drain(self, kinds):
        for distance in range(self.planes):

            def act(far, sign):
                for kind in kinds:
                    if distance or kind != self.COLUMN:
                        self.move(kind, far).wait_send()

            self.each(distance, act)

    def drain_early(self):
        self.drain((self.MATE, self.HX, self.HY))

    def drain_late(self):
        self.drain((self.X, self.Y, self.COLUMN))


class Chain:
    CUT = 6

    @staticmethod
    def scratch():
        half = pltpu.VMEM((N, DI // 2), jnp.bfloat16)
        wide = pltpu.VMEM((N, DI // 2), jnp.float32)
        return [half, half, half, half, half, half, wide, wide, pltpu.SemaphoreType.DMA((2, 2 + Chain.CUT))]

    def __init__(self, part, result, factors, scratch, lead, planes):
        self.part, self.result, self.factors, self.lead, self.planes = part, result, factors, lead, planes
        self.give, self.take, self.leave, self.come, self.back, self.again, self.total, self.front, self.sems = scratch
        self.x, self.y, self.z, self.core = place()
        self.half = DI // 2
        self.leads = self.core == lead
        self.ahead = 1 if lead == 0 else -1
        self.first = self.z == (0 if lead == 0 else planes - 1)
        self.last = self.z == (planes - 1 if lead == 0 else 0)

    def own(self):
        return pl.ds(pl.multiple_of(self.core * self.half, 128), self.half)

    def other(self):
        return pl.ds(pl.multiple_of((1 - self.core) * self.half, 128), self.half)

    def copy(self, k, source, target, device):
        return pltpu.make_async_remote_copy(
            src_ref=source,
            dst_ref=target,
            send_sem=self.sems.at[0, k],
            recv_sem=self.sems.at[1, k],
            device_id=device,
            device_id_type=MESH,
        )

    def mate(self):
        return (1 - self.core, chip(self.x, self.y, self.z))

    def trade(self):
        return self.copy(0, self.give, self.take, self.mate())

    def returned(self):
        return self.copy(1, self.back, self.again, self.mate())

    def hop(self, k):
        cut = self.half // self.CUT
        at = (slice(None), pl.ds(k * cut, cut))
        return self.copy(
            2 + k, self.leave.at[at], self.come.at[at], (self.core, chip(self.x, self.y, self.z + self.ahead))
        )

    def start(self):
        self.give[...] = low(self.part[:, self.other()])
        self.trade().start()

    def rows(self):
        return self.factors[self.lead, 0:1, self.own()], self.factors[1 - self.lead, 0:1, self.own()]

    def merge(self):
        self.trade().wait_recv()
        own = self.part[:, self.own()]
        got = self.take[...].astype(jnp.float32)
        ahead, behind = jnp.where(self.leads, own, got), jnp.where(self.leads, got, own)
        _, following = self.rows()
        self.front[...] = ahead
        self.total[...] = following * ahead + behind

        @pl.when(self.first)
        def _():
            self.come[...] = jnp.zeros(self.come.shape, self.come.dtype)
            self.leave[...] = low(self.total[...])
            for k in range(self.CUT):
                self.hop(k).start()

    def pass_on(self):
        leading, following = self.rows()
        cut = self.half // self.CUT

        @pl.when(jnp.logical_not(self.first))
        def _():
            for k in range(self.CUT):
                self.hop(k).wait_recv()

                @pl.when(jnp.logical_not(self.last))
                def _():
                    at = (slice(None), slice(k * cut, (k + 1) * cut))
                    both = (leading * following)[:, k * cut : (k + 1) * cut]
                    self.leave[at] = low(both * self.come[at].astype(jnp.float32) + self.total[at])
                    self.hop(k).start()

        came = self.come[...].astype(jnp.float32)
        later = low(leading * came + self.front[...])
        self.back[...] = jnp.where(self.leads, later.astype(jnp.float32), came).astype(jnp.bfloat16)
        self.returned().start()
        self.result[:, self.own()] = jnp.where(self.leads, came, later.astype(jnp.float32)).astype(jnp.bfloat16)

    def close(self):
        self.returned().wait_recv()
        self.result[:, self.other()] = self.again[...]

    def finish(self):
        self.trade().wait_send()
        self.returned().wait_send()

        @pl.when(jnp.logical_not(self.last))
        def _():
            for k in range(self.CUT):
                self.hop(k).wait_send()


VMEM = pl.BlockSpec(memory_space=pltpu.VMEM)
ROWS = 256
HALO = 16
WIDE = 2048
TRANS = (((0,), (0,)), ((), ()))
TRANS_B = (((1,), (1,)), ((), ()))


def dot(a, b, dims=(((1,), (0,)), ((), ()))):
    return lax.dot_general(a, b, dims, preferred_element_type=jnp.float32)


def low(a):
    return a.astype(jnp.bfloat16)


class Shuffle:
    def __init__(self, source, target, sems, offset=0, back=False):
        self.source, self.target, self.sems, self.offset, self.back = source, target, sems, offset, back
        self.x, self.y, self.z, self.core = place()

    def piece(self, k):
        x, y, z, c = self.x, self.y, self.z, self.core
        rows = 128
        if self.back:
            source = self.source.at[pl.ds(rows * k, rows)]
            target = self.target.at[x]
        else:
            source = self.source.at[k]
            if len(self.target.shape) == len(self.source.shape):
                target = self.target.at[self.offset + x]
            else:
                target = self.target.at[pl.ds(pl.multiple_of(self.offset + rows * x, 16), rows)]
        stays = jnp.logical_and(x == k, y == c)
        local = pltpu.make_async_copy(source, target, self.sems.at[1, x])
        remote = pltpu.make_async_remote_copy(
            src_ref=source,
            dst_ref=target,
            send_sem=self.sems.at[0, k],
            recv_sem=self.sems.at[1, x],
            device_id=(y, chip(k, c, z)),
            device_id_type=MESH,
        )
        return stays, local, remote

    def start(self):
        for k in range(2):
            stays, local, remote = self.piece(k)
            pl.when(stays)(local.start)
            pl.when(jnp.logical_not(stays))(remote.start)

    def arrived(self):
        x, y, z, c = self.x, self.y, self.z, self.core
        for k in range(2):
            if self.back:
                target = self.target.at[k]
            elif len(self.target.shape) == len(self.source.shape):
                target = self.target.at[self.offset + k]
            else:
                target = self.target.at[pl.ds(self.offset + 128 * k, 128)]
            stays = jnp.logical_and(x == k, y == c)
            local = pltpu.make_async_copy(target, target, self.sems.at[1, k])
            remote = pltpu.make_async_remote_copy(
                src_ref=target,
                dst_ref=target,
                send_sem=self.sems.at[0, k],
                recv_sem=self.sems.at[1, k],
                device_id=(y, chip(k, c, z)),
                device_id_type=MESH,
            )
            pl.when(stays)(local.wait)
            pl.when(jnp.logical_not(stays))(remote.wait_recv)

    def finish(self):
        for k in range(2):
            stays, local, remote = self.piece(k)
            pl.when(jnp.logical_not(stays))(remote.wait_send)


class Before:
    def __init__(self, source, target, sems, planes):
        self.source, self.target, self.sems, self.planes = source, target, sems, planes
        self.x, self.y, self.z, self.core = place()

    def piece(self, m):
        x, y, z, c = self.x, self.y, self.z, self.core
        source = self.source(m)
        return pltpu.make_async_remote_copy(
            src_ref=source,
            dst_ref=self.target,
            send_sem=self.sems.at[0, m],
            recv_sem=self.sems.at[1, 0],
            device_id=(1 - y, chip(m, c, z + y)),
            device_id_type=MESH,
        )

    def when_sending(self):
        return jnp.logical_and(self.x == 1, jnp.logical_or(self.y == 0, self.z < self.planes - 1))

    def start(self):
        @pl.when(self.when_sending())
        def _():
            for m in range(2):
                self.piece(m).start()

    def arrived(self):
        pl.when(self.z + self.core > 0)(self.piece(0).wait_recv)

    def finish(self):
        @pl.when(self.when_sending())
        def _():
            for m in range(2):
                self.piece(m).wait_send()


class ToAll:
    def __init__(self, table, sems, planes):
        self.table, self.sems, self.count = table, sems, planes * 4
        self.me, self.core = lax.axis_index("seq"), lax.axis_index("dp")

    def copy(self, block, other):
        return pltpu.make_async_remote_copy(
            src_ref=self.table.at[block],
            dst_ref=self.table.at[block],
            send_sem=self.sems.at[0, other],
            recv_sem=self.sems.at[1, block],
            device_id=(self.core, other),
            device_id_type=MESH,
        )

    def over(self, act):
        def one(k, carry):
            act(lax.rem(self.me + k, self.count))
            return carry

        lax.fori_loop(1, self.count, one, 0)

    def start(self):
        self.over(lambda other: self.copy(self.me, other).start())

    def arrived(self):
        self.over(lambda other: self.copy(other, self.me).wait_recv())

    def finish(self):
        self.over(lambda other: self.copy(self.me, other).wait_send())


TILE = 128
TILES = DI // TILE


class Names:
    def __init__(self, names, refs):
        for name, ref in zip(names, refs, strict=True):
            setattr(self, name, ref)


def at_tile(j):
    return pl.ds(pl.multiple_of(j * TILE, TILE), TILE)


def at_rows(k, rows):
    return pl.ds(pl.multiple_of(k * rows, rows), rows)


def loop(low_end, high_end, act):
    def one(k, carry):
        act(k)
        return carry

    lax.fori_loop(low_end, high_end, one, 0)


def iota(shape, dim):
    return lax.broadcasted_iota(jnp.int32, shape, dim)


def pieces(a):
    high = low(a)
    rest = a - high.astype(jnp.float32)
    middle = low(rest)
    return high, middle, low(rest - middle.astype(jnp.float32))


def packed(a):
    a = jnp.where(iota(a.shape, 1) < H, a, 0.0)
    high, middle, rest = (part.astype(jnp.float32) for part in pieces(a))
    return low(high + pltpu.roll(middle, 32, 1) + pltpu.roll(rest, 64, 1))


def spread_matrix(width, first=0):
    row, col = iota((128, width), 0), iota((128, width), 1) + first
    return low(jnp.where(jnp.logical_and(row % 32 == col // P_SIZE, row < 96), 1.0, 0.0))


def head_sums(a, j):
    row, col = iota((TILE, 128), 0), iota((TILE, 128), 1)
    pick = low(jnp.where(row // P_SIZE + 2 * j == col, 1.0, 0.0))
    high, middle, _ = pieces(a)
    return dot(jnp.concatenate([high, middle], axis=1), jnp.concatenate([pick, pick], axis=0))


def sigmoid(v):
    return 1.0 / (1.0 + jnp.exp(-v))


GIVEN = ["tok_in", "cot", "seg_in", "small_in", "w_in", "wout"]
MADE = ["act_out", "tokens_out", "grad_a", "grad_z", "grad_out", "small_out"]


def block_scratch(planes):
    f32, bf16 = jnp.float32, jnp.bfloat16
    v = pltpu.VMEM
    dma = pltpu.SemaphoreType.DMA
    two = dma((2, 2))
    return {
        "wa": v((768, WIDE), bf16), "wa_sem": gather_sems(planes), "tok": v((HALO + ROWS, 768), bf16), "seg": v((3, 8, 128), f32),
        "normed": v((HALO + ROWS, 768), bf16), "proj": v((HALO + ROWS, WIDE), f32), "conv": v((8, CH), f32), "gain": v((8, DI), f32),
        "ngain": v((8, 768), f32), "ngrad": v((8, 768), f32), "scale": v((ROWS, 128), f32), "given": v((16, 8, 128), f32), "numbers": v((2, 8, 128), f32),
        "tok_sem": two, "end_sem": two, "seg_sem": two, "segend_sem": two, "given_sem": dma((2, 16)),
        "wz_full": v((768, DI), bf16), "wout_full": v((DI, 768), bf16), "wz_sem": gather_sems(planes), "wout_sem": gather_sems(planes),
        "cot_own": v((ROWS, 768), bf16), "cot_sem": two, "act_sem": two, "back_sem": two,
        "segcol": v((384, 128), f32), "same": v((KC, ROWS + HALO, 128), f32),
        "pre": v((ROWS, CH), f32), "inner": v((ROWS, DI), f32), "bproj": v((ROWS, N), bf16), "cproj": v((ROWS, N), bf16),
        "cumt": v((H, 8, ROWS), f32), "bar": v((ROWS, ROWS), f32), "scores": v((ROWS, ROWS), f32),
        "step": v((ROWS, 128), f32), "cum": v((ROWS, 128), f32), "ein": v((ROWS, 128), f32), "eout": v((ROWS, 128), f32),
        "stepx": v((ROWS, DI), f32), "einx": v((ROWS, DI), f32), "eoutx": v((ROWS, DI), f32), "cumx": v((ROWS, DI), f32),
        "xs": v((ROWS, DI), bf16), "xso": v((ROWS, DI), bf16),
        "part": v((N, DI), f32), "factors": v((2, 8, DI), f32), "factor_sem": dma((2,)), "skipx": v((8, DI), f32),
        "state": v((N, DI), bf16), "dstate": v((N, DI), bf16),
        "y": v((ROWS, DI), f32), "z": v((ROWS, DI), f32), "gated": v((ROWS, DI), bf16), "act_own": v((ROWS, 768), bf16),
        "dz": v((ROWS, DI), bf16), "dy": v((ROWS, DI), bf16), "dyin": v((ROWS, DI), bf16),
        "ggain": v((8, DI), f32), "gskip": v((8, DI), f32),
        "dscores": v((ROWS, ROWS), f32), "dxs": v((ROWS, DI), f32), "sums": v((3, ROWS, 128), f32),
        "dpre": v((KC, ROWS + HALO, TILE), f32), "late": v((8, CH), f32), "dx": v((HALO + ROWS, WIDE), bf16), "tail": v((8, CH), f32), "tail_in": v((8, CH), f32), "tail_sem": dma((2,)),
        "gconv": v((8, CH), f32), "gtok": v((ROWS, 768), bf16),
        "table": v((16, 8, 128), f32), "inbox": v((2, 16, 8, 128), f32), "table_sem": dma((2, 2, 16)),
        "part_a": v((2, 768, WIDE // 2), bf16), "part_z": v((768, DI), bf16), "part_out": v((DI, 768), bf16),
    }


def block_kernel(planes, names, *refs):
    r = Names(GIVEN + MADE + names, refs[: len(GIVEN) + len(MADE) + len(names)])
    extra = list(refs[len(GIVEN) + len(MADE) + len(names) :])
    chain_f, chain_b = extra[0:9], extra[9:15] + extra[6:8] + extra[15:16]
    red_a, red_b, red_z, red_out = extra[16:20], extra[20:24], extra[24:28], extra[28:32]
    x, y, z, c = place()
    me = chip(x, y, z)
    mate = (1 - c, me)
    f32 = jnp.float32
    greet_all(planes)
    r.wa[pl.ds(pl.multiple_of(me * 48, 16), 48), 0:CH] = r.w_in[:, DI : DI + CH]
    step_columns = r.w_in[:, DI + CH :]
    fill = jnp.zeros((48, WIDE - CH - H), step_columns.dtype)
    r.wa[pl.ds(pl.multiple_of(me * 48, 16), 48), CH:] = jnp.concatenate([step_columns, fill], axis=1)
    r.wz_full[pl.ds(pl.multiple_of(me * 48, 16), 48), :] = r.w_in[:, 0:DI]
    r.wout_full[pl.ds(pl.multiple_of(me * 96, 16), 96), :] = r.wout[...]
    r.given[me] = r.small_in[0:8, :]
    for m in range(2):
        r.numbers[m] = jnp.broadcast_to(r.seg_in[m : m + 1, :].astype(f32) + 1.0, (8, 128))

    @pl.when(z + c == 0)
    def _():
        r.tok[0:HALO, :] = jnp.zeros((HALO, 768), r.tok.dtype)
        r.seg[0] = jnp.full((8, 128), -1.0, f32)

    gather_a = Gather(r.wa, 48, "columns", r.wa_sem, planes)
    gather_z = Gather(r.wz_full, 48, "columns", r.wz_sem, planes)
    gather_out = Gather(r.wout_full, 96, "rows", r.wout_sem, planes)
    cots = Shuffle(r.cot, r.cot_own, r.cot_sem)
    moves = [
        Shuffle(r.tok_in, r.tok, r.tok_sem, HALO),
        Before(lambda m: r.tok_in.at[m, pl.ds(128 - HALO, HALO)], r.tok.at[pl.ds(0, HALO)], r.end_sem, planes),
        Shuffle(r.numbers, r.seg, r.seg_sem, 1),
        Before(lambda m: r.numbers.at[m], r.seg.at[0], r.segend_sem, planes),
        ToAll(r.given, r.given_sem, planes),
    ]
    meet_all(planes)
    for item in moves:
        item.start()
    gather_a.begin()
    gather_a.column(1)
    gather_a.sides(0)
    for item in moves:
        item.arrived()
    r.conv[...] = jnp.concatenate([r.given[k, :, 0:112] for k in range(16)], axis=1)
    r.gain[...] = jnp.concatenate([r.given[k, :, 0:96] for k in range(16)], axis=1)
    r.ngain[...] = jnp.concatenate([r.given[k, :, 0:48] for k in range(16)], axis=1)
    gather_a.column(2)
    gather_a.column(3)
    gather_a.sides(1)
    gather_a.diagonal(0)
    u = r.tok[...].astype(f32)
    r.normed[...] = low(u * lax.rsqrt(jnp.mean(u * u, axis=-1, keepdims=True) + EPSILON) * r.ngain[5:6, :])
    gather_z.begin_column()
    gather_a.sides(2)
    gather_a.diagonal(1)

    for k in range(3):
        r.segcol[128 * k : 128 * k + 128, :] = jnp.transpose(jnp.broadcast_to(r.seg[k, 0:1, :], (128, 128)))
    seg = r.segcol[128:384, :]
    for k in range(KC):
        r.same[k] = jnp.zeros((ROWS + HALO, 128), f32)
        r.same[k, 8 : 8 + ROWS, :] = jnp.where(r.segcol[125 + k : 125 + k + ROWS, :] == seg, 1.0, 0.0)
    gather_a.sides(3)
    gather_z.begin_sides()
    gather_a.diagonal(2)
    for d in range(1, planes):
        gather_z.column(d)
    cots.start()
    gather_out.begin()
    gather_a.diagonal(3)
    gather_a.whole_here()

    def project(k):
        at_k = pl.ds(pl.multiple_of(k * 512, 512), 512)
        r.proj[:, at_k] = dot(r.normed[...], r.wa[:, at_k])

    project(WIDE // 512 - 1)

    def convolve(j):
        at = at_tile(j)
        total = jnp.broadcast_to(r.conv[4:5, at], (ROWS, TILE))
        for k in range(KC):
            total = total + r.conv[k : k + 1, at] * r.proj[13 + k : 13 + k + ROWS, at] * r.same[k, 8 : 8 + ROWS, :]
        r.pre[:, at] = total
        return total * sigmoid(total)

    r.bproj[...] = low(convolve(TILES))
    r.cproj[...] = low(convolve(TILES + 1))

    raw = r.proj[HALO:, CH : CH + 128] + r.small_in[8:9, :]
    step = jnp.maximum(raw, 0.0) + jnp.log1p(jnp.exp(-jnp.abs(raw)))
    rate = -jnp.exp(r.small_in[9:10, :])
    lower = jnp.where(iota((ROWS, ROWS), 0) >= iota((ROWS, ROWS), 1), 1.0, 0.0)
    cum = jnp.dot(lower, step * rate, precision=HIGHEST, preferred_element_type=f32)
    r.step[...] = step
    r.cum[...] = cum
    across = jnp.transpose(cum)
    for h in range(H):
        r.cumt[h] = jnp.broadcast_to(across[h : h + 1, :], (8, ROWS))
    last = cum[ROWS - 1 : ROWS, :]
    before = r.segcol[127:128, :]
    first_seg, last_seg = seg[0:1, :], seg[ROWS - 1 : ROWS, :]
    r.ein[...] = jnp.where(seg == before, jnp.exp(cum), 0.0)
    r.eout[...] = jnp.where(seg == last_seg, jnp.exp(last - cum), 0.0)
    through = jnp.logical_and(first_seg == last_seg, first_seg == before)
    factor = jnp.where(through, jnp.exp(last), 0.0)
    segrow = jnp.concatenate([r.seg[1, 0:1, :], r.seg[2, 0:1, :]], axis=1)
    allowed = jnp.logical_and(jnp.concatenate([seg, seg], axis=1) == segrow, iota((ROWS, ROWS), 0) >= iota((ROWS, ROWS), 1))
    r.bar[...] = jnp.where(allowed, 0.0, -1e30)
    rows = packed(jnp.concatenate([jnp.broadcast_to(factor, (8, 128)), jnp.broadcast_to(r.small_in[10:11, :], (8, 128))], axis=0))
    both = dot(rows, spread_matrix(DI))
    r.factors[c] = both[0:8, :]
    r.skipx[...] = both[8:16, :]
    share = pltpu.make_async_remote_copy(
        src_ref=r.factors.at[c], dst_ref=r.factors.at[c], send_sem=r.factor_sem.at[0], recv_sem=r.factor_sem.at[1],
        device_id=mate, device_id_type=MESH,
    )
    share.start()
    spreads = [(r.stepx, packed(step)), (r.einx, packed(r.ein[...])), (r.eoutx, packed(r.eout[...])), (r.cumx, packed(cum))]
    r.stepx[...] = dot(spreads[0][1], spread_matrix(DI))
    r.eoutx[...] = dot(spreads[2][1], spread_matrix(DI))
    loop(0, WIDE // 512 - 1, project)

    def trade_order(k):
        return lax.rem(k + TILES // 2 * (1 - c), TILES)

    def outgoing(k):
        j = trade_order(k)
        at = at_tile(j)
        inner = convolve(j)
        r.inner[:, at] = inner
        scaled = r.stepx[:, at] * inner
        r.xs[:, at] = low(scaled)
        xso = low(scaled * r.eoutx[:, at])
        r.xso[:, at] = xso
        r.part[:, at] = dot(r.bproj[...], xso, TRANS)

    loop(0, TILES // 2, outgoing)
    forward = Chain(r.part, r.state, r.factors, chain_f, 0, planes)
    forward.start()
    loop(TILES // 2, TILES, outgoing)
    share.wait_recv()
    forward.merge()
    r.scores[...] = dot(r.cproj[...], r.bproj[...], TRANS_B)
    r.einx[...] = dot(spreads[1][1], spread_matrix(DI))
    r.cumx[...] = dot(spreads[3][1], spread_matrix(DI))
    gather_z.sides(0)
    for d in range(1, planes):
        gather_out.column(d)

    first_half = iota((1, TILE), 1) < P_SIZE

    def decays(j, band):
        size = 128 * (band + 1)
        rows = slice(128 * band, 128 * band + 128)
        tile = r.cumx[rows, at_tile(j)]
        turned = pltpu.roll(tile, P_SIZE, 1)
        out = []
        for k in range(2):
            column = jnp.where(first_half, tile, turned) if k == 0 else jnp.where(first_half, turned, tile)
            wide = column if band == 0 else jnp.concatenate([column, column], axis=1)
            out.append(jnp.exp(wide - r.cumt[2 * j + k, 0:1, 0:size] + r.bar[rows, 0:size]))
        return out

    def halves(tile):
        zero = jnp.zeros_like(tile)
        return jnp.where(first_half, tile, zero), jnp.where(first_half, zero, tile)

    def within(j):
        at = at_tile(j)
        for band in range(2):
            size = 128 * (band + 1)
            rows = slice(128 * band, 128 * band + 128)
            inside = halves(r.xs[0:size, at])
            total = 0.0
            for decay, xs in zip(decays(j, band), inside):
                total = total + dot(low(decay * r.scores[rows, 0:size]), xs)
            r.y[rows, at] = total

    def turn(chain, when):
        for k in range(planes):
            if when[k]:
                position = k if chain.lead == 0 else planes - 1 - k
                pl.when(z == position)(chain.pass_on)

    turn(forward, [1, 0, 0, 0])
    loop(0, 4, within)
    turn(forward, [0, 1, 0, 0])
    gather_z.sides(1)
    gather_z.diagonal(0)
    gather_out.sides(0)
    loop(4, 8, within)
    turn(forward, [0, 0, 1, 0])
    gather_z.sides(2)
    gather_z.diagonal(1)
    gather_out.sides(1)
    gather_out.diagonal(0)
    loop(8, 12, within)
    gather_z.sides(3)
    gather_z.diagonal(2)
    for item in moves + [gather_a]:
        item.finish()
    turn(forward, [0, 0, 0, 1])
    gather_out.sides(2)
    gather_out.diagonal(1)
    gather_z.diagonal(3)
    forward.close()

    def carried(j):
        at = at_tile(j)
        r.y[:, at] = r.y[:, at] + r.einx[:, at] * dot(r.cproj[...], r.state[:, at])

    loop(0, TILES, carried)
    gather_z.whole_here()

    def project_z(j):
        at = at_rows(j, 512)
        r.z[:, at] = dot(r.normed[HALO:, :], r.wz_full[:, at])

    loop(0, 3, project_z)
    gather_out.sides(3)
    gather_out.diagonal(2)

    def gated_values(rows):
        gate_in = r.z[rows, :]
        sig = sigmoid(gate_in)
        mixed = r.y[rows, :] + r.skipx[0:1, :] * r.inner[rows, :]
        return gate_in, sig, mixed, mixed * (gate_in * sig)

    def gate(k):
        rows = at_rows(k, 16)
        _, _, _, v = gated_values(rows)
        scale = lax.rsqrt(jnp.mean(v * v, axis=-1, keepdims=True) + EPSILON)
        r.scale[rows, :] = jnp.broadcast_to(scale, (16, 128))
        r.gated[rows, :] = low(v * scale * r.gain[6:7, :])

    loop(0, ROWS // 16, gate)
    gather_out.diagonal(3)
    gather_out.whole_here()
    cots.arrived()

    def project_cot(j):
        at = at_rows(j, 512)
        r.dxs[:, at] = dot(r.cot_own[...], r.wout_full[at, :], TRANS_B)

    loop(0, 3, project_cot)
    r.ggain[...] = jnp.zeros((8, DI), f32)
    r.gskip[...] = jnp.zeros((8, DI), f32)

    def gate_back(k):
        rows = at_rows(k, 16)
        gate_in, sig, mixed, v = gated_values(rows)
        scale = r.scale[rows, 0:1]
        dgated = r.dxs[rows, :]
        weighed = dgated * (v * scale)
        r.ggain[...] = r.ggain[...] + weighed[0:8, :] + weighed[8:16, :]
        a = r.gain[6:7, :] * dgated
        dv = scale * (a - v * (scale * scale) * jnp.mean(v * a, axis=-1, keepdims=True))
        dmixed = dv * (gate_in * sig)
        r.z[rows, :] = dmixed
        r.dy[rows, :] = low(dmixed)
        r.dyin[rows, :] = low(dmixed * r.einx[rows, :])
        r.dz[rows, :] = low(dv * mixed * (sig * (1.0 + gate_in * (1.0 - sig))))
        skip = dmixed * r.inner[rows, :]
        r.gskip[...] = r.gskip[...] + skip[0:8, :] + skip[8:16, :]

    loop(0, ROWS // 16, gate_back)

    def incoming(j):
        at = at_tile(j)
        r.part[:, at] = dot(r.cproj[...], r.dyin[:, at], TRANS)

    loop(0, TILES // 2, lambda k: incoming(trade_order(k)))
    backward = Chain(r.part, r.dstate, r.factors, chain_b, 1, planes)
    backward.start()
    loop(TILES // 2, TILES, lambda k: incoming(trade_order(k)))
    reduce_out = Reduce(r.part_out, r.grad_out, 96, "rows", red_out, planes)
    reduce_z = Reduce(r.part_z, r.grad_z, 48, "columns", red_z, planes)
    every = range(planes - 1, -1, -1)

    def project_out(k):
        at = at_rows(k, 256)
        r.act_own[:, at] = low(r.tok[HALO:, at].astype(f32) + dot(r.gated[...], r.wout_full[:, at]))

    loop(0, 3, project_out)
    acts = Shuffle(r.act_own, r.act_out, r.act_sem, back=True)
    acts.start()

    def weights_out(k):
        far = lax.rem(z + 1 + k, planes)
        at = pl.ds(pl.multiple_of(far * (DI // planes), 128), DI // planes)
        r.part_out[at, :] = low(dot(r.gated[:, at], r.cot_own[...], TRANS))
        reduce_out.move(reduce_out.MATE, far).start()

    loop(0, 2, weights_out)
    backward.merge()
    turn(backward, [1, 0, 0, 0])
    loop(2, planes, weights_out)

    def weights_z(k):
        half = lax.rem(k // 3 + 1 + c, 2)
        at = pl.ds(pl.multiple_of(half * (DI // 2) + k % 3 * 256, 256), 256)
        r.part_z[:, at] = low(dot(r.normed[HALO:, :], r.dz[:, at], TRANS))

    loop(0, 3, weights_z)
    for d in every:
        reduce_z.start(d)
    for d in every:
        reduce_out.fold(d)
    turn(backward, [0, 1, 0, 0])
    loop(3, 6, weights_z)
    for d in every:
        reduce_z.fold(d)

    def back_z(k):
        at = at_rows(k, 256)
        r.einx[:, at] = dot(r.dz[...], r.wz_full[at, :], TRANS_B)

    loop(0, 3, back_z)

    def reduce_sides(d):
        reduce_out.sides(d)
        reduce_z.sides(d)

    def reduce_column(d):
        reduce_out.column(d)
        reduce_z.column(d)

    r.dscores[...] = jnp.zeros((ROWS, ROWS), f32)
    r.sums[...] = jnp.zeros((3, ROWS, 128), f32)

    def within_back(j):
        at = at_tile(j)
        upper = lower = 0.0
        for band in range(2):
            size = 128 * (band + 1)
            rows = slice(128 * band, 128 * band + 128)
            xs = r.xs[0:size, at]
            grads = 0.0
            for decay, dy in zip(decays(j, band), halves(r.dy[rows, at])):
                weight = low(decay * r.scores[rows, 0:size])
                grads = grads + decay * dot(dy, xs, TRANS_B)
                upper = upper + dot(weight[:, 0:128], dy, TRANS)
                if band:
                    lower = lower + dot(weight[:, 128:256], dy, TRANS)
            r.dscores[rows, 0:size] = r.dscores[rows, 0:size] + grads
        r.dxs[0:128, at] = upper
        r.dxs[128:256, at] = lower
        gain = r.dy[:, at].astype(f32) * r.y[:, at] - r.xs[:, at].astype(f32) * r.dxs[:, at]
        r.sums[0] = r.sums[0] + head_sums(gain, j)
        inside = r.dxs[:, at]
        r.sums[2] = r.sums[2] + head_sums(r.inner[:, at] * inside, j)
        r.dxs[:, at] = r.skipx[0:1, at] * r.z[:, at] + r.stepx[:, at] * inside

    loop(0, 2, within_back)
    turn(backward, [0, 0, 1, 0])
    reduce_sides(3)
    loop(2, 5, within_back)
    reduce_sides(2)
    reduce_column(3)
    loop(5, 8, within_back)
    reduce_sides(1)
    reduce_column(2)
    turn(backward, [0, 0, 0, 1])
    loop(8, 12, within_back)
    for item in (gather_z, gather_out, cots, forward):
        item.finish()
    share.wait_send()
    backward.close()
    reduce_sides(0)

    def last_sums(j):
        at = at_tile(j)
        far = r.eoutx[:, at] * dot(r.bproj[...], r.dstate[:, at])
        r.sums[1] = r.sums[1] + head_sums(r.inner[:, at] * far, j)
        return r.dxs[:, at] + r.stepx[:, at] * far

    def unconvolve(j, grad):
        at = at_tile(j)
        pre = r.pre[:, at]
        sig = sigmoid(pre)
        grad = grad * (sig * (1.0 + pre * (1.0 - sig)))
        taps = []
        for k in range(KC):
            kept = grad if k == KC - 1 else grad * r.same[k, 8 : 8 + ROWS, :]
            r.dpre[k, 8 : 8 + ROWS, :] = kept
            taps.append(jnp.sum(kept * r.proj[13 + k : 13 + k + ROWS, at], axis=0, keepdims=True))
        taps += [jnp.sum(grad, axis=0, keepdims=True), jnp.zeros((3, TILE), f32)]
        r.gconv[:, at] = jnp.concatenate(taps, axis=0)
        total = 0.0
        for k in range(KC):
            total = total + r.conv[k : k + 1, at] * r.dpre[k, 3 - k : 3 - k + 8 + ROWS, :]
        r.tail[:, at] = total[0:8, :]
        r.dx[0:HALO, at] = low(jnp.concatenate([jnp.zeros((8, TILE), f32), total[0:8, :]], axis=0))
        r.dx[HALO:, at] = low(total[8:, :])
        r.late[:, at] = total[ROWS : ROWS + 8, :]

    reduce_first = Reduce(r.part_a.at[0], r.grad_a.at[0], 48, "columns", red_a, planes)
    reduce_second = Reduce(r.part_a.at[1], r.grad_a.at[1], 48, "columns", red_b, planes)

    def weights_a(group, k):
        half = lax.rem(k + 1 + c, 2)
        at = pl.ds(pl.multiple_of(half * (WIDE // 4), 512), 512)
        from_ = pl.ds(pl.multiple_of(group * (WIDE // 2) + half * (WIDE // 4), 512), 512)
        r.part_a[group, :, at] = low(dot(r.normed[...], r.dx[:, from_], TRANS))

    def columns_back(j):
        unconvolve(j, last_sums(j))

    r.dx[0:HALO, CH:] = jnp.zeros((HALO, WIDE - CH), jnp.bfloat16)
    r.dx[HALO:, CH + 128 :] = jnp.zeros((ROWS, WIDE - CH - 128), jnp.bfloat16)
    r.dpre[...] = jnp.zeros((KC, ROWS + HALO, TILE), f32)
    loop(0, 8, columns_back)
    weights_a(0, 0)
    for d in every:
        reduce_first.start(d)
    weights_a(0, 1)
    reduce_column(1)
    loop(8, 12, columns_back)
    for d in every:
        reduce_first.fold(d)
    dscores = low(r.dscores[...])
    dbproj = dot(dscores, r.cproj[...], TRANS) + dot(r.xso[...], r.dstate[...], TRANS_B)
    dcproj = dot(dscores, r.bproj[...]) + dot(r.dyin[...], r.state[...], TRANS_B)
    pick = jnp.where(iota((DI, 128), 0) // P_SIZE == iota((DI, 128), 1), 1.0, 0.0)
    crossing = jnp.sum(r.dstate[...].astype(f32) * r.state[...].astype(f32), axis=0, keepdims=True) * r.factors[c, 0:1, :]
    rows = jnp.concatenate([jnp.broadcast_to(crossing, (8, DI)), r.gskip[...]], axis=0)
    rows = jnp.dot(rows, pick, precision=HIGHEST, preferred_element_type=f32)
    at_end, gskip = rows[0:1, :], jnp.sum(rows[8:16, :], axis=0, keepdims=True)
    upper = jnp.where(iota((ROWS, ROWS), 0) <= iota((ROWS, ROWS), 1), 1.0, 0.0)
    strict = jnp.where(iota((ROWS, ROWS), 0) > iota((ROWS, ROWS), 1), 1.0, 0.0)
    dlog = (
        jnp.dot(upper, r.sums[0], precision=HIGHEST, preferred_element_type=f32)
        + jnp.dot(strict, r.step[...] * r.sums[1], precision=HIGHEST, preferred_element_type=f32)
        + at_end
    )
    step = r.step[...]
    dstep = r.sums[1] + r.sums[2] + rate * dlog
    draw = dstep * sigmoid(r.proj[HALO:, CH : CH + 128] + r.small_in[8:9, :])
    lanes = iota((1, 128), 1) < H
    draw = jnp.where(lanes, draw, 0.0)
    gbias = jnp.sum(draw, axis=0, keepdims=True)
    glog = jnp.where(lanes, jnp.sum(step * dlog, axis=0, keepdims=True) * rate, 0.0)
    r.dx[HALO:, CH : CH + 128] = low(draw)
    unconvolve(TILES, dbproj)
    unconvolve(TILES + 1, dcproj)
    tails = [
        pltpu.make_async_remote_copy(
            src_ref=r.tail, dst_ref=r.tail_in, send_sem=r.tail_sem.at[0], recv_sem=r.tail_sem.at[1],
            device_id=(1 - c, chip(x, y, z - 1 + c)), device_id_type=MESH,
        )
    ]
    pl.when(z + c > 0)(tails[0].start)

    @pl.when(z + c == planes)
    def _():
        r.tail_in[...] = jnp.zeros((8, CH), f32)

    weights_a(1, 0)
    for d in every:
        reduce_second.start(d)
    weights_a(1, 1)
    reduce_first.sides(3)
    reduce_column(0)
    for d in every:
        reduce_second.fold(d)
    reduce_first.sides(2)
    reduce_out.close()
    reduce_z.close()
    pl.when(z + c < planes)(tails[0].wait_recv)
    r.dx[HALO + ROWS - 16 :, 0:CH] = low(
        jnp.concatenate([r.dx[HALO + ROWS - 16 : HALO + ROWS - 8, 0:CH].astype(f32), r.late[...] + r.tail_in[...]], axis=0)
    )

    def back_in(k):
        at = at_rows(k, 256)
        r.y[:, at] = r.einx[:, at] + dot(r.dx[HALO:, :], r.wa[at, :], TRANS_B)

    loop(0, 3, back_in)
    reduce_first.sides(1)
    reduce_first.column(3)
    reduce_second.sides(3)
    r.ngrad[...] = jnp.zeros((8, 768), f32)

    def norm_back(k):
        rows = at_rows(k, 16)
        dnormed = r.y[rows, 0:768]
        u = r.tok[pl.ds(pl.multiple_of(HALO + 16 * k, 16), 16), :].astype(f32)
        scale = lax.rsqrt(jnp.mean(u * u, axis=-1, keepdims=True) + EPSILON)
        weighed = dnormed * u * scale
        r.ngrad[...] = r.ngrad[...] + weighed[0:8] + weighed[8:16]
        a = r.ngain[5:6, :] * dnormed
        grad = scale * (a - u * (scale * scale) * jnp.mean(u * a, axis=-1, keepdims=True))
        r.gtok[rows, :] = low(r.cot_own[rows, :].astype(f32) + grad)

    loop(0, 8, norm_back)
    reduce_first.sides(0)
    reduce_first.column(2)
    reduce_second.sides(2)
    reduce_second.column(3)
    loop(8, 16, norm_back)
    grads = Shuffle(r.gtok, r.tokens_out, r.back_sem, back=True)
    grads.start()
    reduce_first.column(1)
    reduce_second.sides(1)
    reduce_second.column(2)
    ngain = jnp.sum(r.ngrad[...], axis=0, keepdims=True)
    ggain = jnp.sum(r.ggain[...], axis=0, keepdims=True)
    lane_heads = jnp.concatenate([gbias[:, 0:H], glog[:, 0:H], gskip[:, 0:H], jnp.zeros((1, 128 - 3 * H), f32)], axis=1)
    for k in range(16):
        convs = jnp.concatenate([r.gconv[0:5, 112 * k : 112 * k + 112], jnp.zeros((5, 16), f32)], axis=1)
        first = jnp.concatenate([ngain[:, 48 * k : 48 * k + 48], jnp.zeros((1, 80), f32)], axis=1)
        second = jnp.concatenate([ggain[:, 96 * k : 96 * k + 96], jnp.zeros((1, 32), f32)], axis=1)
        r.table[k] = jnp.concatenate([convs, first, second, lane_heads], axis=0)

    def to_all(k, act):
        other = lax.rem(me + k, 16)
        for far in range(2):
            copy = pltpu.make_async_remote_copy(
                src_ref=r.table.at[other], dst_ref=r.inbox.at[c, me], send_sem=r.table_sem.at[0, far, other],
                recv_sem=r.table_sem.at[1, c, me], device_id=(far, other), device_id_type=MESH,
            )
            pl.when(jnp.logical_or(k > 0, far != c))(functools.partial(act, copy))

    def from_all(k):
        other = lax.rem(me + k, 16)
        for far in range(2):
            copy = pltpu.make_async_remote_copy(
                src_ref=r.table.at[other], dst_ref=r.inbox.at[far, other], send_sem=r.table_sem.at[0, far, other],
                recv_sem=r.table_sem.at[1, far, other], device_id=(far, other), device_id_type=MESH,
            )
            pl.when(jnp.logical_or(k > 0, far != c))(copy.wait_recv)

    loop(0, 16, lambda k: to_all(k, lambda copy: copy.start()))
    r.inbox[c, me] = r.table[me]
    for item in (reduce_out, reduce_z):
        item.drain_early()
        item.drain_late()
        item.finish()
    for item in (backward, acts):
        item.finish()
    acts.arrived()
    reduce_second.sides(0)
    reduce_first.column(0)
    reduce_second.column(1)
    reduce_first.close()
    reduce_first.drain_early()
    reduce_second.drain_early()
    reduce_first.drain_late()
    loop(0, 16, lambda k: to_all(k, lambda copy: copy.wait_send()))
    pl.when(z + c > 0)(tails[0].wait_send)
    reduce_second.column(0)
    reduce_second.close()
    loop(0, 16, from_all)
    r.small_out[...] = jnp.sum(jnp.sum(r.inbox[...], axis=0), axis=0)
    reduce_second.drain_late()
    grads.finish()
    grads.arrived()
    reduce_first.finish()
    reduce_second.finish()


def block(given, planes):
    f32, bf16 = jnp.float32, jnp.bfloat16
    shape = jax.ShapeDtypeStruct
    named = block_scratch(planes)
    extra = Chain.scratch() + Chain.scratch()[:6] + Chain.scratch()[8:]
    extra += Reduce.scratch(48, WIDE // 2, "columns", planes) + Reduce.scratch(48, WIDE // 2, "columns", planes) + Reduce.scratch(48, DI, "columns", planes)
    extra += Reduce.scratch(96, 768, "rows", planes)
    return pl.pallas_call(
        functools.partial(block_kernel, planes, list(named)),
        out_shape=[
            shape((2, 128, 768), bf16), shape((2, 128, 768), bf16), shape((2, 48, WIDE // 2), f32),
            shape((48, DI), f32), shape((96, 768), f32), shape((8, 128), f32),
        ],
        in_specs=[VMEM] * len(GIVEN),
        out_specs=[VMEM] * len(MADE),
        scratch_shapes=list(named.values()) + extra,
        compiler_params=pltpu.CompilerParams(collective_id=0, has_side_effects=True, vmem_limit_bytes=62 << 20),
    )(*given)


def deliver_kernel(acts, tokens, grad_a, grad_z, grad_out, sums, *out):
    out[0][...] = acts[...]
    out[1][...] = tokens[...]
    out[2][...] = sums[5:6, 0:48]
    out[3][:, 0:DI] = grad_z[...]
    out[3][:, DI : DI + WIDE // 2] = grad_a[0]
    out[3][:, DI + WIDE // 2 :] = grad_a[1, :, 0 : CH + H - WIDE // 2]
    out[4][...] = sums[0:4, 0:112]
    out[5][...] = sums[4:5, 0:112]
    out[6][...] = sums[7:8, 0:H]
    out[7][...] = sums[7:8, H : 2 * H]
    out[8][...] = sums[7:8, 2 * H : 3 * H]
    out[9][...] = sums[6:7, 0:96]
    out[10][...] = grad_out[...]


def deliver(made):
    f32, bf16 = jnp.float32, jnp.bfloat16
    shapes = [
        ((2, 128, 768), bf16), ((2, 128, 768), bf16), ((1, 48), f32), ((48, DI + CH + H), f32), ((4, 112), f32), ((1, 112), f32),
        ((1, H), f32), ((1, H), f32), ((1, H), f32), ((1, 96), f32), ((96, 768), f32),
    ]
    return pl.pallas_call(
        deliver_kernel,
        out_shape=[jax.ShapeDtypeStruct(*s) for s in shapes],
        in_specs=[VMEM] * len(made),
        out_specs=[VMEM] * len(shapes),
    )(*made)


def fast_body(
    planes, tokens, cotangent, segments, norm_gain, w_in, conv_weight, conv_bias, step_bias, log_rate, skip_gain, gate_gain, w_out
):
    def at_row(row, values):
        values = values.astype(jnp.float32).reshape(-1, values.shape[-1])
        return jnp.pad(values, ((row, 16 - row - values.shape[0]), (0, 128 - values.shape[1])))

    rows = ((0, conv_weight), (4, conv_bias), (5, norm_gain), (6, gate_gain), (8, step_bias), (9, log_rate), (10, skip_gain))
    small = sum(at_row(row, values) for row, values in rows)
    made = block((tokens[:, 0], cotangent[:, 0], segments[:, 0], small, w_in, w_out), planes)
    out = deliver(made)
    return (
        out[0][:, None], out[1][:, None], out[2][0], out[3], out[4], out[5][0], out[6][0], out[7][0], out[8][0], out[9][0], out[10],
    )


def solution(mesh):
    in_specs = (
        P(None, "dp", "seq", None),
        P(None, "dp", "seq", None),
        P(None, "dp", "seq"),
        P("seq"),
        P("seq", None),
        P(None, "seq"),
        P("seq"),
        P(),
        P(),
        P(),
        P("seq"),
        P("seq", None),
    )
    out_specs = (
        P(None, "dp", "seq", None),
        P(None, "dp", "seq", None),
        P("seq"),
        P("seq", None),
        P(None, "seq"),
        P("seq"),
        P(),
        P(),
        P(),
        P("seq"),
        P("seq", None),
    )
    work = partial(fast_body, mesh.shape["seq"] // 4) if mesh.shape["seq"] == 16 else body
    return jax.shard_map(work, mesh=mesh, in_specs=in_specs, out_specs=out_specs, check_vma=False)
```

```python
import functools
from functools import partial

import jax
import jax.numpy as jnp
from jax import lax
from jax.experimental import pallas as pl
from jax.experimental.pallas import tpu as pltpu
from jax.sharding import PartitionSpec as P

DI = 1536
H = 24
P_SIZE = 64
N = 128
KC = 4
CH = 1792


EPSILON = 1e-05
HIGHEST = lax.Precision.HIGHEST


def passed_along(array, axis, by):
    devices = lax.axis_size(axis)
    pairs = [(i, i + by) for i in range(devices) if 0 <= i + by < devices]
    return lax.ppermute(array, axis, pairs)


def prefix(array, axis, combine, identity, reverse):
    devices, place = (lax.axis_size(axis), lax.axis_index(axis))
    everything = jax.tree.map(lambda part: lax.all_gather(part, axis), array)
    start = jax.tree.map(
        lambda part, zero: jnp.broadcast_to(jnp.asarray(zero, part.dtype), part.shape),
        array,
        identity,
    )

    def lap(k, before):
        at = devices - 1 - k if reverse else k
        reached = at > place if reverse else at < place
        new = combine(before, jax.tree.map(lambda part: part[at], everything))
        return jax.tree.map(lambda a, b: jnp.where(reached, a, b), new, before)

    return lax.fori_loop(0, devices, lap, start)


def for_sending(array):
    return jax.tree.map(lambda a: a.astype(jnp.bfloat16) if a.dtype == jnp.float32 else a, array)


def rms_scale(values, gain_vec):
    return (
        values * lax.rsqrt(jnp.mean(values * values, axis=-1, keepdims=True) + EPSILON) * gain_vec
    )


def causal_conv(padded, seg_pad, seg_one, kernel, offset):
    length_t = seg_one.shape[0]
    total = jnp.zeros((length_t, padded.shape[1]), jnp.float32) + offset[None, :]
    for tap_index in range(KC):
        window = padded[tap_index : tap_index + length_t]
        same_doc = (seg_pad[tap_index : tap_index + length_t] == seg_one).astype(jnp.float32)
        total = total + kernel[tap_index][None, :] * window * same_doc[:, None]
    return total


def cumulative(step_size, rate):
    length_t = step_size.shape[0]
    lower = jnp.tril(jnp.ones((length_t, length_t), jnp.float32))
    return jnp.dot(lower, step_size * rate[None, :], precision=HIGHEST)


def block_state(inner, b_proj, step_size, rate, seg_one, previous):
    cum_decay = cumulative(step_size, rate)
    last_seg = seg_one[-1]
    to_end = (
        jnp.where((seg_one == last_seg)[:, None], jnp.exp(cum_decay[-1][None, :] - cum_decay), 0.0)
        * step_size
    )
    state_part = jnp.einsum("uhp,un->hpn", inner * to_end[:, :, None], b_proj, precision=HIGHEST)
    through = jnp.logical_and(seg_one[0] == last_seg, seg_one[0] == previous).astype(jnp.float32)
    return (state_part, jnp.exp(cum_decay[-1]) * through)


def block_output(inner, b_proj, c_proj, step_size, rate, state_in, seg_one, previous):
    cum_decay = cumulative(step_size, rate)
    length_t = seg_one.shape[0]
    row_index = lax.broadcasted_iota(jnp.int32, (length_t, length_t), 0)
    col_index = lax.broadcasted_iota(jnp.int32, (length_t, length_t), 1)
    allowed = jnp.logical_and(row_index >= col_index, seg_one[:, None] == seg_one[None, :])[
        :, :, None
    ]
    spread = cum_decay[:, None, :] - cum_decay[None, :, :]
    decays = jnp.where(allowed, jnp.exp(jnp.where(allowed, spread, 0.0)), 0.0)
    scores = jnp.dot(c_proj, b_proj.T, precision=HIGHEST)
    weights = decays * scores[:, :, None] * step_size[None, :, :]
    local_part = jnp.einsum("tuh,uhp->thp", weights, inner, precision=HIGHEST)
    carried = (seg_one == previous).astype(jnp.float32)[:, None] * jnp.exp(cum_decay)
    return local_part + carried[:, :, None] * jnp.einsum(
        "tn,hpn->thp", c_proj, state_in, precision=HIGHEST
    )


def prepare(proj_out, tail_rows, kernel, offset, step_bias, log_rate, tail_seg, seg_one):
    length_t = proj_out.shape[0]
    padded = jnp.concatenate([tail_rows, proj_out[:, DI : DI + CH]], axis=0)
    seg_pad = jnp.concatenate([tail_seg, seg_one])
    activated = jax.nn.silu(causal_conv(padded, seg_pad, seg_one, kernel, offset))
    inner = activated[:, :DI].reshape(length_t, H, P_SIZE)
    b_proj = activated[:, DI : DI + N]
    c_proj = activated[:, DI + N :]
    step_size = jax.nn.softplus(proj_out[:, DI + CH :] + step_bias[None, :])
    rate = -jnp.exp(log_rate)
    return (inner, b_proj, c_proj, step_size, rate, proj_out[:, :DI])


def finish(
    inner,
    b_proj,
    c_proj,
    step_size,
    rate,
    gate_in,
    state_in,
    skip_gain,
    gate_gain,
    seg_one,
    previous,
):
    length_t = inner.shape[0]
    mixed = block_output(inner, b_proj, c_proj, step_size, rate, state_in, seg_one, previous)
    mixed = mixed + skip_gain[None, :, None] * inner
    gated = mixed.reshape(length_t, DI) * jax.nn.silu(gate_in)
    return rms_scale(gated, gate_gain)


def chain_link(earlier, later):
    return (earlier[0] * later[0], later[0][:, None, None] * earlier[1] + later[1])


def body(
    tokens,
    cotangent,
    segments,
    norm_gain,
    w_in,
    conv_weight,
    conv_bias,
    step_bias,
    log_rate,
    skip_gain,
    gate_gain,
    w_out,
):
    batches = tokens.shape[0]
    length_t = tokens.shape[2]
    halo_rows = KC - 1
    identity = (jnp.ones((H,), jnp.float32), jnp.zeros((H, P_SIZE, N), jnp.float32))
    totals = None
    head_totals = (
        jnp.zeros((H,), jnp.float32),
        jnp.zeros((H,), jnp.float32),
        jnp.zeros((H,), jnp.float32),
    )
    act_list = []
    grad_list = []
    for micro in range(batches):
        gathered = (
            lax.all_gather(w_in, "seq", axis=0, tiled=True),
            lax.all_gather(w_out, "seq", axis=0, tiled=True),
            lax.all_gather(conv_weight, "seq", axis=1, tiled=True),
            lax.all_gather(conv_bias, "seq", axis=0, tiled=True),
            lax.all_gather(norm_gain, "seq", axis=0, tiled=True),
            lax.all_gather(gate_gain, "seq", axis=0, tiled=True),
        )
        in_full = gathered[0]
        out_full = gathered[1]
        kernel = gathered[2].astype(jnp.float32)
        offset = gathered[3].astype(jnp.float32)
        gain_one = gathered[4].astype(jnp.float32)
        gain_two = gathered[5].astype(jnp.float32)
        resid = tokens[micro, 0].astype(jnp.float32)
        seg_one = segments[micro, 0].astype(jnp.float32) + 1.0
        normed, norm_back = jax.vjp(rms_scale, resid, gain_one)
        normed_low = normed.astype(jnp.bfloat16)
        proj_out = jnp.dot(normed_low, in_full, preferred_element_type=jnp.float32)
        tail_rows, tail_seg = passed_along(
            (proj_out[length_t - halo_rows :, DI : DI + CH], seg_one[length_t - halo_rows :]),
            "seq",
            1,
        )
        previous = tail_seg[halo_rows - 1]
        prepared, prep_back = jax.vjp(
            partial(prepare, tail_seg=tail_seg, seg_one=seg_one),
            proj_out,
            tail_rows,
            kernel,
            offset,
            step_bias,
            log_rate,
        )
        inner, b_proj, c_proj, step_size, rate, gate_in = prepared
        state_out, state_back = jax.vjp(
            partial(block_state, seg_one=seg_one, previous=previous), inner, b_proj, step_size, rate
        )
        state_part, through = state_out
        state_in = prefix((through, state_part), "seq", chain_link, identity, False)[1]
        normed_two, finish_back = jax.vjp(
            partial(finish, seg_one=seg_one, previous=previous),
            inner,
            b_proj,
            c_proj,
            step_size,
            rate,
            gate_in,
            state_in,
            skip_gain,
            gain_two,
        )
        gate_low = normed_two.astype(jnp.bfloat16)
        branch = jnp.dot(gate_low, out_full, preferred_element_type=jnp.float32)
        act_list.append((resid + branch).astype(jnp.bfloat16))
        cot_low = cotangent[micro, 0]
        again = (
            lax.all_gather(w_in, "seq", axis=0, tiled=True),
            lax.all_gather(w_out, "seq", axis=0, tiled=True),
        )
        in_back = again[0]
        out_back = again[1]
        out_term = lax.dot_general(
            gate_low, cot_low, (((0,), (0,)), ((), ())), preferred_element_type=jnp.float32
        )
        grad_gate = lax.dot_general(
            cot_low, out_back, (((1,), (1,)), ((), ())), preferred_element_type=jnp.float32
        )
        g_inner, g_bproj, g_cproj, g_step, g_rate, g_gate_in, g_state_in, g_skip, g_gain_two = (
            finish_back(grad_gate)
        )
        carried = prefix((through, g_state_in), "seq", chain_link, identity, True)[1]
        h_inner, h_bproj, h_step, h_rate = state_back(
            (carried, jnp.sum(carried * state_in, axis=(1, 2)))
        )
        g_proj, g_tail, g_kernel, g_offset, g_bias, g_log = prep_back(
            (
                g_inner + h_inner,
                g_bproj + h_bproj,
                g_cproj,
                g_step + h_step,
                g_rate + h_rate,
                g_gate_in,
            )
        )
        returned = passed_along(g_tail, "seq", -1)
        width_after = proj_out.shape[1] - DI - CH
        g_proj = g_proj + jnp.pad(returned, ((length_t - halo_rows, 0), (DI, width_after)))
        proj_grad_low = g_proj.astype(jnp.bfloat16)
        grad_normed = lax.dot_general(
            proj_grad_low, in_back, (((1,), (1,)), ((), ())), preferred_element_type=jnp.float32
        )
        grad_resid, g_gain_one = norm_back(grad_normed)
        grad_list.append((cot_low.astype(jnp.float32) + grad_resid).astype(jnp.bfloat16))
        in_shard = lax.psum_scatter(
            lax.dot_general(
                normed_low,
                proj_grad_low,
                (((0,), (0,)), ((), ())),
                preferred_element_type=jnp.float32,
            ),
            "seq",
            scatter_dimension=0,
            tiled=True,
        )
        shards = (
            lax.psum_scatter(out_term, "seq", scatter_dimension=0, tiled=True),
            lax.psum_scatter(g_kernel, "seq", scatter_dimension=1, tiled=True),
            lax.psum_scatter(g_offset, "seq", scatter_dimension=0, tiled=True),
            lax.psum_scatter(g_gain_one, "seq", scatter_dimension=0, tiled=True),
            lax.psum_scatter(g_gain_two, "seq", scatter_dimension=0, tiled=True),
        )
        this_round = (in_shard, shards[0], shards[1], shards[2], shards[3], shards[4])
        if totals is None:
            totals = this_round
        else:
            totals = tuple((prior + fresh for prior, fresh in zip(totals, this_round)))
        head_totals = (head_totals[0] + g_bias, head_totals[1] + g_log, head_totals[2] + g_skip)
    summed = jax.tree.map(
        lambda part: part.astype(jnp.float32), lax.psum(for_sending(totals), "dp")
    )
    heads = lax.psum((head_totals[0], head_totals[1], head_totals[2]), ("dp", "seq"))
    activations = jnp.stack(act_list)[:, None]
    grad_tokens = jnp.stack(grad_list)[:, None]
    return (
        activations,
        grad_tokens,
        summed[4],
        summed[0],
        summed[2],
        summed[3],
        heads[0],
        heads[1],
        heads[2],
        summed[5],
        summed[1],
    )


MESH = pl.DeviceIdType.MESH


def chip(x, y, z):
    return z * 4 + y * 2 + x


def place():
    core = lax.axis_index("dp")
    at = lax.axis_index("seq")
    return at % 2, (at // 2) % 2, at // 4, core


def greet_all(planes):
    barrier = pltpu.get_barrier_semaphore()
    me = lax.axis_index("seq")
    core = lax.axis_index("dp")
    count = planes * 4

    def greet(k, carry):
        other = lax.rem(me + k, count)
        for far in range(2):

            @pl.when(jnp.logical_or(k > 0, far != core))
            def _():
                pl.semaphore_signal(barrier, inc=1, device_id=(far, other), device_id_type=MESH)

        return carry

    lax.fori_loop(0, count, greet, 0)


def meet_all(planes):
    pl.semaphore_wait(pltpu.get_barrier_semaphore(), 8 * planes - 1)


COLUMN, SIDE_X, SIDE_Y, HALF_X, HALF_Y, MATE_Z, MATE_X, MATE_Y, MATE_HX, MATE_HY = range(10)


class Gather:
    def __init__(self, whole, rows, quarter, sems, planes):
        self.whole, self.rows, self.quarter, self.sems, self.planes = whole, rows, quarter, sems, planes
        self.x, self.y, self.z, self.core = place()

    def region(self, block, core, part=None):
        width = self.whole.shape[1] // 2
        start = pl.multiple_of(block * self.rows, 16)
        left = pl.multiple_of(core * width, 128)
        if part is None:
            return self.whole.at[pl.ds(start, self.rows), pl.ds(left, width)]
        if self.quarter == "rows":
            half = self.rows // 2
            return self.whole.at[pl.ds(pl.multiple_of(start + part * half, 16), half), pl.ds(left, width)]
        half = width // 2
        return self.whole.at[pl.ds(start, self.rows), pl.ds(pl.multiple_of(left + part * half, 128), half)]

    def copy(self, kind, leaves, lands, block, core, part, device):
        region = self.region(block, core, part)
        return pltpu.make_async_remote_copy(
            src_ref=region,
            dst_ref=region,
            send_sem=self.sems.at[0, kind, leaves],
            recv_sem=self.sems.at[1, kind, lands],
            device_id=device,
            device_id_type=MESH,
        )

    def out(self, kind, far):
        x, y, z, c = self.x, self.y, self.z, self.core
        if kind == COLUMN:
            return self.copy(kind, far, z, chip(x, y, z), c, None, (c, chip(x, y, far)))
        own, by_x, by_y, across = chip(x, y, far), chip(1 - x, y, far), chip(x, 1 - y, far), chip(1 - x, 1 - y, far)
        mate = (1 - c, chip(x, y, z))
        to_x, to_y = (c, chip(1 - x, y, z)), (c, chip(x, 1 - y, z))
        block, part, device = {
            SIDE_X: (own, None, to_x),
            SIDE_Y: (own, None, to_y),
            HALF_X: (by_y, 1, to_x),
            HALF_Y: (by_x, 0, to_y),
            MATE_Z: (own, None, mate),
            MATE_X: (by_x, None, mate),
            MATE_Y: (by_y, None, mate),
            MATE_HX: (across, 1, mate),
            MATE_HY: (across, 0, mate),
        }[kind]
        return self.copy(kind, far, far, block, c, part, device)

    def send(self, kind, far):
        self.out(kind, far).start()

    def arrived(self, kind, far):
        x, y = self.x, self.y
        own, by_x, by_y, across = chip(x, y, far), chip(1 - x, y, far), chip(x, 1 - y, far), chip(1 - x, 1 - y, far)
        block, part, mine = {
            COLUMN: (own, None, True),
            SIDE_X: (by_x, None, True),
            SIDE_Y: (by_y, None, True),
            HALF_X: (across, 1, True),
            HALF_Y: (across, 0, True),
            MATE_Z: (own, None, False),
            MATE_X: (by_x, None, False),
            MATE_Y: (by_y, None, False),
            MATE_HX: (across, 1, False),
            MATE_HY: (across, 0, False),
        }[kind]
        core = self.core if mine else 1 - self.core
        self.copy(kind, far, far, block, core, part, (1 - self.core, chip(x, y, self.z))).wait_recv()

    def each(self, distance, act):
        for sign in (-1, 1) if distance else (1,):
            far = self.z + sign * distance
            if distance:
                pl.when(jnp.logical_and(far >= 0, far < self.planes))(functools.partial(act, far))
            else:
                act(far)

    def begin_sides(self):
        self.send(SIDE_X, self.z)
        self.send(SIDE_Y, self.z)

    def begin_column(self):
        for distance in range(1, self.planes):
            self.each(distance, lambda far: self.send(COLUMN, far))

    def begin(self):
        self.begin_sides()
        self.begin_column()

    def column(self, distance):
        def act(far):
            self.arrived(COLUMN, far)
            self.send(SIDE_X, far)
            self.send(SIDE_Y, far)
            self.send(MATE_Z, far)

        self.each(distance, act)

    def sides(self, distance):
        def act(far):
            self.arrived(SIDE_X, far)
            self.send(HALF_Y, far)
            self.send(MATE_X, far)
            self.arrived(SIDE_Y, far)
            self.send(HALF_X, far)
            self.send(MATE_Y, far)

        self.each(distance, act)

    def diagonal(self, distance):
        def act(far):
            self.arrived(HALF_Y, far)
            self.send(MATE_HY, far)
            self.arrived(HALF_X, far)
            self.send(MATE_HX, far)

        self.each(distance, act)

    def whole_here(self):
        for distance in range(self.planes):

            def act(far):
                for kind in (MATE_X, MATE_Y, MATE_HX, MATE_HY) + ((MATE_Z,) if distance else ()):
                    self.arrived(kind, far)

            self.each(distance, act)

    def finish(self):
        for distance in range(self.planes):

            def act(far):
                kinds = (SIDE_X, SIDE_Y, HALF_X, HALF_Y, MATE_X, MATE_Y, MATE_HX, MATE_HY)
                for kind in kinds + ((MATE_Z, COLUMN) if distance else ()):
                    self.out(kind, far).wait_send()

            self.each(distance, act)


def gather_sems(planes):
    return pltpu.SemaphoreType.DMA((2, 10, planes))


class Reduce:
    X, Y, HX, HY, COLUMN, MATE, LAST = range(7)

    @staticmethod
    def scratch(rows, width, quarter, planes):
        half = width // 2
        corner = (rows // 2, half) if quarter == "rows" else (rows, half // 2)
        bf16 = jnp.bfloat16
        return [
            pltpu.VMEM((4 * planes * rows, half), bf16),
            pltpu.VMEM((3, planes, rows, half), bf16),
            pltpu.VMEM((2, planes) + corner, bf16),
            pltpu.SemaphoreType.DMA((2, 7, planes)),
        ]

    def __init__(self, part, out, rows, quarter, scratch, planes):
        self.part, self.out, self.rows, self.quarter, self.planes = part, out, rows, quarter, planes
        self.mate_in, self.side_in, self.corner_in, self.sems = scratch
        self.x, self.y, self.z, self.core = place()
        self.half = part.shape[1] // 2

    def block(self, owner, part=None):
        start = pl.multiple_of(owner * self.rows, 16)
        left = pl.multiple_of(self.core * self.half, 128)
        if part is None:
            return pl.ds(start, self.rows), pl.ds(left, self.half)
        if self.quarter == "rows":
            return pl.ds(pl.multiple_of(start + part * (self.rows // 2), 16), self.rows // 2), pl.ds(left, self.half)
        quarter = self.half // 2
        return pl.ds(start, self.rows), pl.ds(pl.multiple_of(left + part * quarter, 128), quarter)

    def copy(self, kind, far, source, target, device):
        return pltpu.make_async_remote_copy(
            src_ref=source,
            dst_ref=target,
            send_sem=self.sems.at[0, kind, far],
            recv_sem=self.sems.at[1, kind, far],
            device_id=device,
            device_id_type=MESH,
        )

    def move(self, kind, far):
        x, y, z, c = self.x, self.y, self.z, self.core
        part = self.part
        to_x, to_y, mate = (c, chip(1 - x, y, z)), (c, chip(x, 1 - y, z)), (1 - c, chip(x, y, z))
        if kind == self.X:
            return self.copy(kind, far, part.at[self.block(chip(1 - x, y, far))], self.side_in.at[0, far], to_x)
        if kind == self.Y:
            return self.copy(kind, far, part.at[self.block(chip(x, 1 - y, far))], self.side_in.at[1, far], to_y)
        if kind == self.HX:
            return self.copy(kind, far, part.at[self.block(chip(1 - x, 1 - y, far), 0)], self.corner_in.at[0, far], to_x)
        if kind == self.HY:
            return self.copy(kind, far, part.at[self.block(chip(1 - x, 1 - y, far), 1)], self.corner_in.at[1, far], to_y)
        if kind == self.COLUMN:
            return pltpu.make_async_remote_copy(
                src_ref=part.at[self.block(chip(x, y, far))],
                dst_ref=self.side_in.at[2, z],
                send_sem=self.sems.at[0, kind, far],
                recv_sem=self.sems.at[1, kind, z],
                device_id=(c, chip(x, y, far)),
                device_id_type=MESH,
            )
        if kind == self.MATE:
            rows = pl.ds(pl.multiple_of(far * 4 * self.rows, 16), 4 * self.rows)
            left = pl.multiple_of((1 - c) * self.half, 128)
            return self.copy(kind, far, part.at[rows, pl.ds(left, self.half)], self.mate_in.at[rows], mate)
        left = pl.multiple_of(c * self.half, 128)
        region = self.out.at[:, pl.ds(left, self.half)]
        return self.copy(kind, 0, region, region, mate)

    def add(self, at, *refs):
        total = self.part[at].astype(jnp.float32)
        for ref in refs:
            total = total + ref[...].astype(jnp.float32)
        self.part[at] = low(total)

    def each(self, distance, act):
        for sign in (-1, 1) if distance else (1,):
            far = self.z + sign * distance
            if distance:
                pl.when(jnp.logical_and(far >= 0, far < self.planes))(functools.partial(act, far, sign))
            else:
                act(far, sign)

    def start(self, distance):
        self.each(distance, lambda far, sign: self.move(self.MATE, far).start())

    def fold(self, distance):
        def act(far, sign):
            self.move(self.MATE, far).wait_recv()

            def rows(k, carry):
                start = pl.multiple_of((far * 4 + k) * self.rows, 16)
                left = pl.multiple_of(self.core * self.half, 128)
                self.add((pl.ds(start, self.rows), pl.ds(left, self.half)), self.mate_in.at[pl.ds(start, self.rows)])
                return carry

            lax.fori_loop(0, 4, rows, 0)
            self.move(self.HX, far).start()
            self.move(self.HY, far).start()

        self.each(distance, act)

    def sides(self, distance):
        x, y = self.x, self.y

        def act(far, sign):
            self.move(self.HX, far).wait_recv()
            self.add(self.block(chip(x, 1 - y, far), 0), self.corner_in.at[0, far])
            self.move(self.Y, far).start()
            self.move(self.HY, far).wait_recv()
            self.add(self.block(chip(1 - x, y, far), 1), self.corner_in.at[1, far])
            self.move(self.X, far).start()

        self.each(distance, act)

    def column(self, distance):
        x, y, z = self.x, self.y, self.z

        def act(far, sign):
            self.move(self.X, far).wait_recv()
            self.move(self.Y, far).wait_recv()
            if distance:
                self.add(self.block(chip(x, y, far)), self.side_in.at[0, far], self.side_in.at[1, far])
                self.move(self.COLUMN, far).start()

        self.each(distance, act)

    def close(self):
        z = self.z
        at = self.block(chip(self.x, self.y, z))
        left = pl.multiple_of(self.core * self.half, 128)
        here = (slice(None), pl.ds(left, self.half))
        total = self.part[at].astype(jnp.float32)
        self.out[here] = total + self.side_in[0, z].astype(jnp.float32) + self.side_in[1, z].astype(jnp.float32)
        for distance in range(self.planes - 1, 0, -1):

            def act(far, sign):
                self.copy(self.COLUMN, far, self.side_in.at[2, far], self.side_in.at[2, far], (self.core, chip(self.x, self.y, far))).wait_recv()
                self.out[here] = self.out[here] + self.side_in[2, far].astype(jnp.float32)

            self.each(distance, act)
        self.move(self.LAST, 0).start()

    def finish(self):
        last = self.move(self.LAST, 0)
        left = pl.multiple_of((1 - self.core) * self.half, 128)
        region = self.out.at[:, pl.ds(left, self.half)]
        self.copy(self.LAST, 0, region, region, (1 - self.core, chip(self.x, self.y, self.z))).wait_recv()
        last.wait_send()

    def drain(self, kinds):
        for distance in range(self.planes):

            def act(far, sign):
                for kind in kinds:
                    if distance or kind != self.COLUMN:
                        self.move(kind, far).wait_send()

            self.each(distance, act)

    def drain_early(self):
        self.drain((self.MATE, self.HX, self.HY))

    def drain_late(self):
        self.drain((self.X, self.Y, self.COLUMN))


class Chain:
    CUT = 6

    @staticmethod
    def scratch():
        half = pltpu.VMEM((N, DI // 2), jnp.bfloat16)
        wide = pltpu.VMEM((N, DI // 2), jnp.float32)
        return [half, half, half, half, half, half, wide, wide, pltpu.SemaphoreType.DMA((2, 2 + Chain.CUT))]

    def __init__(self, part, result, factors, scratch, lead, planes):
        self.part, self.result, self.factors, self.lead, self.planes = part, result, factors, lead, planes
        self.give, self.take, self.leave, self.come, self.back, self.again, self.total, self.front, self.sems = scratch
        self.x, self.y, self.z, self.core = place()
        self.half = DI // 2
        self.leads = self.core == lead
        self.ahead = 1 if lead == 0 else -1
        self.first = self.z == (0 if lead == 0 else planes - 1)
        self.last = self.z == (planes - 1 if lead == 0 else 0)

    def own(self):
        return pl.ds(pl.multiple_of(self.core * self.half, 128), self.half)

    def other(self):
        return pl.ds(pl.multiple_of((1 - self.core) * self.half, 128), self.half)

    def copy(self, k, source, target, device):
        return pltpu.make_async_remote_copy(
            src_ref=source,
            dst_ref=target,
            send_sem=self.sems.at[0, k],
            recv_sem=self.sems.at[1, k],
            device_id=device,
            device_id_type=MESH,
        )

    def mate(self):
        return (1 - self.core, chip(self.x, self.y, self.z))

    def trade(self):
        return self.copy(0, self.give, self.take, self.mate())

    def returned(self):
        return self.copy(1, self.back, self.again, self.mate())

    def hop(self, k):
        cut = self.half // self.CUT
        at = (slice(None), pl.ds(k * cut, cut))
        return self.copy(
            2 + k, self.leave.at[at], self.come.at[at], (self.core, chip(self.x, self.y, self.z + self.ahead))
        )

    def start(self):
        self.give[...] = low(self.part[:, self.other()])
        self.trade().start()

    def rows(self):
        return self.factors[self.lead, 0:1, self.own()], self.factors[1 - self.lead, 0:1, self.own()]

    def merge(self):
        self.trade().wait_recv()
        own = self.part[:, self.own()]
        got = self.take[...].astype(jnp.float32)
        ahead, behind = jnp.where(self.leads, own, got), jnp.where(self.leads, got, own)
        _, following = self.rows()
        self.front[...] = ahead
        self.total[...] = following * ahead + behind

        @pl.when(self.first)
        def _():
            self.come[...] = jnp.zeros(self.come.shape, self.come.dtype)
            self.leave[...] = low(self.total[...])
            for k in range(self.CUT):
                self.hop(k).start()

    def pass_on(self):
        leading, following = self.rows()
        cut = self.half // self.CUT

        @pl.when(jnp.logical_not(self.first))
        def _():
            for k in range(self.CUT):
                self.hop(k).wait_recv()

                @pl.when(jnp.logical_not(self.last))
                def _():
                    at = (slice(None), slice(k * cut, (k + 1) * cut))
                    both = (leading * following)[:, k * cut : (k + 1) * cut]
                    self.leave[at] = low(both * self.come[at].astype(jnp.float32) + self.total[at])
                    self.hop(k).start()

        came = self.come[...].astype(jnp.float32)
        later = low(leading * came + self.front[...])
        self.back[...] = jnp.where(self.leads, later.astype(jnp.float32), came).astype(jnp.bfloat16)
        self.returned().start()
        self.result[:, self.own()] = jnp.where(self.leads, came, later.astype(jnp.float32)).astype(jnp.bfloat16)

    def close(self):
        self.returned().wait_recv()
        self.result[:, self.other()] = self.again[...]

    def finish(self):
        self.trade().wait_send()
        self.returned().wait_send()

        @pl.when(jnp.logical_not(self.last))
        def _():
            for k in range(self.CUT):
                self.hop(k).wait_send()


VMEM = pl.BlockSpec(memory_space=pltpu.VMEM)
ROWS = 256
HALO = 16
WIDE = 2048
TRANS = (((0,), (0,)), ((), ()))
TRANS_B = (((1,), (1,)), ((), ()))


def dot(a, b, dims=(((1,), (0,)), ((), ()))):
    return lax.dot_general(a, b, dims, preferred_element_type=jnp.float32)


def low(a):
    return a.astype(jnp.bfloat16)


class Shuffle:
    def __init__(self, source, target, sems, offset=0, back=False):
        self.source, self.target, self.sems, self.offset, self.back = source, target, sems, offset, back
        self.x, self.y, self.z, self.core = place()

    def piece(self, k):
        x, y, z, c = self.x, self.y, self.z, self.core
        rows = 128
        if self.back:
            source = self.source.at[pl.ds(rows * k, rows)]
            target = self.target.at[x]
        else:
            source = self.source.at[k]
            if len(self.target.shape) == len(self.source.shape):
                target = self.target.at[self.offset + x]
            else:
                target = self.target.at[pl.ds(pl.multiple_of(self.offset + rows * x, 16), rows)]
        stays = jnp.logical_and(x == k, y == c)
        local = pltpu.make_async_copy(source, target, self.sems.at[1, x])
        remote = pltpu.make_async_remote_copy(
            src_ref=source,
            dst_ref=target,
            send_sem=self.sems.at[0, k],
            recv_sem=self.sems.at[1, x],
            device_id=(y, chip(k, c, z)),
            device_id_type=MESH,
        )
        return stays, local, remote

    def start(self):
        for k in range(2):
            stays, local, remote = self.piece(k)
            pl.when(stays)(local.start)
            pl.when(jnp.logical_not(stays))(remote.start)

    def arrived(self):
        x, y, z, c = self.x, self.y, self.z, self.core
        for k in range(2):
            if self.back:
                target = self.target.at[k]
            elif len(self.target.shape) == len(self.source.shape):
                target = self.target.at[self.offset + k]
            else:
                target = self.target.at[pl.ds(self.offset + 128 * k, 128)]
            stays = jnp.logical_and(x == k, y == c)
            local = pltpu.make_async_copy(target, target, self.sems.at[1, k])
            remote = pltpu.make_async_remote_copy(
                src_ref=target,
                dst_ref=target,
                send_sem=self.sems.at[0, k],
                recv_sem=self.sems.at[1, k],
                device_id=(y, chip(k, c, z)),
                device_id_type=MESH,
            )
            pl.when(stays)(local.wait)
            pl.when(jnp.logical_not(stays))(remote.wait_recv)

    def finish(self):
        for k in range(2):
            stays, local, remote = self.piece(k)
            pl.when(jnp.logical_not(stays))(remote.wait_send)


class Before:
    def __init__(self, source, target, sems, planes):
        self.source, self.target, self.sems, self.planes = source, target, sems, planes
        self.x, self.y, self.z, self.core = place()

    def piece(self, m):
        x, y, z, c = self.x, self.y, self.z, self.core
        source = self.source(m)
        return pltpu.make_async_remote_copy(
            src_ref=source,
            dst_ref=self.target,
            send_sem=self.sems.at[0, m],
            recv_sem=self.sems.at[1, 0],
            device_id=(1 - y, chip(m, c, z + y)),
            device_id_type=MESH,
        )

    def when_sending(self):
        return jnp.logical_and(self.x == 1, jnp.logical_or(self.y == 0, self.z < self.planes - 1))

    def start(self):
        @pl.when(self.when_sending())
        def _():
            for m in range(2):
                self.piece(m).start()

    def arrived(self):
        pl.when(self.z + self.core > 0)(self.piece(0).wait_recv)

    def finish(self):
        @pl.when(self.when_sending())
        def _():
            for m in range(2):
                self.piece(m).wait_send()


class ToAll:
    def __init__(self, table, sems, planes):
        self.table, self.sems, self.count = table, sems, planes * 4
        self.me, self.core = lax.axis_index("seq"), lax.axis_index("dp")

    def copy(self, block, other):
        return pltpu.make_async_remote_copy(
            src_ref=self.table.at[block],
            dst_ref=self.table.at[block],
            send_sem=self.sems.at[0, other],
            recv_sem=self.sems.at[1, block],
            device_id=(self.core, other),
            device_id_type=MESH,
        )

    def over(self, act):
        def one(k, carry):
            act(lax.rem(self.me + k, self.count))
            return carry

        lax.fori_loop(1, self.count, one, 0)

    def start(self):
        self.over(lambda other: self.copy(self.me, other).start())

    def arrived(self):
        self.over(lambda other: self.copy(other, self.me).wait_recv())

    def finish(self):
        self.over(lambda other: self.copy(self.me, other).wait_send())


TILE = 128
TILES = DI // TILE


class Names:
    def __init__(self, names, refs):
        for name, ref in zip(names, refs, strict=True):
            setattr(self, name, ref)


def at_tile(j):
    return pl.ds(pl.multiple_of(j * TILE, TILE), TILE)


def at_rows(k, rows):
    return pl.ds(pl.multiple_of(k * rows, rows), rows)


def loop(low_end, high_end, act):
    count = high_end - low_end
    width = next(w for w in (4, 3, 2, 1) if count % w == 0)

    def several(k, carry):
        for i in range(width):
            act(low_end + width * k + i)
        return carry

    lax.fori_loop(0, count // width, several, 0)


def iota(shape, dim):
    return lax.broadcasted_iota(jnp.int32, shape, dim)


def pieces(a):
    high = low(a)
    rest = a - high.astype(jnp.float32)
    middle = low(rest)
    return high, middle, low(rest - middle.astype(jnp.float32))


def packed(a):
    a = jnp.where(iota(a.shape, 1) < H, a, 0.0)
    high, middle, rest = (part.astype(jnp.float32) for part in pieces(a))
    return low(high + pltpu.roll(middle, 32, 1) + pltpu.roll(rest, 64, 1))


def spread_matrix(width, first=0):
    row, col = iota((128, width), 0), iota((128, width), 1) + first
    return low(jnp.where(jnp.logical_and(row % 32 == col // P_SIZE, row < 96), 1.0, 0.0))


def head_sums(a, j):
    row, col = iota((TILE, 128), 0), iota((TILE, 128), 1)
    pick = low(jnp.where(row // P_SIZE + 2 * j == col, 1.0, 0.0))
    high, middle, _ = pieces(a)
    return dot(jnp.concatenate([high, middle], axis=1), jnp.concatenate([pick, pick], axis=0))


def sigmoid(v):
    return 1.0 / (1.0 + jnp.exp(-v))


GIVEN = ["tok_in", "cot", "seg_in", "small_in", "w_in", "wout"]
MADE = ["act_out", "tokens_out", "grad_a", "grad_z", "grad_out", "small_out"]


def block_scratch(planes):
    f32, bf16 = jnp.float32, jnp.bfloat16
    v = pltpu.VMEM
    dma = pltpu.SemaphoreType.DMA
    two = dma((2, 2))
    return {
        "wa": v((768, WIDE), bf16), "wa_sem": gather_sems(planes), "tok": v((HALO + ROWS, 768), bf16), "seg": v((3, 8, 128), f32),
        "normed": v((HALO + ROWS, 768), bf16), "proj": v((HALO + ROWS, WIDE), f32), "conv": v((8, CH), f32), "gain": v((8, DI), f32),
        "ngain": v((8, 768), f32), "ngrad": v((8, 768), f32), "scale": v((ROWS, 128), f32), "given": v((16, 8, 128), f32), "numbers": v((2, 8, 128), f32),
        "tok_sem": two, "end_sem": two, "seg_sem": two, "segend_sem": two, "given_sem": dma((2, 16)),
        "wz_full": v((768, DI), bf16), "wout_full": v((DI, 768), bf16), "wz_sem": gather_sems(planes), "wout_sem": gather_sems(planes),
        "cot_own": v((ROWS, 768), bf16), "cot_sem": two, "act_sem": two, "back_sem": two,
        "segcol": v((384, 128), f32), "same": v((KC - 1, ROWS, 128), f32),
        "pre": v((ROWS, CH), f32), "inner": v((ROWS, DI), f32), "bproj": v((ROWS, N), bf16), "cproj": v((ROWS, N), bf16),
        "cumt": v((H, 8, ROWS), f32), "bar": v((ROWS, ROWS), f32), "scores": v((ROWS, ROWS), f32),
        "step": v((ROWS, 128), f32), "ein": v((ROWS, 128), f32), "eout": v((ROWS, 128), f32),
        "stepx": v((ROWS, DI), f32), "einx": v((ROWS, DI), f32), "eoutx": v((ROWS, DI), f32), "cumx": v((ROWS, DI), f32),
        "xs": v((ROWS, DI), bf16), "xso": v((ROWS, DI), bf16),
        "part": v((N, DI), f32), "factors": v((2, 8, DI), f32), "factor_sem": dma((2,)), "skipx": v((8, DI), f32),
        "state": v((N, DI), bf16), "dstate": v((N, DI), bf16),
        "y": v((ROWS, DI), f32), "z": v((ROWS, DI), f32), "gated": v((ROWS, DI), bf16), "act_own": v((ROWS, 768), bf16),
        "dz": v((ROWS, DI), bf16), "dy": v((ROWS, DI), bf16), "dyin": v((ROWS, DI), bf16),
        "ggain": v((8, DI), f32), "gskip": v((8, DI), f32),
        "dscores": v((ROWS, ROWS), f32), "dxs": v((ROWS, DI), f32), "sums": v((3, ROWS, 128), f32),
        "dpre": v((KC, ROWS + HALO, TILE), f32), "late": v((8, CH), f32), "dx": v((HALO + ROWS, WIDE), bf16), "tail": v((8, CH), f32), "tail_in": v((8, CH), f32), "tail_sem": dma((2,)),
        "gconv": v((8, CH), f32), "gtok": v((ROWS, 768), bf16),
        "table": v((16, 8, 128), f32), "inbox": v((2, 16, 8, 128), f32), "table_sem": dma((2, 2, 16)),
        "part_a": v((2, 768, WIDE // 2), bf16), "part_z": v((768, DI), bf16), "part_out": v((DI, 768), bf16),
    }


def block_kernel(planes, names, *refs):
    r = Names(GIVEN + MADE + names, refs[: len(GIVEN) + len(MADE) + len(names)])
    extra = list(refs[len(GIVEN) + len(MADE) + len(names) :])
    chain_f, chain_b = extra[0:9], extra[9:15] + extra[6:8] + extra[15:16]
    red_a, red_b, red_z, red_out = extra[16:20], extra[20:24], extra[24:28], extra[28:32]
    x, y, z, c = place()
    me = chip(x, y, z)
    mate = (1 - c, me)
    f32 = jnp.float32
    greet_all(planes)
    r.wa[pl.ds(pl.multiple_of(me * 48, 16), 48), 0:CH] = r.w_in[:, DI : DI + CH]
    step_columns = r.w_in[:, DI + CH :]
    fill = jnp.zeros((48, WIDE - CH - H), step_columns.dtype)
    r.wa[pl.ds(pl.multiple_of(me * 48, 16), 48), CH:] = jnp.concatenate([step_columns, fill], axis=1)
    r.wz_full[pl.ds(pl.multiple_of(me * 48, 16), 48), :] = r.w_in[:, 0:DI]
    r.wout_full[pl.ds(pl.multiple_of(me * 96, 16), 96), :] = r.wout[...]
    r.given[me] = r.small_in[0:8, :]
    for m in range(2):
        r.numbers[m] = jnp.broadcast_to(r.seg_in[m : m + 1, :].astype(f32) + 1.0, (8, 128))

    @pl.when(z + c == 0)
    def _():
        r.tok[0:HALO, :] = jnp.zeros((HALO, 768), r.tok.dtype)
        r.seg[0] = jnp.full((8, 128), -1.0, f32)

    gather_a = Gather(r.wa, 48, "columns", r.wa_sem, planes)
    gather_z = Gather(r.wz_full, 48, "columns", r.wz_sem, planes)
    gather_out = Gather(r.wout_full, 96, "rows", r.wout_sem, planes)
    cots = Shuffle(r.cot, r.cot_own, r.cot_sem)
    moves = [
        Shuffle(r.tok_in, r.tok, r.tok_sem, HALO),
        Before(lambda m: r.tok_in.at[m, pl.ds(128 - HALO, HALO)], r.tok.at[pl.ds(0, HALO)], r.end_sem, planes),
        Shuffle(r.numbers, r.seg, r.seg_sem, 1),
        Before(lambda m: r.numbers.at[m], r.seg.at[0], r.segend_sem, planes),
        ToAll(r.given, r.given_sem, planes),
    ]
    meet_all(planes)
    for item in moves:
        item.start()
    gather_a.begin()
    gather_a.column(1)
    gather_a.sides(0)
    for item in moves:
        item.arrived()
    r.conv[...] = jnp.concatenate([r.given[k, :, 0:112] for k in range(16)], axis=1)
    r.gain[...] = jnp.concatenate([r.given[k, :, 0:96] for k in range(16)], axis=1)
    r.ngain[...] = jnp.concatenate([r.given[k, :, 0:48] for k in range(16)], axis=1)
    gather_a.column(2)
    gather_a.column(3)
    gather_a.sides(1)
    gather_a.diagonal(0)
    u = r.tok[...].astype(f32)
    r.normed[...] = low(u * lax.rsqrt(jnp.mean(u * u, axis=-1, keepdims=True) + EPSILON) * r.ngain[5:6, :])
    gather_z.begin_column()
    gather_a.sides(2)
    gather_a.diagonal(1)

    for k in range(3):
        r.segcol[128 * k : 128 * k + 128, :] = jnp.transpose(jnp.broadcast_to(r.seg[k, 0:1, :], (128, 128)))
    seg = r.segcol[128:384, :]
    for k in range(KC - 1):
        r.same[k] = jnp.where(r.segcol[125 + k : 125 + k + ROWS, :] == seg, 1.0, 0.0)
    gather_a.sides(3)
    gather_z.begin_sides()
    gather_a.diagonal(2)
    for d in range(1, planes):
        gather_z.column(d)
    cots.start()
    gather_out.begin()
    gather_a.diagonal(3)
    gather_a.whole_here()

    def project(k):
        at_k = pl.ds(pl.multiple_of(k * 512, 512), 512)
        r.proj[:, at_k] = dot(r.normed[...], r.wa[:, at_k])

    project(WIDE // 512 - 1)

    def convolve(j):
        at = at_tile(j)
        total = jnp.broadcast_to(r.conv[4:5, at], (ROWS, TILE))
        for k in range(KC):
            term = r.conv[k : k + 1, at] * r.proj[13 + k : 13 + k + ROWS, at]
            total = total + (term if k == KC - 1 else term * r.same[k])
        r.pre[:, at] = total
        return total * sigmoid(total)

    r.bproj[...] = low(convolve(TILES))
    r.cproj[...] = low(convolve(TILES + 1))

    raw = r.proj[HALO:, CH : CH + 128] + r.small_in[8:9, :]
    step = jnp.maximum(raw, 0.0) + jnp.log1p(jnp.exp(-jnp.abs(raw)))
    rate = -jnp.exp(r.small_in[9:10, :])
    lower = jnp.where(iota((ROWS, ROWS), 0) >= iota((ROWS, ROWS), 1), 1.0, 0.0)
    cum = jnp.dot(lower, step * rate, precision=HIGHEST, preferred_element_type=f32)
    r.step[...] = step
    across = jnp.transpose(cum)
    for h in range(H):
        r.cumt[h] = jnp.broadcast_to(across[h : h + 1, :], (8, ROWS))
    last = cum[ROWS - 1 : ROWS, :]
    before = r.segcol[127:128, :]
    first_seg, last_seg = seg[0:1, :], seg[ROWS - 1 : ROWS, :]
    r.ein[...] = jnp.where(seg == before, jnp.exp(cum), 0.0)
    r.eout[...] = jnp.where(seg == last_seg, jnp.exp(last - cum), 0.0)
    through = jnp.logical_and(first_seg == last_seg, first_seg == before)
    factor = jnp.where(through, jnp.exp(last), 0.0)
    segrow = jnp.concatenate([r.seg[1, 0:1, :], r.seg[2, 0:1, :]], axis=1)
    allowed = jnp.logical_and(jnp.concatenate([seg, seg], axis=1) == segrow, iota((ROWS, ROWS), 0) >= iota((ROWS, ROWS), 1))
    r.bar[...] = jnp.where(allowed, 0.0, -1e30)
    rows = packed(jnp.concatenate([jnp.broadcast_to(factor, (8, 128)), jnp.broadcast_to(r.small_in[10:11, :], (8, 128))], axis=0))
    both = dot(rows, spread_matrix(DI))
    r.factors[c] = both[0:8, :]
    r.skipx[...] = both[8:16, :]
    share = pltpu.make_async_remote_copy(
        src_ref=r.factors.at[c], dst_ref=r.factors.at[c], send_sem=r.factor_sem.at[0], recv_sem=r.factor_sem.at[1],
        device_id=mate, device_id_type=MESH,
    )
    share.start()
    spreads = [(r.stepx, packed(step)), (r.einx, packed(r.ein[...])), (r.eoutx, packed(r.eout[...])), (r.cumx, packed(cum))]
    r.stepx[...] = dot(spreads[0][1], spread_matrix(DI))
    r.eoutx[...] = dot(spreads[2][1], spread_matrix(DI))
    loop(0, WIDE // 512 - 1, project)

    def trade_order(k):
        return lax.rem(k + TILES // 2 * (1 - c), TILES)

    def outgoing(k):
        j = trade_order(k)
        at = at_tile(j)
        inner = convolve(j)
        r.inner[:, at] = inner
        scaled = r.stepx[:, at] * inner
        r.xs[:, at] = low(scaled)
        xso = low(scaled * r.eoutx[:, at])
        r.xso[:, at] = xso
        r.part[:, at] = dot(r.bproj[...], xso, TRANS)

    loop(0, TILES // 2, outgoing)
    forward = Chain(r.part, r.state, r.factors, chain_f, 0, planes)
    forward.start()
    loop(TILES // 2, TILES, outgoing)
    share.wait_recv()
    forward.merge()
    r.scores[...] = dot(r.cproj[...], r.bproj[...], TRANS_B)
    r.einx[...] = dot(spreads[1][1], spread_matrix(DI))
    r.cumx[...] = dot(spreads[3][1], spread_matrix(DI))
    gather_z.sides(0)
    for d in range(1, planes):
        gather_out.column(d)

    first_half = iota((1, TILE), 1) < P_SIZE

    def decays(j, band):
        size = 128 * (band + 1)
        rows = slice(128 * band, 128 * band + 128)
        tile = r.cumx[rows, at_tile(j)]
        turned = pltpu.roll(tile, P_SIZE, 1)
        out = []
        for k in range(2):
            column = jnp.where(first_half, tile, turned) if k == 0 else jnp.where(first_half, turned, tile)
            wide = column if band == 0 else jnp.concatenate([column, column], axis=1)
            out.append(jnp.exp(wide - r.cumt[2 * j + k, 0:1, 0:size] + r.bar[rows, 0:size]))
        return out

    def halves(tile):
        zero = jnp.zeros_like(tile)
        return jnp.where(first_half, tile, zero), jnp.where(first_half, zero, tile)

    def within(j):
        at = at_tile(j)
        for band in range(2):
            size = 128 * (band + 1)
            rows = slice(128 * band, 128 * band + 128)
            inside = halves(r.xs[0:size, at])
            total = 0.0
            for decay, xs in zip(decays(j, band), inside):
                total = total + dot(low(decay * r.scores[rows, 0:size]), xs)
            r.y[rows, at] = total

    def turn(chain, when):
        for k in range(planes):
            if when[k]:
                position = k if chain.lead == 0 else planes - 1 - k
                pl.when(z == position)(chain.pass_on)

    turn(forward, [1, 0, 0, 0])
    loop(0, 4, within)
    turn(forward, [0, 1, 0, 0])
    gather_z.sides(1)
    gather_z.diagonal(0)
    gather_out.sides(0)
    loop(4, 8, within)
    turn(forward, [0, 0, 1, 0])
    gather_z.sides(2)
    gather_z.diagonal(1)
    gather_out.sides(1)
    gather_out.diagonal(0)
    loop(8, 12, within)
    gather_z.sides(3)
    gather_z.diagonal(2)
    for item in moves + [gather_a]:
        item.finish()
    turn(forward, [0, 0, 0, 1])
    gather_out.sides(2)
    gather_out.diagonal(1)
    gather_z.diagonal(3)
    forward.close()

    def carried(j):
        at = at_tile(j)
        r.y[:, at] = r.y[:, at] + r.einx[:, at] * dot(r.cproj[...], r.state[:, at])

    loop(0, TILES, carried)
    gather_z.whole_here()

    def project_z(j):
        at = at_rows(j, 512)
        r.z[:, at] = dot(r.normed[HALO:, :], r.wz_full[:, at])

    loop(0, 3, project_z)
    gather_out.sides(3)
    gather_out.diagonal(2)

    def gated_values(rows):
        gate_in = r.z[rows, :]
        sig = sigmoid(gate_in)
        mixed = r.y[rows, :] + r.skipx[0:1, :] * r.inner[rows, :]
        return gate_in, sig, mixed, mixed * (gate_in * sig)

    def gate(k):
        rows = at_rows(k, 16)
        _, _, _, v = gated_values(rows)
        scale = lax.rsqrt(jnp.mean(v * v, axis=-1, keepdims=True) + EPSILON)
        r.scale[rows, :] = jnp.broadcast_to(scale, (16, 128))
        r.gated[rows, :] = low(v * scale * r.gain[6:7, :])

    loop(0, ROWS // 16, gate)
    gather_out.diagonal(3)
    gather_out.whole_here()
    cots.arrived()

    def project_cot(j):
        at = at_rows(j, 512)
        r.dxs[:, at] = dot(r.cot_own[...], r.wout_full[at, :], TRANS_B)

    loop(0, 3, project_cot)
    r.ggain[...] = jnp.zeros((8, DI), f32)
    r.gskip[...] = jnp.zeros((8, DI), f32)

    def gate_back(k):
        rows = at_rows(k, 32)
        gate_in, sig, mixed, v = gated_values(rows)
        scale = r.scale[rows, 0:1]
        dgated = r.dxs[rows, :]
        weighed = dgated * (v * scale)
        r.ggain[...] = r.ggain[...] + weighed[0:8, :] + weighed[8:16, :] + weighed[16:24, :] + weighed[24:32, :]
        a = r.gain[6:7, :] * dgated
        dv = scale * (a - v * (scale * scale) * jnp.mean(v * a, axis=-1, keepdims=True))
        dmixed = dv * (gate_in * sig)
        r.z[rows, :] = dmixed
        r.dy[rows, :] = low(dmixed)
        r.dyin[rows, :] = low(dmixed * r.einx[rows, :])
        r.dz[rows, :] = low(dv * mixed * (sig * (1.0 + gate_in * (1.0 - sig))))
        skip = dmixed * r.inner[rows, :]
        r.gskip[...] = r.gskip[...] + skip[0:8, :] + skip[8:16, :] + skip[16:24, :] + skip[24:32, :]

    loop(0, ROWS // 32, gate_back)

    def incoming(j):
        at = at_tile(j)
        r.part[:, at] = dot(r.cproj[...], r.dyin[:, at], TRANS)

    loop(0, TILES // 2, lambda k: incoming(trade_order(k)))
    backward = Chain(r.part, r.dstate, r.factors, chain_b, 1, planes)
    backward.start()
    loop(TILES // 2, TILES, lambda k: incoming(trade_order(k)))
    reduce_out = Reduce(r.part_out, r.grad_out, 96, "rows", red_out, planes)
    reduce_z = Reduce(r.part_z, r.grad_z, 48, "columns", red_z, planes)
    every = range(planes - 1, -1, -1)

    def project_out(k):
        at = at_rows(k, 256)
        r.act_own[:, at] = low(r.tok[HALO:, at].astype(f32) + dot(r.gated[...], r.wout_full[:, at]))

    loop(0, 3, project_out)
    acts = Shuffle(r.act_own, r.act_out, r.act_sem, back=True)
    acts.start()

    def weights_out(k):
        far = lax.rem(z + 1 + k, planes)
        at = pl.ds(pl.multiple_of(far * (DI // planes), 128), DI // planes)
        r.part_out[at, :] = low(dot(r.gated[:, at], r.cot_own[...], TRANS))
        reduce_out.move(reduce_out.MATE, far).start()

    loop(0, 2, weights_out)
    backward.merge()
    turn(backward, [1, 0, 0, 0])
    loop(2, planes, weights_out)

    def weights_z(k):
        half = lax.rem(k // 3 + 1 + c, 2)
        at = pl.ds(pl.multiple_of(half * (DI // 2) + k % 3 * 256, 256), 256)
        r.part_z[:, at] = low(dot(r.normed[HALO:, :], r.dz[:, at], TRANS))

    loop(0, 3, weights_z)
    for d in every:
        reduce_z.start(d)
    for d in every:
        reduce_out.fold(d)
    turn(backward, [0, 1, 0, 0])
    loop(3, 6, weights_z)
    for d in every:
        reduce_z.fold(d)

    def back_z(k):
        at = at_rows(k, 256)
        r.einx[:, at] = dot(r.dz[...], r.wz_full[at, :], TRANS_B)

    loop(0, 3, back_z)

    def reduce_sides(d):
        reduce_out.sides(d)
        reduce_z.sides(d)

    def reduce_column(d):
        reduce_out.column(d)
        reduce_z.column(d)

    r.dscores[...] = jnp.zeros((ROWS, ROWS), f32)
    r.sums[...] = jnp.zeros((3, ROWS, 128), f32)

    def within_back(j):
        at = at_tile(j)
        upper = lower = 0.0
        for band in range(2):
            size = 128 * (band + 1)
            rows = slice(128 * band, 128 * band + 128)
            xs = r.xs[0:size, at]
            grads = 0.0
            for decay, dy in zip(decays(j, band), halves(r.dy[rows, at])):
                weight = low(decay * r.scores[rows, 0:size])
                grads = grads + decay * dot(dy, xs, TRANS_B)
                upper = upper + dot(weight[:, 0:128], dy, TRANS)
                if band:
                    lower = lower + dot(weight[:, 128:256], dy, TRANS)
            r.dscores[rows, 0:size] = r.dscores[rows, 0:size] + grads
        r.dxs[0:128, at] = upper
        r.dxs[128:256, at] = lower
        gain = r.dy[:, at].astype(f32) * r.y[:, at] - r.xs[:, at].astype(f32) * r.dxs[:, at]
        r.sums[0] = r.sums[0] + head_sums(gain, j)
        inside = r.dxs[:, at]
        r.sums[2] = r.sums[2] + head_sums(r.inner[:, at] * inside, j)
        r.dxs[:, at] = r.skipx[0:1, at] * r.z[:, at] + r.stepx[:, at] * inside

    loop(0, 2, within_back)
    turn(backward, [0, 0, 1, 0])
    reduce_sides(3)
    loop(2, 5, within_back)
    reduce_sides(2)
    reduce_column(3)
    loop(5, 8, within_back)
    reduce_sides(1)
    reduce_column(2)
    turn(backward, [0, 0, 0, 1])
    loop(8, 12, within_back)
    for item in (gather_z, gather_out, cots, forward):
        item.finish()
    share.wait_send()
    backward.close()
    reduce_sides(0)

    def last_sums(j):
        at = at_tile(j)
        far = r.eoutx[:, at] * dot(r.bproj[...], r.dstate[:, at])
        r.sums[1] = r.sums[1] + head_sums(r.inner[:, at] * far, j)
        return r.dxs[:, at] + r.stepx[:, at] * far

    def unconvolve(j, grad):
        at = at_tile(j)
        pre = r.pre[:, at]
        sig = sigmoid(pre)
        grad = grad * (sig * (1.0 + pre * (1.0 - sig)))
        taps = []
        for k in range(KC):
            kept = grad if k == KC - 1 else grad * r.same[k]
            r.dpre[k, 8 : 8 + ROWS, :] = kept
            taps.append(jnp.sum(kept * r.proj[13 + k : 13 + k + ROWS, at], axis=0, keepdims=True))
        taps += [jnp.sum(grad, axis=0, keepdims=True), jnp.zeros((3, TILE), f32)]
        r.gconv[:, at] = jnp.concatenate(taps, axis=0)
        total = 0.0
        for k in range(KC):
            total = total + r.conv[k : k + 1, at] * r.dpre[k, 3 - k : 3 - k + 8 + ROWS, :]
        r.tail[:, at] = total[0:8, :]
        r.dx[0:HALO, at] = low(jnp.concatenate([jnp.zeros((8, TILE), f32), total[0:8, :]], axis=0))
        r.dx[HALO:, at] = low(total[8:, :])
        r.late[:, at] = total[ROWS : ROWS + 8, :]

    reduce_first = Reduce(r.part_a.at[0], r.grad_a.at[0], 48, "columns", red_a, planes)
    reduce_second = Reduce(r.part_a.at[1], r.grad_a.at[1], 48, "columns", red_b, planes)

    def weights_a(group, k):
        half = lax.rem(k + 1 + c, 2)
        at = pl.ds(pl.multiple_of(half * (WIDE // 4), 512), 512)
        from_ = pl.ds(pl.multiple_of(group * (WIDE // 2) + half * (WIDE // 4), 512), 512)
        r.part_a[group, :, at] = low(dot(r.normed[...], r.dx[:, from_], TRANS))

    def columns_back(j):
        unconvolve(j, last_sums(j))

    r.dx[0:HALO, CH:] = jnp.zeros((HALO, WIDE - CH), jnp.bfloat16)
    r.dx[HALO:, CH + 128 :] = jnp.zeros((ROWS, WIDE - CH - 128), jnp.bfloat16)
    r.dpre[...] = jnp.zeros((KC, ROWS + HALO, TILE), f32)
    loop(0, 8, columns_back)
    weights_a(0, 0)
    for d in every:
        reduce_first.start(d)
    weights_a(0, 1)
    reduce_column(1)
    loop(8, 12, columns_back)
    for d in every:
        reduce_first.fold(d)
    dscores = low(r.dscores[...])
    dbproj = dot(dscores, r.cproj[...], TRANS) + dot(r.xso[...], r.dstate[...], TRANS_B)
    dcproj = dot(dscores, r.bproj[...]) + dot(r.dyin[...], r.state[...], TRANS_B)
    pick = jnp.where(iota((DI, 128), 0) // P_SIZE == iota((DI, 128), 1), 1.0, 0.0)
    crossing = jnp.sum(r.dstate[...].astype(f32) * r.state[...].astype(f32), axis=0, keepdims=True) * r.factors[c, 0:1, :]
    rows = jnp.concatenate([jnp.broadcast_to(crossing, (8, DI)), r.gskip[...]], axis=0)
    rows = jnp.dot(rows, pick, precision=HIGHEST, preferred_element_type=f32)
    at_end, gskip = rows[0:1, :], jnp.sum(rows[8:16, :], axis=0, keepdims=True)
    upper = jnp.where(iota((ROWS, ROWS), 0) <= iota((ROWS, ROWS), 1), 1.0, 0.0)
    strict = jnp.where(iota((ROWS, ROWS), 0) > iota((ROWS, ROWS), 1), 1.0, 0.0)
    dlog = (
        jnp.dot(upper, r.sums[0], precision=HIGHEST, preferred_element_type=f32)
        + jnp.dot(strict, r.step[...] * r.sums[1], precision=HIGHEST, preferred_element_type=f32)
        + at_end
    )
    step = r.step[...]
    dstep = r.sums[1] + r.sums[2] + rate * dlog
    draw = dstep * sigmoid(r.proj[HALO:, CH : CH + 128] + r.small_in[8:9, :])
    lanes = iota((1, 128), 1) < H
    draw = jnp.where(lanes, draw, 0.0)
    gbias = jnp.sum(draw, axis=0, keepdims=True)
    glog = jnp.where(lanes, jnp.sum(step * dlog, axis=0, keepdims=True) * rate, 0.0)
    r.dx[HALO:, CH : CH + 128] = low(draw)
    unconvolve(TILES, dbproj)
    unconvolve(TILES + 1, dcproj)
    tails = [
        pltpu.make_async_remote_copy(
            src_ref=r.tail, dst_ref=r.tail_in, send_sem=r.tail_sem.at[0], recv_sem=r.tail_sem.at[1],
            device_id=(1 - c, chip(x, y, z - 1 + c)), device_id_type=MESH,
        )
    ]
    pl.when(z + c > 0)(tails[0].start)

    @pl.when(z + c == planes)
    def _():
        r.tail_in[...] = jnp.zeros((8, CH), f32)

    weights_a(1, 0)
    for d in every:
        reduce_second.start(d)
    weights_a(1, 1)
    reduce_first.sides(3)
    reduce_column(0)
    for d in every:
        reduce_second.fold(d)
    reduce_first.sides(2)
    reduce_out.close()
    reduce_z.close()
    pl.when(z + c < planes)(tails[0].wait_recv)
    r.dx[HALO + ROWS - 16 :, 0:CH] = low(
        jnp.concatenate([r.dx[HALO + ROWS - 16 : HALO + ROWS - 8, 0:CH].astype(f32), r.late[...] + r.tail_in[...]], axis=0)
    )

    def back_in(k):
        at = at_rows(k, 256)
        r.y[:, at] = r.einx[:, at] + dot(r.dx[HALO:, :], r.wa[at, :], TRANS_B)

    loop(0, 3, back_in)
    reduce_first.sides(1)
    reduce_first.column(3)
    reduce_second.sides(3)
    r.ngrad[...] = jnp.zeros((8, 768), f32)

    def norm_back(k):
        rows = at_rows(k, 16)
        dnormed = r.y[rows, 0:768]
        u = r.tok[pl.ds(pl.multiple_of(HALO + 16 * k, 16), 16), :].astype(f32)
        scale = lax.rsqrt(jnp.mean(u * u, axis=-1, keepdims=True) + EPSILON)
        weighed = dnormed * u * scale
        r.ngrad[...] = r.ngrad[...] + weighed[0:8] + weighed[8:16]
        a = r.ngain[5:6, :] * dnormed
        grad = scale * (a - u * (scale * scale) * jnp.mean(u * a, axis=-1, keepdims=True))
        r.gtok[rows, :] = low(r.cot_own[rows, :].astype(f32) + grad)

    loop(0, 8, norm_back)
    reduce_first.sides(0)
    reduce_first.column(2)
    reduce_second.sides(2)
    reduce_second.column(3)
    loop(8, 16, norm_back)
    grads = Shuffle(r.gtok, r.tokens_out, r.back_sem, back=True)
    grads.start()
    reduce_first.column(1)
    reduce_second.sides(1)
    reduce_second.column(2)
    ngain = jnp.sum(r.ngrad[...], axis=0, keepdims=True)
    ggain = jnp.sum(r.ggain[...], axis=0, keepdims=True)
    lane_heads = jnp.concatenate([gbias[:, 0:H], glog[:, 0:H], gskip[:, 0:H], jnp.zeros((1, 128 - 3 * H), f32)], axis=1)
    for k in range(16):
        convs = jnp.concatenate([r.gconv[0:5, 112 * k : 112 * k + 112], jnp.zeros((5, 16), f32)], axis=1)
        first = jnp.concatenate([ngain[:, 48 * k : 48 * k + 48], jnp.zeros((1, 80), f32)], axis=1)
        second = jnp.concatenate([ggain[:, 96 * k : 96 * k + 96], jnp.zeros((1, 32), f32)], axis=1)
        r.table[k] = jnp.concatenate([convs, first, second, lane_heads], axis=0)

    def to_all(k, act):
        other = lax.rem(me + k, 16)
        for far in range(2):
            copy = pltpu.make_async_remote_copy(
                src_ref=r.table.at[other], dst_ref=r.inbox.at[c, me], send_sem=r.table_sem.at[0, far, other],
                recv_sem=r.table_sem.at[1, c, me], device_id=(far, other), device_id_type=MESH,
            )
            pl.when(jnp.logical_or(k > 0, far != c))(functools.partial(act, copy))

    def from_all(k):
        other = lax.rem(me + k, 16)
        for far in range(2):
            copy = pltpu.make_async_remote_copy(
                src_ref=r.table.at[other], dst_ref=r.inbox.at[far, other], send_sem=r.table_sem.at[0, far, other],
                recv_sem=r.table_sem.at[1, far, other], device_id=(far, other), device_id_type=MESH,
            )
            pl.when(jnp.logical_or(k > 0, far != c))(copy.wait_recv)

    loop(0, 16, lambda k: to_all(k, lambda copy: copy.start()))
    r.inbox[c, me] = r.table[me]
    for item in (reduce_out, reduce_z):
        item.drain_early()
        item.drain_late()
        item.finish()
    for item in (backward, acts):
        item.finish()
    acts.arrived()
    reduce_second.sides(0)
    reduce_first.column(0)
    reduce_second.column(1)
    reduce_first.close()
    reduce_first.drain_early()
    reduce_second.drain_early()
    reduce_first.drain_late()
    loop(0, 16, lambda k: to_all(k, lambda copy: copy.wait_send()))
    pl.when(z + c > 0)(tails[0].wait_send)
    reduce_second.column(0)
    reduce_second.close()
    loop(0, 16, from_all)
    r.small_out[...] = jnp.sum(jnp.sum(r.inbox[...], axis=0), axis=0)
    reduce_second.drain_late()
    grads.finish()
    grads.arrived()
    reduce_first.finish()
    reduce_second.finish()


def block(given, planes):
    f32, bf16 = jnp.float32, jnp.bfloat16
    shape = jax.ShapeDtypeStruct
    named = block_scratch(planes)
    extra = Chain.scratch() + Chain.scratch()[:6] + Chain.scratch()[8:]
    extra += Reduce.scratch(48, WIDE // 2, "columns", planes) + Reduce.scratch(48, WIDE // 2, "columns", planes) + Reduce.scratch(48, DI, "columns", planes)
    extra += Reduce.scratch(96, 768, "rows", planes)
    return pl.pallas_call(
        functools.partial(block_kernel, planes, list(named)),
        out_shape=[
            shape((2, 128, 768), bf16), shape((2, 128, 768), bf16), shape((2, 48, WIDE // 2), f32),
            shape((48, DI), f32), shape((96, 768), f32), shape((8, 128), f32),
        ],
        in_specs=[VMEM] * len(GIVEN),
        out_specs=[VMEM] * len(MADE),
        scratch_shapes=list(named.values()) + extra,
        compiler_params=pltpu.CompilerParams(collective_id=0, has_side_effects=True, vmem_limit_bytes=62 << 20),
    )(*given)


def deliver_kernel(acts, tokens, grad_a, grad_z, grad_out, sums, *out):
    out[0][...] = acts[...]
    out[1][...] = tokens[...]
    out[2][...] = sums[5:6, 0:48]
    out[3][:, 0:DI] = grad_z[...]
    out[3][:, DI : DI + WIDE // 2] = grad_a[0]
    out[3][:, DI + WIDE // 2 :] = grad_a[1, :, 0 : CH + H - WIDE // 2]
    out[4][...] = sums[0:4, 0:112]
    out[5][...] = sums[4:5, 0:112]
    out[6][...] = sums[7:8, 0:H]
    out[7][...] = sums[7:8, H : 2 * H]
    out[8][...] = sums[7:8, 2 * H : 3 * H]
    out[9][...] = sums[6:7, 0:96]
    out[10][...] = grad_out[...]


def deliver(made):
    f32, bf16 = jnp.float32, jnp.bfloat16
    shapes = [
        ((2, 128, 768), bf16), ((2, 128, 768), bf16), ((1, 48), f32), ((48, DI + CH + H), f32), ((4, 112), f32), ((1, 112), f32),
        ((1, H), f32), ((1, H), f32), ((1, H), f32), ((1, 96), f32), ((96, 768), f32),
    ]
    return pl.pallas_call(
        deliver_kernel,
        out_shape=[jax.ShapeDtypeStruct(*s) for s in shapes],
        in_specs=[VMEM] * len(made),
        out_specs=[VMEM] * len(shapes),
    )(*made)


def fast_body(
    planes, tokens, cotangent, segments, norm_gain, w_in, conv_weight, conv_bias, step_bias, log_rate, skip_gain, gate_gain, w_out
):
    def at_row(row, values):
        values = values.astype(jnp.float32).reshape(-1, values.shape[-1])
        return jnp.pad(values, ((row, 16 - row - values.shape[0]), (0, 128 - values.shape[1])))

    rows = ((0, conv_weight), (4, conv_bias), (5, norm_gain), (6, gate_gain), (8, step_bias), (9, log_rate), (10, skip_gain))
    small = sum(at_row(row, values) for row, values in rows)
    made = block((tokens[:, 0], cotangent[:, 0], segments[:, 0], small, w_in, w_out), planes)
    out = deliver(made)
    return (
        out[0][:, None], out[1][:, None], out[2][0], out[3], out[4], out[5][0], out[6][0], out[7][0], out[8][0], out[9][0], out[10],
    )


def solution(mesh):
    in_specs = (
        P(None, "dp", "seq", None),
        P(None, "dp", "seq", None),
        P(None, "dp", "seq"),
        P("seq"),
        P("seq", None),
        P(None, "seq"),
        P("seq"),
        P(),
        P(),
        P(),
        P("seq"),
        P("seq", None),
    )
    out_specs = (
        P(None, "dp", "seq", None),
        P(None, "dp", "seq", None),
        P("seq"),
        P("seq", None),
        P(None, "seq"),
        P("seq"),
        P(),
        P(),
        P(),
        P("seq"),
        P("seq", None),
    )
    work = partial(fast_body, mesh.shape["seq"] // 4) if mesh.shape["seq"] == 16 else body
    return jax.shard_map(work, mesh=mesh, in_specs=in_specs, out_specs=out_specs, check_vma=False)
```

```python
import functools
from functools import partial

import jax
import jax.numpy as jnp
from jax import lax
from jax.experimental import pallas as pl
from jax.experimental.pallas import tpu as pltpu
from jax.sharding import PartitionSpec as P

DI = 1536
H = 24
P_SIZE = 64
N = 128
KC = 4
CH = 1792


EPSILON = 1e-05
HIGHEST = lax.Precision.HIGHEST


def passed_along(array, axis, by):
    devices = lax.axis_size(axis)
    pairs = [(i, i + by) for i in range(devices) if 0 <= i + by < devices]
    return lax.ppermute(array, axis, pairs)


def prefix(array, axis, combine, identity, reverse):
    devices, place = (lax.axis_size(axis), lax.axis_index(axis))
    everything = jax.tree.map(lambda part: lax.all_gather(part, axis), array)
    start = jax.tree.map(
        lambda part, zero: jnp.broadcast_to(jnp.asarray(zero, part.dtype), part.shape),
        array,
        identity,
    )

    def lap(k, before):
        at = devices - 1 - k if reverse else k
        reached = at > place if reverse else at < place
        new = combine(before, jax.tree.map(lambda part: part[at], everything))
        return jax.tree.map(lambda a, b: jnp.where(reached, a, b), new, before)

    return lax.fori_loop(0, devices, lap, start)


def for_sending(array):
    return jax.tree.map(lambda a: a.astype(jnp.bfloat16) if a.dtype == jnp.float32 else a, array)


def rms_scale(values, gain_vec):
    return (
        values * lax.rsqrt(jnp.mean(values * values, axis=-1, keepdims=True) + EPSILON) * gain_vec
    )


def causal_conv(padded, seg_pad, seg_one, kernel, offset):
    length_t = seg_one.shape[0]
    total = jnp.zeros((length_t, padded.shape[1]), jnp.float32) + offset[None, :]
    for tap_index in range(KC):
        window = padded[tap_index : tap_index + length_t]
        same_doc = (seg_pad[tap_index : tap_index + length_t] == seg_one).astype(jnp.float32)
        total = total + kernel[tap_index][None, :] * window * same_doc[:, None]
    return total


def cumulative(step_size, rate):
    length_t = step_size.shape[0]
    lower = jnp.tril(jnp.ones((length_t, length_t), jnp.float32))
    return jnp.dot(lower, step_size * rate[None, :], precision=HIGHEST)


def block_state(inner, b_proj, step_size, rate, seg_one, previous):
    cum_decay = cumulative(step_size, rate)
    last_seg = seg_one[-1]
    to_end = (
        jnp.where((seg_one == last_seg)[:, None], jnp.exp(cum_decay[-1][None, :] - cum_decay), 0.0)
        * step_size
    )
    state_part = jnp.einsum("uhp,un->hpn", inner * to_end[:, :, None], b_proj, precision=HIGHEST)
    through = jnp.logical_and(seg_one[0] == last_seg, seg_one[0] == previous).astype(jnp.float32)
    return (state_part, jnp.exp(cum_decay[-1]) * through)


def block_output(inner, b_proj, c_proj, step_size, rate, state_in, seg_one, previous):
    cum_decay = cumulative(step_size, rate)
    length_t = seg_one.shape[0]
    row_index = lax.broadcasted_iota(jnp.int32, (length_t, length_t), 0)
    col_index = lax.broadcasted_iota(jnp.int32, (length_t, length_t), 1)
    allowed = jnp.logical_and(row_index >= col_index, seg_one[:, None] == seg_one[None, :])[
        :, :, None
    ]
    spread = cum_decay[:, None, :] - cum_decay[None, :, :]
    decays = jnp.where(allowed, jnp.exp(jnp.where(allowed, spread, 0.0)), 0.0)
    scores = jnp.dot(c_proj, b_proj.T, precision=HIGHEST)
    weights = decays * scores[:, :, None] * step_size[None, :, :]
    local_part = jnp.einsum("tuh,uhp->thp", weights, inner, precision=HIGHEST)
    carried = (seg_one == previous).astype(jnp.float32)[:, None] * jnp.exp(cum_decay)
    return local_part + carried[:, :, None] * jnp.einsum(
        "tn,hpn->thp", c_proj, state_in, precision=HIGHEST
    )


def prepare(proj_out, tail_rows, kernel, offset, step_bias, log_rate, tail_seg, seg_one):
    length_t = proj_out.shape[0]
    padded = jnp.concatenate([tail_rows, proj_out[:, DI : DI + CH]], axis=0)
    seg_pad = jnp.concatenate([tail_seg, seg_one])
    activated = jax.nn.silu(causal_conv(padded, seg_pad, seg_one, kernel, offset))
    inner = activated[:, :DI].reshape(length_t, H, P_SIZE)
    b_proj = activated[:, DI : DI + N]
    c_proj = activated[:, DI + N :]
    step_size = jax.nn.softplus(proj_out[:, DI + CH :] + step_bias[None, :])
    rate = -jnp.exp(log_rate)
    return (inner, b_proj, c_proj, step_size, rate, proj_out[:, :DI])


def finish(
    inner,
    b_proj,
    c_proj,
    step_size,
    rate,
    gate_in,
    state_in,
    skip_gain,
    gate_gain,
    seg_one,
    previous,
):
    length_t = inner.shape[0]
    mixed = block_output(inner, b_proj, c_proj, step_size, rate, state_in, seg_one, previous)
    mixed = mixed + skip_gain[None, :, None] * inner
    gated = mixed.reshape(length_t, DI) * jax.nn.silu(gate_in)
    return rms_scale(gated, gate_gain)


def chain_link(earlier, later):
    return (earlier[0] * later[0], later[0][:, None, None] * earlier[1] + later[1])


def body(
    tokens,
    cotangent,
    segments,
    norm_gain,
    w_in,
    conv_weight,
    conv_bias,
    step_bias,
    log_rate,
    skip_gain,
    gate_gain,
    w_out,
):
    batches = tokens.shape[0]
    length_t = tokens.shape[2]
    halo_rows = KC - 1
    identity = (jnp.ones((H,), jnp.float32), jnp.zeros((H, P_SIZE, N), jnp.float32))
    totals = None
    head_totals = (
        jnp.zeros((H,), jnp.float32),
        jnp.zeros((H,), jnp.float32),
        jnp.zeros((H,), jnp.float32),
    )
    act_list = []
    grad_list = []
    for micro in range(batches):
        gathered = (
            lax.all_gather(w_in, "seq", axis=0, tiled=True),
            lax.all_gather(w_out, "seq", axis=0, tiled=True),
            lax.all_gather(conv_weight, "seq", axis=1, tiled=True),
            lax.all_gather(conv_bias, "seq", axis=0, tiled=True),
            lax.all_gather(norm_gain, "seq", axis=0, tiled=True),
            lax.all_gather(gate_gain, "seq", axis=0, tiled=True),
        )
        in_full = gathered[0]
        out_full = gathered[1]
        kernel = gathered[2].astype(jnp.float32)
        offset = gathered[3].astype(jnp.float32)
        gain_one = gathered[4].astype(jnp.float32)
        gain_two = gathered[5].astype(jnp.float32)
        resid = tokens[micro, 0].astype(jnp.float32)
        seg_one = segments[micro, 0].astype(jnp.float32) + 1.0
        normed, norm_back = jax.vjp(rms_scale, resid, gain_one)
        normed_low = normed.astype(jnp.bfloat16)
        proj_out = jnp.dot(normed_low, in_full, preferred_element_type=jnp.float32)
        tail_rows, tail_seg = passed_along(
            (proj_out[length_t - halo_rows :, DI : DI + CH], seg_one[length_t - halo_rows :]),
            "seq",
            1,
        )
        previous = tail_seg[halo_rows - 1]
        prepared, prep_back = jax.vjp(
            partial(prepare, tail_seg=tail_seg, seg_one=seg_one),
            proj_out,
            tail_rows,
            kernel,
            offset,
            step_bias,
            log_rate,
        )
        inner, b_proj, c_proj, step_size, rate, gate_in = prepared
        state_out, state_back = jax.vjp(
            partial(block_state, seg_one=seg_one, previous=previous), inner, b_proj, step_size, rate
        )
        state_part, through = state_out
        state_in = prefix((through, state_part), "seq", chain_link, identity, False)[1]
        normed_two, finish_back = jax.vjp(
            partial(finish, seg_one=seg_one, previous=previous),
            inner,
            b_proj,
            c_proj,
            step_size,
            rate,
            gate_in,
            state_in,
            skip_gain,
            gain_two,
        )
        gate_low = normed_two.astype(jnp.bfloat16)
        branch = jnp.dot(gate_low, out_full, preferred_element_type=jnp.float32)
        act_list.append((resid + branch).astype(jnp.bfloat16))
        cot_low = cotangent[micro, 0]
        again = (
            lax.all_gather(w_in, "seq", axis=0, tiled=True),
            lax.all_gather(w_out, "seq", axis=0, tiled=True),
        )
        in_back = again[0]
        out_back = again[1]
        out_term = lax.dot_general(
            gate_low, cot_low, (((0,), (0,)), ((), ())), preferred_element_type=jnp.float32
        )
        grad_gate = lax.dot_general(
            cot_low, out_back, (((1,), (1,)), ((), ())), preferred_element_type=jnp.float32
        )
        g_inner, g_bproj, g_cproj, g_step, g_rate, g_gate_in, g_state_in, g_skip, g_gain_two = (
            finish_back(grad_gate)
        )
        carried = prefix((through, g_state_in), "seq", chain_link, identity, True)[1]
        h_inner, h_bproj, h_step, h_rate = state_back(
            (carried, jnp.sum(carried * state_in, axis=(1, 2)))
        )
        g_proj, g_tail, g_kernel, g_offset, g_bias, g_log = prep_back(
            (
                g_inner + h_inner,
                g_bproj + h_bproj,
                g_cproj,
                g_step + h_step,
                g_rate + h_rate,
                g_gate_in,
            )
        )
        returned = passed_along(g_tail, "seq", -1)
        width_after = proj_out.shape[1] - DI - CH
        g_proj = g_proj + jnp.pad(returned, ((length_t - halo_rows, 0), (DI, width_after)))
        proj_grad_low = g_proj.astype(jnp.bfloat16)
        grad_normed = lax.dot_general(
            proj_grad_low, in_back, (((1,), (1,)), ((), ())), preferred_element_type=jnp.float32
        )
        grad_resid, g_gain_one = norm_back(grad_normed)
        grad_list.append((cot_low.astype(jnp.float32) + grad_resid).astype(jnp.bfloat16))
        in_shard = lax.psum_scatter(
            lax.dot_general(
                normed_low,
                proj_grad_low,
                (((0,), (0,)), ((), ())),
                preferred_element_type=jnp.float32,
            ),
            "seq",
            scatter_dimension=0,
            tiled=True,
        )
        shards = (
            lax.psum_scatter(out_term, "seq", scatter_dimension=0, tiled=True),
            lax.psum_scatter(g_kernel, "seq", scatter_dimension=1, tiled=True),
            lax.psum_scatter(g_offset, "seq", scatter_dimension=0, tiled=True),
            lax.psum_scatter(g_gain_one, "seq", scatter_dimension=0, tiled=True),
            lax.psum_scatter(g_gain_two, "seq", scatter_dimension=0, tiled=True),
        )
        this_round = (in_shard, shards[0], shards[1], shards[2], shards[3], shards[4])
        if totals is None:
            totals = this_round
        else:
            totals = tuple((prior + fresh for prior, fresh in zip(totals, this_round)))
        head_totals = (head_totals[0] + g_bias, head_totals[1] + g_log, head_totals[2] + g_skip)
    summed = jax.tree.map(
        lambda part: part.astype(jnp.float32), lax.psum(for_sending(totals), "dp")
    )
    heads = lax.psum((head_totals[0], head_totals[1], head_totals[2]), ("dp", "seq"))
    activations = jnp.stack(act_list)[:, None]
    grad_tokens = jnp.stack(grad_list)[:, None]
    return (
        activations,
        grad_tokens,
        summed[4],
        summed[0],
        summed[2],
        summed[3],
        heads[0],
        heads[1],
        heads[2],
        summed[5],
        summed[1],
    )


MESH = pl.DeviceIdType.MESH


def chip(x, y, z):
    return z * 4 + y * 2 + x


def place():
    core = lax.axis_index("dp")
    at = lax.axis_index("seq")
    return at % 2, (at // 2) % 2, at // 4, core


def greet_all(planes):
    barrier = pltpu.get_barrier_semaphore()
    me = lax.axis_index("seq")
    core = lax.axis_index("dp")
    count = planes * 4

    def greet(k, carry):
        other = lax.rem(me + k, count)
        for far in range(2):

            @pl.when(jnp.logical_or(k > 0, far != core))
            def _():
                pl.semaphore_signal(barrier, inc=1, device_id=(far, other), device_id_type=MESH)

        return carry

    lax.fori_loop(0, count, greet, 0)


def meet_all(planes):
    pl.semaphore_wait(pltpu.get_barrier_semaphore(), 8 * planes - 1)


COLUMN, SIDE_X, SIDE_Y, HALF_X, HALF_Y, MATE_Z, MATE_X, MATE_Y, MATE_HX, MATE_HY = range(10)


class Gather:
    def __init__(self, whole, rows, quarter, sems, planes):
        self.whole, self.rows, self.quarter, self.sems, self.planes = whole, rows, quarter, sems, planes
        self.x, self.y, self.z, self.core = place()

    def region(self, block, core, part=None):
        width = self.whole.shape[1] // 2
        start = pl.multiple_of(block * self.rows, 16)
        left = pl.multiple_of(core * width, 128)
        if part is None:
            return self.whole.at[pl.ds(start, self.rows), pl.ds(left, width)]
        if self.quarter == "rows":
            half = self.rows // 2
            return self.whole.at[pl.ds(pl.multiple_of(start + part * half, 16), half), pl.ds(left, width)]
        half = width // 2
        return self.whole.at[pl.ds(start, self.rows), pl.ds(pl.multiple_of(left + part * half, 128), half)]

    def copy(self, kind, leaves, lands, block, core, part, device):
        region = self.region(block, core, part)
        return pltpu.make_async_remote_copy(
            src_ref=region,
            dst_ref=region,
            send_sem=self.sems.at[0, kind, leaves],
            recv_sem=self.sems.at[1, kind, lands],
            device_id=device,
            device_id_type=MESH,
        )

    def out(self, kind, far):
        x, y, z, c = self.x, self.y, self.z, self.core
        if kind == COLUMN:
            return self.copy(kind, far, z, chip(x, y, z), c, None, (c, chip(x, y, far)))
        own, by_x, by_y, across = chip(x, y, far), chip(1 - x, y, far), chip(x, 1 - y, far), chip(1 - x, 1 - y, far)
        mate = (1 - c, chip(x, y, z))
        to_x, to_y = (c, chip(1 - x, y, z)), (c, chip(x, 1 - y, z))
        block, part, device = {
            SIDE_X: (own, None, to_x),
            SIDE_Y: (own, None, to_y),
            HALF_X: (by_y, 1, to_x),
            HALF_Y: (by_x, 0, to_y),
            MATE_Z: (own, None, mate),
            MATE_X: (by_x, None, mate),
            MATE_Y: (by_y, None, mate),
            MATE_HX: (across, 1, mate),
            MATE_HY: (across, 0, mate),
        }[kind]
        return self.copy(kind, far, far, block, c, part, device)

    def send(self, kind, far):
        self.out(kind, far).start()

    def arrived(self, kind, far):
        x, y = self.x, self.y
        own, by_x, by_y, across = chip(x, y, far), chip(1 - x, y, far), chip(x, 1 - y, far), chip(1 - x, 1 - y, far)
        block, part, mine = {
            COLUMN: (own, None, True),
            SIDE_X: (by_x, None, True),
            SIDE_Y: (by_y, None, True),
            HALF_X: (across, 1, True),
            HALF_Y: (across, 0, True),
            MATE_Z: (own, None, False),
            MATE_X: (by_x, None, False),
            MATE_Y: (by_y, None, False),
            MATE_HX: (across, 1, False),
            MATE_HY: (across, 0, False),
        }[kind]
        core = self.core if mine else 1 - self.core
        self.copy(kind, far, far, block, core, part, (1 - self.core, chip(x, y, self.z))).wait_recv()

    def each(self, distance, act):
        for sign in (-1, 1) if distance else (1,):
            far = self.z + sign * distance
            if distance:
                pl.when(jnp.logical_and(far >= 0, far < self.planes))(functools.partial(act, far))
            else:
                act(far)

    def begin_sides(self):
        self.send(SIDE_X, self.z)
        self.send(SIDE_Y, self.z)

    def begin_column(self):
        for distance in range(1, self.planes):
            self.each(distance, lambda far: self.send(COLUMN, far))

    def begin(self):
        self.begin_sides()
        self.begin_column()

    def column(self, distance):
        def act(far):
            self.arrived(COLUMN, far)
            self.send(SIDE_X, far)
            self.send(SIDE_Y, far)
            self.send(MATE_Z, far)

        self.each(distance, act)

    def sides(self, distance):
        def act(far):
            self.arrived(SIDE_X, far)
            self.send(HALF_Y, far)
            self.send(MATE_X, far)
            self.arrived(SIDE_Y, far)
            self.send(HALF_X, far)
            self.send(MATE_Y, far)

        self.each(distance, act)

    def diagonal(self, distance):
        def act(far):
            self.arrived(HALF_Y, far)
            self.send(MATE_HY, far)
            self.arrived(HALF_X, far)
            self.send(MATE_HX, far)

        self.each(distance, act)

    def whole_here(self):
        for distance in range(self.planes):

            def act(far):
                for kind in (MATE_X, MATE_Y, MATE_HX, MATE_HY) + ((MATE_Z,) if distance else ()):
                    self.arrived(kind, far)

            self.each(distance, act)

    def finish(self):
        for distance in range(self.planes):

            def act(far):
                kinds = (SIDE_X, SIDE_Y, HALF_X, HALF_Y, MATE_X, MATE_Y, MATE_HX, MATE_HY)
                for kind in kinds + ((MATE_Z, COLUMN) if distance else ()):
                    self.out(kind, far).wait_send()

            self.each(distance, act)


def gather_sems(planes):
    return pltpu.SemaphoreType.DMA((2, 10, planes))


class Reduce:
    X, Y, HX, HY, COLUMN, MATE, LAST = range(7)

    @staticmethod
    def scratch(rows, width, quarter, planes):
        half = width // 2
        corner = (rows // 2, half) if quarter == "rows" else (rows, half // 2)
        bf16 = jnp.bfloat16
        return [
            pltpu.VMEM((4 * planes * rows, half), bf16),
            pltpu.VMEM((3, planes, rows, half), bf16),
            pltpu.VMEM((2, planes) + corner, bf16),
            pltpu.SemaphoreType.DMA((2, 7, planes)),
        ]

    def __init__(self, part, out, rows, quarter, scratch, planes):
        self.part, self.out, self.rows, self.quarter, self.planes = part, out, rows, quarter, planes
        self.mate_in, self.side_in, self.corner_in, self.sems = scratch
        self.x, self.y, self.z, self.core = place()
        self.half = part.shape[1] // 2

    def block(self, owner, part=None):
        start = pl.multiple_of(owner * self.rows, 16)
        left = pl.multiple_of(self.core * self.half, 128)
        if part is None:
            return pl.ds(start, self.rows), pl.ds(left, self.half)
        if self.quarter == "rows":
            return pl.ds(pl.multiple_of(start + part * (self.rows // 2), 16), self.rows // 2), pl.ds(left, self.half)
        quarter = self.half // 2
        return pl.ds(start, self.rows), pl.ds(pl.multiple_of(left + part * quarter, 128), quarter)

    def copy(self, kind, far, source, target, device):
        return pltpu.make_async_remote_copy(
            src_ref=source,
            dst_ref=target,
            send_sem=self.sems.at[0, kind, far],
            recv_sem=self.sems.at[1, kind, far],
            device_id=device,
            device_id_type=MESH,
        )

    def move(self, kind, far):
        x, y, z, c = self.x, self.y, self.z, self.core
        part = self.part
        to_x, to_y, mate = (c, chip(1 - x, y, z)), (c, chip(x, 1 - y, z)), (1 - c, chip(x, y, z))
        if kind == self.X:
            return self.copy(kind, far, part.at[self.block(chip(1 - x, y, far))], self.side_in.at[0, far], to_x)
        if kind == self.Y:
            return self.copy(kind, far, part.at[self.block(chip(x, 1 - y, far))], self.side_in.at[1, far], to_y)
        if kind == self.HX:
            return self.copy(kind, far, part.at[self.block(chip(1 - x, 1 - y, far), 0)], self.corner_in.at[0, far], to_x)
        if kind == self.HY:
            return self.copy(kind, far, part.at[self.block(chip(1 - x, 1 - y, far), 1)], self.corner_in.at[1, far], to_y)
        if kind == self.COLUMN:
            return pltpu.make_async_remote_copy(
                src_ref=part.at[self.block(chip(x, y, far))],
                dst_ref=self.side_in.at[2, z],
                send_sem=self.sems.at[0, kind, far],
                recv_sem=self.sems.at[1, kind, z],
                device_id=(c, chip(x, y, far)),
                device_id_type=MESH,
            )
        if kind == self.MATE:
            rows = pl.ds(pl.multiple_of(far * 4 * self.rows, 16), 4 * self.rows)
            left = pl.multiple_of((1 - c) * self.half, 128)
            return self.copy(kind, far, part.at[rows, pl.ds(left, self.half)], self.mate_in.at[rows], mate)
        left = pl.multiple_of(c * self.half, 128)
        region = self.out.at[:, pl.ds(left, self.half)]
        return self.copy(kind, 0, region, region, mate)

    def add(self, at, *refs):
        total = self.part[at].astype(jnp.float32)
        for ref in refs:
            total = total + ref[...].astype(jnp.float32)
        self.part[at] = low(total)

    def each(self, distance, act):
        for sign in (-1, 1) if distance else (1,):
            far = self.z + sign * distance
            if distance:
                pl.when(jnp.logical_and(far >= 0, far < self.planes))(functools.partial(act, far, sign))
            else:
                act(far, sign)

    def start(self, distance):
        self.each(distance, lambda far, sign: self.move(self.MATE, far).start())

    def fold(self, distance):
        def act(far, sign):
            self.move(self.MATE, far).wait_recv()

            def rows(k, carry):
                start = pl.multiple_of((far * 4 + k) * self.rows, 16)
                left = pl.multiple_of(self.core * self.half, 128)
                self.add((pl.ds(start, self.rows), pl.ds(left, self.half)), self.mate_in.at[pl.ds(start, self.rows)])
                return carry

            lax.fori_loop(0, 4, rows, 0)
            self.move(self.HX, far).start()
            self.move(self.HY, far).start()

        self.each(distance, act)

    def sides(self, distance):
        x, y = self.x, self.y

        def act(far, sign):
            self.move(self.HX, far).wait_recv()
            self.add(self.block(chip(x, 1 - y, far), 0), self.corner_in.at[0, far])
            self.move(self.Y, far).start()
            self.move(self.HY, far).wait_recv()
            self.add(self.block(chip(1 - x, y, far), 1), self.corner_in.at[1, far])
            self.move(self.X, far).start()

        self.each(distance, act)

    def column(self, distance):
        x, y, z = self.x, self.y, self.z

        def act(far, sign):
            self.move(self.X, far).wait_recv()
            self.move(self.Y, far).wait_recv()
            if distance:
                self.add(self.block(chip(x, y, far)), self.side_in.at[0, far], self.side_in.at[1, far])
                self.move(self.COLUMN, far).start()

        self.each(distance, act)

    def close(self):
        z = self.z
        at = self.block(chip(self.x, self.y, z))
        left = pl.multiple_of(self.core * self.half, 128)
        here = (slice(None), pl.ds(left, self.half))
        total = self.part[at].astype(jnp.float32)
        self.out[here] = total + self.side_in[0, z].astype(jnp.float32) + self.side_in[1, z].astype(jnp.float32)
        for distance in range(self.planes - 1, 0, -1):

            def act(far, sign):
                self.copy(self.COLUMN, far, self.side_in.at[2, far], self.side_in.at[2, far], (self.core, chip(self.x, self.y, far))).wait_recv()
                self.out[here] = self.out[here] + self.side_in[2, far].astype(jnp.float32)

            self.each(distance, act)
        self.move(self.LAST, 0).start()

    def finish(self):
        last = self.move(self.LAST, 0)
        left = pl.multiple_of((1 - self.core) * self.half, 128)
        region = self.out.at[:, pl.ds(left, self.half)]
        self.copy(self.LAST, 0, region, region, (1 - self.core, chip(self.x, self.y, self.z))).wait_recv()
        last.wait_send()

    def drain(self, kinds):
        for distance in range(self.planes):

            def act(far, sign):
                for kind in kinds:
                    if distance or kind != self.COLUMN:
                        self.move(kind, far).wait_send()

            self.each(distance, act)

    def drain_early(self):
        self.drain((self.MATE, self.HX, self.HY))

    def drain_late(self):
        self.drain((self.X, self.Y, self.COLUMN))


class Chain:
    CUT = 6

    @staticmethod
    def scratch():
        half = pltpu.VMEM((N, DI // 2), jnp.bfloat16)
        wide = pltpu.VMEM((N, DI // 2), jnp.float32)
        return [half, half, half, half, half, half, wide, wide, pltpu.SemaphoreType.DMA((2, 2 + Chain.CUT))]

    def __init__(self, part, result, factors, scratch, lead, planes):
        self.part, self.result, self.factors, self.lead, self.planes = part, result, factors, lead, planes
        self.give, self.take, self.leave, self.come, self.back, self.again, self.total, self.front, self.sems = scratch
        self.x, self.y, self.z, self.core = place()
        self.half = DI // 2
        self.leads = self.core == lead
        self.ahead = 1 if lead == 0 else -1
        self.first = self.z == (0 if lead == 0 else planes - 1)
        self.last = self.z == (planes - 1 if lead == 0 else 0)

    def own(self):
        return pl.ds(pl.multiple_of(self.core * self.half, 128), self.half)

    def other(self):
        return pl.ds(pl.multiple_of((1 - self.core) * self.half, 128), self.half)

    def copy(self, k, source, target, device):
        return pltpu.make_async_remote_copy(
            src_ref=source,
            dst_ref=target,
            send_sem=self.sems.at[0, k],
            recv_sem=self.sems.at[1, k],
            device_id=device,
            device_id_type=MESH,
        )

    def mate(self):
        return (1 - self.core, chip(self.x, self.y, self.z))

    def trade(self):
        return self.copy(0, self.give, self.take, self.mate())

    def returned(self):
        return self.copy(1, self.back, self.again, self.mate())

    def hop(self, k):
        cut = self.half // self.CUT
        at = (slice(None), pl.ds(k * cut, cut))
        return self.copy(
            2 + k, self.leave.at[at], self.come.at[at], (self.core, chip(self.x, self.y, self.z + self.ahead))
        )

    def start(self):
        self.give[...] = low(self.part[:, self.other()])
        self.trade().start()

    def rows(self):
        return self.factors[self.lead, 0:1, self.own()], self.factors[1 - self.lead, 0:1, self.own()]

    def merge(self):
        self.trade().wait_recv()
        own = self.part[:, self.own()]
        got = self.take[...].astype(jnp.float32)
        ahead, behind = jnp.where(self.leads, own, got), jnp.where(self.leads, got, own)
        _, following = self.rows()
        self.front[...] = ahead
        self.total[...] = following * ahead + behind

        @pl.when(self.first)
        def _():
            self.come[...] = jnp.zeros(self.come.shape, self.come.dtype)
            self.leave[...] = low(self.total[...])
            for k in range(self.CUT):
                self.hop(k).start()

    def pass_on(self):
        leading, following = self.rows()
        cut = self.half // self.CUT

        @pl.when(jnp.logical_not(self.first))
        def _():
            for k in range(self.CUT):
                self.hop(k).wait_recv()

                @pl.when(jnp.logical_not(self.last))
                def _():
                    at = (slice(None), slice(k * cut, (k + 1) * cut))
                    both = (leading * following)[:, k * cut : (k + 1) * cut]
                    self.leave[at] = low(both * self.come[at].astype(jnp.float32) + self.total[at])
                    self.hop(k).start()

        came = self.come[...].astype(jnp.float32)
        later = low(leading * came + self.front[...])
        self.back[...] = jnp.where(self.leads, later.astype(jnp.float32), came).astype(jnp.bfloat16)
        self.returned().start()
        self.result[:, self.own()] = jnp.where(self.leads, came, later.astype(jnp.float32)).astype(jnp.bfloat16)

    def close(self):
        self.returned().wait_recv()
        self.result[:, self.other()] = self.again[...]

    def finish(self):
        self.trade().wait_send()
        self.returned().wait_send()

        @pl.when(jnp.logical_not(self.last))
        def _():
            for k in range(self.CUT):
                self.hop(k).wait_send()


VMEM = pl.BlockSpec(memory_space=pltpu.VMEM)
ROWS = 256
HALO = 16
WIDE = 2048
TRANS = (((0,), (0,)), ((), ()))
TRANS_B = (((1,), (1,)), ((), ()))


def dot(a, b, dims=(((1,), (0,)), ((), ()))):
    return lax.dot_general(a, b, dims, preferred_element_type=jnp.float32)


def low(a):
    return a.astype(jnp.bfloat16)


class Shuffle:
    def __init__(self, source, target, sems, offset=0, back=False):
        self.source, self.target, self.sems, self.offset, self.back = source, target, sems, offset, back
        self.x, self.y, self.z, self.core = place()

    def piece(self, k):
        x, y, z, c = self.x, self.y, self.z, self.core
        rows = 128
        if self.back:
            source = self.source.at[pl.ds(rows * k, rows)]
            target = self.target.at[x]
        else:
            source = self.source.at[k]
            if len(self.target.shape) == len(self.source.shape):
                target = self.target.at[self.offset + x]
            else:
                target = self.target.at[pl.ds(pl.multiple_of(self.offset + rows * x, 16), rows)]
        stays = jnp.logical_and(x == k, y == c)
        local = pltpu.make_async_copy(source, target, self.sems.at[1, x])
        remote = pltpu.make_async_remote_copy(
            src_ref=source,
            dst_ref=target,
            send_sem=self.sems.at[0, k],
            recv_sem=self.sems.at[1, x],
            device_id=(y, chip(k, c, z)),
            device_id_type=MESH,
        )
        return stays, local, remote

    def start(self):
        for k in range(2):
            stays, local, remote = self.piece(k)
            pl.when(stays)(local.start)
            pl.when(jnp.logical_not(stays))(remote.start)

    def arrived(self):
        x, y, z, c = self.x, self.y, self.z, self.core
        for k in range(2):
            if self.back:
                target = self.target.at[k]
            elif len(self.target.shape) == len(self.source.shape):
                target = self.target.at[self.offset + k]
            else:
                target = self.target.at[pl.ds(self.offset + 128 * k, 128)]
            stays = jnp.logical_and(x == k, y == c)
            local = pltpu.make_async_copy(target, target, self.sems.at[1, k])
            remote = pltpu.make_async_remote_copy(
                src_ref=target,
                dst_ref=target,
                send_sem=self.sems.at[0, k],
                recv_sem=self.sems.at[1, k],
                device_id=(y, chip(k, c, z)),
                device_id_type=MESH,
            )
            pl.when(stays)(local.wait)
            pl.when(jnp.logical_not(stays))(remote.wait_recv)

    def finish(self):
        for k in range(2):
            stays, local, remote = self.piece(k)
            pl.when(jnp.logical_not(stays))(remote.wait_send)


class Before:
    def __init__(self, source, target, sems, planes):
        self.source, self.target, self.sems, self.planes = source, target, sems, planes
        self.x, self.y, self.z, self.core = place()

    def piece(self, m):
        x, y, z, c = self.x, self.y, self.z, self.core
        source = self.source(m)
        return pltpu.make_async_remote_copy(
            src_ref=source,
            dst_ref=self.target,
            send_sem=self.sems.at[0, m],
            recv_sem=self.sems.at[1, 0],
            device_id=(1 - y, chip(m, c, z + y)),
            device_id_type=MESH,
        )

    def when_sending(self):
        return jnp.logical_and(self.x == 1, jnp.logical_or(self.y == 0, self.z < self.planes - 1))

    def start(self):
        @pl.when(self.when_sending())
        def _():
            for m in range(2):
                self.piece(m).start()

    def arrived(self):
        pl.when(self.z + self.core > 0)(self.piece(0).wait_recv)

    def finish(self):
        @pl.when(self.when_sending())
        def _():
            for m in range(2):
                self.piece(m).wait_send()


class ToAll:
    def __init__(self, table, sems, planes):
        self.table, self.sems, self.count = table, sems, planes * 4
        self.me, self.core = lax.axis_index("seq"), lax.axis_index("dp")

    def copy(self, block, other):
        return pltpu.make_async_remote_copy(
            src_ref=self.table.at[block],
            dst_ref=self.table.at[block],
            send_sem=self.sems.at[0, other],
            recv_sem=self.sems.at[1, block],
            device_id=(self.core, other),
            device_id_type=MESH,
        )

    def over(self, act):
        def one(k, carry):
            act(lax.rem(self.me + k, self.count))
            return carry

        lax.fori_loop(1, self.count, one, 0)

    def start(self):
        self.over(lambda other: self.copy(self.me, other).start())

    def arrived(self):
        self.over(lambda other: self.copy(other, self.me).wait_recv())

    def finish(self):
        self.over(lambda other: self.copy(self.me, other).wait_send())


TILE = 128
TILES = DI // TILE


class Names:
    def __init__(self, names, refs):
        for name, ref in zip(names, refs, strict=True):
            setattr(self, name, ref)


def at_tile(j):
    return pl.ds(pl.multiple_of(j * TILE, TILE), TILE)


def at_rows(k, rows):
    return pl.ds(pl.multiple_of(k * rows, rows), rows)


def loop(low_end, high_end, act):
    count = high_end - low_end
    width = next(w for w in (6, 4, 3, 2, 1) if count % w == 0)

    def several(k, carry):
        for i in range(width):
            act(low_end + width * k + i)
        return carry

    lax.fori_loop(0, count // width, several, 0)


def iota(shape, dim):
    return lax.broadcasted_iota(jnp.int32, shape, dim)


def pieces(a):
    high = low(a)
    rest = a - high.astype(jnp.float32)
    middle = low(rest)
    return high, middle, low(rest - middle.astype(jnp.float32))


def packed(a):
    a = jnp.where(iota(a.shape, 1) < H, a, 0.0)
    high, middle, rest = (part.astype(jnp.float32) for part in pieces(a))
    return low(high + pltpu.roll(middle, 32, 1) + pltpu.roll(rest, 64, 1))


def spread_matrix(width, first=0):
    row, col = iota((128, width), 0), iota((128, width), 1) + first
    return low(jnp.where(jnp.logical_and(row % 32 == col // P_SIZE, row < 96), 1.0, 0.0))


def head_sums(a, j):
    row, col = iota((TILE, 128), 0), iota((TILE, 128), 1)
    pick = low(jnp.where(row // P_SIZE + 2 * j == col, 1.0, 0.0))
    high, middle, _ = pieces(a)
    return dot(jnp.concatenate([high, middle], axis=1), jnp.concatenate([pick, pick], axis=0))


def sigmoid(v):
    return 1.0 / (1.0 + jnp.exp(-v))


GIVEN = ["tok_in", "cot", "seg_in", "small_in", "w_in", "wout"]
MADE = ["act_out", "tokens_out", "grad_a", "grad_z", "grad_out", "small_out"]


def block_scratch(planes):
    f32, bf16 = jnp.float32, jnp.bfloat16
    v = pltpu.VMEM
    dma = pltpu.SemaphoreType.DMA
    two = dma((2, 2))
    return {
        "wa": v((768, WIDE), bf16), "wa_sem": gather_sems(planes), "tok": v((HALO + ROWS, 768), bf16), "seg": v((3, 8, 128), f32),
        "normed": v((HALO + ROWS, 768), bf16), "proj": v((HALO + ROWS, WIDE), f32), "conv": v((8, CH), f32), "gain": v((8, DI), f32),
        "ngain": v((8, 768), f32), "ngrad": v((8, 768), f32), "scale": v((ROWS, 128), f32), "given": v((16, 8, 128), f32), "numbers": v((2, 8, 128), f32),
        "tok_sem": two, "end_sem": two, "seg_sem": two, "segend_sem": two, "given_sem": dma((2, 16)),
        "wz_full": v((768, DI), bf16), "wout_full": v((DI, 768), bf16), "wz_sem": gather_sems(planes), "wout_sem": gather_sems(planes),
        "cot_own": v((ROWS, 768), bf16), "cot_sem": two, "act_sem": two, "back_sem": two,
        "segcol": v((384, 128), f32), "same": v((KC - 1, ROWS, 128), f32),
        "pre": v((ROWS, CH), f32), "inner": v((ROWS, DI), f32), "bproj": v((ROWS, N), bf16), "cproj": v((ROWS, N), bf16),
        "cumt": v((H, 8, ROWS), f32), "bar": v((ROWS, ROWS), f32), "scores": v((ROWS, ROWS), f32),
        "step": v((ROWS, 128), f32), "ein": v((ROWS, 128), f32), "eout": v((ROWS, 128), f32),
        "stepx": v((ROWS, DI), f32), "einx": v((ROWS, DI), f32), "eoutx": v((ROWS, DI), f32), "cumx": v((ROWS, DI), f32),
        "xs": v((ROWS, DI), bf16), "xso": v((ROWS, DI), bf16),
        "part": v((N, DI), f32), "factors": v((2, 8, DI), f32), "factor_sem": dma((2,)), "skipx": v((8, DI), f32),
        "state": v((N, DI), bf16), "dstate": v((N, DI), bf16),
        "y": v((ROWS, DI), f32), "z": v((ROWS, DI), f32), "gated": v((ROWS, DI), bf16), "act_own": v((ROWS, 768), bf16),
        "dz": v((ROWS, DI), bf16), "dy": v((ROWS, DI), bf16), "dyin": v((ROWS, DI), bf16),
        "ggain": v((8, DI), f32), "gskip": v((8, DI), f32),
        "dscores": v((ROWS, ROWS), f32), "dxs": v((ROWS, DI), f32), "sums": v((3, ROWS, 128), f32),
        "dpre": v((KC, ROWS + HALO, TILE), f32), "late": v((8, CH), f32), "dx": v((HALO + ROWS, WIDE), bf16), "tail": v((8, CH), f32), "tail_in": v((8, CH), f32), "tail_sem": dma((2,)),
        "gconv": v((8, CH), f32), "gtok": v((ROWS, 768), bf16),
        "table": v((16, 8, 128), f32), "inbox": v((2, 16, 8, 128), f32), "table_sem": dma((2, 2, 16)),
        "part_a": v((2, 768, WIDE // 2), bf16), "part_z": v((768, DI), bf16), "part_out": v((DI, 768), bf16),
    }


def block_kernel(planes, names, *refs):
    r = Names(GIVEN + MADE + names, refs[: len(GIVEN) + len(MADE) + len(names)])
    extra = list(refs[len(GIVEN) + len(MADE) + len(names) :])
    chain_f, chain_b = extra[0:9], extra[9:15] + extra[6:8] + extra[15:16]
    red_a, red_b, red_z, red_out = extra[16:20], extra[20:24], extra[24:28], extra[28:32]
    x, y, z, c = place()
    me = chip(x, y, z)
    mate = (1 - c, me)
    f32 = jnp.float32
    greet_all(planes)
    r.wa[pl.ds(pl.multiple_of(me * 48, 16), 48), 0:CH] = r.w_in[:, DI : DI + CH]
    step_columns = r.w_in[:, DI + CH :]
    fill = jnp.zeros((48, WIDE - CH - H), step_columns.dtype)
    r.wa[pl.ds(pl.multiple_of(me * 48, 16), 48), CH:] = jnp.concatenate([step_columns, fill], axis=1)
    r.wz_full[pl.ds(pl.multiple_of(me * 48, 16), 48), :] = r.w_in[:, 0:DI]
    r.wout_full[pl.ds(pl.multiple_of(me * 96, 16), 96), :] = r.wout[...]
    r.given[me] = r.small_in[0:8, :]
    for m in range(2):
        r.numbers[m] = jnp.broadcast_to(r.seg_in[m : m + 1, :].astype(f32) + 1.0, (8, 128))

    @pl.when(z + c == 0)
    def _():
        r.tok[0:HALO, :] = jnp.zeros((HALO, 768), r.tok.dtype)
        r.seg[0] = jnp.full((8, 128), -1.0, f32)

    gather_a = Gather(r.wa, 48, "columns", r.wa_sem, planes)
    gather_z = Gather(r.wz_full, 48, "columns", r.wz_sem, planes)
    gather_out = Gather(r.wout_full, 96, "rows", r.wout_sem, planes)
    cots = Shuffle(r.cot, r.cot_own, r.cot_sem)
    moves = [
        Shuffle(r.tok_in, r.tok, r.tok_sem, HALO),
        Before(lambda m: r.tok_in.at[m, pl.ds(128 - HALO, HALO)], r.tok.at[pl.ds(0, HALO)], r.end_sem, planes),
        Shuffle(r.numbers, r.seg, r.seg_sem, 1),
        Before(lambda m: r.numbers.at[m], r.seg.at[0], r.segend_sem, planes),
        ToAll(r.given, r.given_sem, planes),
    ]
    meet_all(planes)
    for item in moves:
        item.start()
    gather_a.begin()
    gather_a.column(1)
    gather_a.sides(0)
    for item in moves:
        item.arrived()
    r.conv[...] = jnp.concatenate([r.given[k, :, 0:112] for k in range(16)], axis=1)
    r.gain[...] = jnp.concatenate([r.given[k, :, 0:96] for k in range(16)], axis=1)
    r.ngain[...] = jnp.concatenate([r.given[k, :, 0:48] for k in range(16)], axis=1)
    gather_a.column(2)
    gather_a.column(3)
    gather_a.sides(1)
    gather_a.diagonal(0)
    u = r.tok[...].astype(f32)
    r.normed[...] = low(u * lax.rsqrt(jnp.mean(u * u, axis=-1, keepdims=True) + EPSILON) * r.ngain[5:6, :])
    gather_z.begin_column()
    gather_a.sides(2)
    gather_a.diagonal(1)

    for k in range(3):
        r.segcol[128 * k : 128 * k + 128, :] = jnp.transpose(jnp.broadcast_to(r.seg[k, 0:1, :], (128, 128)))
    seg = r.segcol[128:384, :]
    for k in range(KC - 1):
        r.same[k] = jnp.where(r.segcol[125 + k : 125 + k + ROWS, :] == seg, 1.0, 0.0)
    gather_a.sides(3)
    gather_z.begin_sides()
    gather_a.diagonal(2)
    for d in range(1, planes):
        gather_z.column(d)
    cots.start()
    gather_out.begin()
    gather_a.diagonal(3)
    gather_a.whole_here()

    def project(k):
        at_k = pl.ds(pl.multiple_of(k * 512, 512), 512)
        r.proj[:, at_k] = dot(r.normed[...], r.wa[:, at_k])

    project(WIDE // 512 - 1)

    def convolve(j):
        at = at_tile(j)
        total = jnp.broadcast_to(r.conv[4:5, at], (ROWS, TILE))
        for k in range(KC):
            term = r.conv[k : k + 1, at] * r.proj[13 + k : 13 + k + ROWS, at]
            total = total + (term if k == KC - 1 else term * r.same[k])
        r.pre[:, at] = total
        return total * sigmoid(total)

    r.bproj[...] = low(convolve(TILES))
    r.cproj[...] = low(convolve(TILES + 1))

    raw = r.proj[HALO:, CH : CH + 128] + r.small_in[8:9, :]
    step = jnp.maximum(raw, 0.0) + jnp.log1p(jnp.exp(-jnp.abs(raw)))
    rate = -jnp.exp(r.small_in[9:10, :])
    lower = jnp.where(iota((ROWS, ROWS), 0) >= iota((ROWS, ROWS), 1), 1.0, 0.0)
    cum = jnp.dot(lower, step * rate, precision=HIGHEST, preferred_element_type=f32)
    r.step[...] = step
    across = jnp.transpose(cum)
    for h in range(H):
        r.cumt[h] = jnp.broadcast_to(across[h : h + 1, :], (8, ROWS))
    last = cum[ROWS - 1 : ROWS, :]
    before = r.segcol[127:128, :]
    first_seg, last_seg = seg[0:1, :], seg[ROWS - 1 : ROWS, :]
    r.ein[...] = jnp.where(seg == before, jnp.exp(cum), 0.0)
    r.eout[...] = jnp.where(seg == last_seg, jnp.exp(last - cum), 0.0)
    through = jnp.logical_and(first_seg == last_seg, first_seg == before)
    factor = jnp.where(through, jnp.exp(last), 0.0)
    segrow = jnp.concatenate([r.seg[1, 0:1, :], r.seg[2, 0:1, :]], axis=1)
    allowed = jnp.logical_and(jnp.concatenate([seg, seg], axis=1) == segrow, iota((ROWS, ROWS), 0) >= iota((ROWS, ROWS), 1))
    r.bar[...] = jnp.where(allowed, 0.0, -1e30)
    rows = packed(jnp.concatenate([jnp.broadcast_to(factor, (8, 128)), jnp.broadcast_to(r.small_in[10:11, :], (8, 128))], axis=0))
    both = dot(rows, spread_matrix(DI))
    r.factors[c] = both[0:8, :]
    r.skipx[...] = both[8:16, :]
    share = pltpu.make_async_remote_copy(
        src_ref=r.factors.at[c], dst_ref=r.factors.at[c], send_sem=r.factor_sem.at[0], recv_sem=r.factor_sem.at[1],
        device_id=mate, device_id_type=MESH,
    )
    share.start()
    spreads = [(r.stepx, packed(step)), (r.einx, packed(r.ein[...])), (r.eoutx, packed(r.eout[...])), (r.cumx, packed(cum))]
    r.stepx[...] = dot(spreads[0][1], spread_matrix(DI))
    r.eoutx[...] = dot(spreads[2][1], spread_matrix(DI))
    loop(0, WIDE // 512 - 1, project)

    def trade_order(k):
        return lax.rem(k + TILES // 2 * (1 - c), TILES)

    def outgoing(k):
        j = trade_order(k)
        at = at_tile(j)
        inner = convolve(j)
        r.inner[:, at] = inner
        scaled = r.stepx[:, at] * inner
        r.xs[:, at] = low(scaled)
        xso = low(scaled * r.eoutx[:, at])
        r.xso[:, at] = xso
        r.part[:, at] = dot(r.bproj[...], xso, TRANS)

    loop(0, TILES // 2, outgoing)
    forward = Chain(r.part, r.state, r.factors, chain_f, 0, planes)
    forward.start()
    loop(TILES // 2, TILES, outgoing)
    share.wait_recv()
    forward.merge()
    r.scores[...] = dot(r.cproj[...], r.bproj[...], TRANS_B)
    r.einx[...] = dot(spreads[1][1], spread_matrix(DI))
    r.cumx[...] = dot(spreads[3][1], spread_matrix(DI))
    gather_z.sides(0)
    for d in range(1, planes):
        gather_out.column(d)

    first_half = iota((1, TILE), 1) < P_SIZE

    def decays(j, band):
        size = 128 * (band + 1)
        rows = slice(128 * band, 128 * band + 128)
        tile = r.cumx[rows, at_tile(j)]
        turned = pltpu.roll(tile, P_SIZE, 1)
        out = []
        for k in range(2):
            column = jnp.where(first_half, tile, turned) if k == 0 else jnp.where(first_half, turned, tile)
            wide = column if band == 0 else jnp.concatenate([column, column], axis=1)
            out.append(jnp.exp(wide - r.cumt[2 * j + k, 0:1, 0:size] + r.bar[rows, 0:size]))
        return out

    def halves(tile):
        zero = jnp.zeros_like(tile)
        return jnp.where(first_half, tile, zero), jnp.where(first_half, zero, tile)

    def within(j):
        at = at_tile(j)
        for band in range(2):
            size = 128 * (band + 1)
            rows = slice(128 * band, 128 * band + 128)
            inside = halves(r.xs[0:size, at])
            total = 0.0
            for decay, xs in zip(decays(j, band), inside):
                total = total + dot(low(decay * r.scores[rows, 0:size]), xs)
            r.y[rows, at] = total

    def turn(chain, when):
        for k in range(planes):
            if when[k]:
                position = k if chain.lead == 0 else planes - 1 - k
                pl.when(z == position)(chain.pass_on)

    turn(forward, [1, 0, 0, 0])
    loop(0, 4, within)
    turn(forward, [0, 1, 0, 0])
    gather_z.sides(1)
    gather_z.diagonal(0)
    gather_out.sides(0)
    loop(4, 8, within)
    turn(forward, [0, 0, 1, 0])
    gather_z.sides(2)
    gather_z.diagonal(1)
    gather_out.sides(1)
    gather_out.diagonal(0)
    loop(8, 12, within)
    gather_z.sides(3)
    gather_z.diagonal(2)
    for item in moves + [gather_a]:
        item.finish()
    turn(forward, [0, 0, 0, 1])
    gather_out.sides(2)
    gather_out.diagonal(1)
    gather_z.diagonal(3)
    forward.close()

    def carried(j):
        at = at_tile(j)
        r.y[:, at] = r.y[:, at] + r.einx[:, at] * dot(r.cproj[...], r.state[:, at])

    loop(0, TILES, carried)
    gather_z.whole_here()

    def project_z(j):
        at = at_rows(j, 512)
        r.z[:, at] = dot(r.normed[HALO:, :], r.wz_full[:, at])

    loop(0, 3, project_z)
    gather_out.sides(3)
    gather_out.diagonal(2)

    def gated_values(rows):
        gate_in = r.z[rows, :]
        sig = sigmoid(gate_in)
        mixed = r.y[rows, :] + r.skipx[0:1, :] * r.inner[rows, :]
        return gate_in, sig, mixed, mixed * (gate_in * sig)

    def gate(k):
        rows = at_rows(k, 16)
        _, _, _, v = gated_values(rows)
        scale = lax.rsqrt(jnp.mean(v * v, axis=-1, keepdims=True) + EPSILON)
        r.scale[rows, :] = jnp.broadcast_to(scale, (16, 128))
        r.gated[rows, :] = low(v * scale * r.gain[6:7, :])

    loop(0, ROWS // 16, gate)
    gather_out.diagonal(3)
    gather_out.whole_here()
    cots.arrived()

    def project_cot(j):
        at = at_rows(j, 512)
        r.dxs[:, at] = dot(r.cot_own[...], r.wout_full[at, :], TRANS_B)

    loop(0, 3, project_cot)
    r.ggain[...] = jnp.zeros((8, DI), f32)
    r.gskip[...] = jnp.zeros((8, DI), f32)

    def gate_back(k):
        rows = at_rows(k, 32)
        gate_in, sig, mixed, v = gated_values(rows)
        scale = r.scale[rows, 0:1]
        dgated = r.dxs[rows, :]
        weighed = dgated * (v * scale)
        r.ggain[...] = r.ggain[...] + weighed[0:8, :] + weighed[8:16, :] + weighed[16:24, :] + weighed[24:32, :]
        a = r.gain[6:7, :] * dgated
        dv = scale * (a - v * (scale * scale) * jnp.mean(v * a, axis=-1, keepdims=True))
        dmixed = dv * (gate_in * sig)
        r.z[rows, :] = dmixed
        r.dy[rows, :] = low(dmixed)
        r.dyin[rows, :] = low(dmixed * r.einx[rows, :])
        r.dz[rows, :] = low(dv * mixed * (sig * (1.0 + gate_in * (1.0 - sig))))
        skip = dmixed * r.inner[rows, :]
        r.gskip[...] = r.gskip[...] + skip[0:8, :] + skip[8:16, :] + skip[16:24, :] + skip[24:32, :]

    loop(0, ROWS // 32, gate_back)

    def incoming(j):
        at = at_tile(j)
        r.part[:, at] = dot(r.cproj[...], r.dyin[:, at], TRANS)

    loop(0, TILES // 2, lambda k: incoming(trade_order(k)))
    backward = Chain(r.part, r.dstate, r.factors, chain_b, 1, planes)
    backward.start()
    loop(TILES // 2, TILES, lambda k: incoming(trade_order(k)))
    reduce_out = Reduce(r.part_out, r.grad_out, 96, "rows", red_out, planes)
    reduce_z = Reduce(r.part_z, r.grad_z, 48, "columns", red_z, planes)
    every = range(planes - 1, -1, -1)

    def project_out(k):
        at = at_rows(k, 256)
        r.act_own[:, at] = low(r.tok[HALO:, at].astype(f32) + dot(r.gated[...], r.wout_full[:, at]))

    loop(0, 3, project_out)
    acts = Shuffle(r.act_own, r.act_out, r.act_sem, back=True)
    acts.start()

    def weights_out(k):
        far = lax.rem(z + 1 + k, planes)
        at = pl.ds(pl.multiple_of(far * (DI // planes), 128), DI // planes)
        r.part_out[at, :] = low(dot(r.gated[:, at], r.cot_own[...], TRANS))
        reduce_out.move(reduce_out.MATE, far).start()

    loop(0, 2, weights_out)
    backward.merge()
    turn(backward, [1, 0, 0, 0])
    loop(2, planes, weights_out)

    def weights_z(k):
        half = lax.rem(k // 3 + 1 + c, 2)
        at = pl.ds(pl.multiple_of(half * (DI // 2) + k % 3 * 256, 256), 256)
        r.part_z[:, at] = low(dot(r.normed[HALO:, :], r.dz[:, at], TRANS))

    loop(0, 3, weights_z)
    for d in every:
        reduce_z.start(d)
    for d in every:
        reduce_out.fold(d)
    turn(backward, [0, 1, 0, 0])
    loop(3, 6, weights_z)
    for d in every:
        reduce_z.fold(d)

    def back_z(k):
        at = at_rows(k, 256)
        r.einx[:, at] = dot(r.dz[...], r.wz_full[at, :], TRANS_B)

    loop(0, 3, back_z)

    def reduce_sides(d):
        reduce_out.sides(d)
        reduce_z.sides(d)

    def reduce_column(d):
        reduce_out.column(d)
        reduce_z.column(d)

    r.dscores[...] = jnp.zeros((ROWS, ROWS), f32)
    r.sums[...] = jnp.zeros((3, ROWS, 128), f32)

    def within_back(j):
        at = at_tile(j)
        upper = lower = 0.0
        for band in range(2):
            size = 128 * (band + 1)
            rows = slice(128 * band, 128 * band + 128)
            xs = r.xs[0:size, at]
            grads = 0.0
            for decay, dy in zip(decays(j, band), halves(r.dy[rows, at])):
                weight = low(decay * r.scores[rows, 0:size])
                grads = grads + decay * dot(dy, xs, TRANS_B)
                upper = upper + dot(weight[:, 0:128], dy, TRANS)
                if band:
                    lower = lower + dot(weight[:, 128:256], dy, TRANS)
            r.dscores[rows, 0:size] = r.dscores[rows, 0:size] + grads
        r.dxs[0:128, at] = upper
        r.dxs[128:256, at] = lower
        gain = r.dy[:, at].astype(f32) * r.y[:, at] - r.xs[:, at].astype(f32) * r.dxs[:, at]
        r.sums[0] = r.sums[0] + head_sums(gain, j)
        inside = r.dxs[:, at]
        r.sums[2] = r.sums[2] + head_sums(r.inner[:, at] * inside, j)
        r.dxs[:, at] = r.skipx[0:1, at] * r.z[:, at] + r.stepx[:, at] * inside

    loop(0, 2, within_back)
    turn(backward, [0, 0, 1, 0])
    reduce_sides(3)
    loop(2, 5, within_back)
    reduce_sides(2)
    reduce_column(3)
    loop(5, 8, within_back)
    reduce_sides(1)
    reduce_column(2)
    turn(backward, [0, 0, 0, 1])
    loop(8, 12, within_back)
    for item in (gather_z, gather_out, cots, forward):
        item.finish()
    share.wait_send()
    backward.close()
    reduce_sides(0)

    def last_sums(j):
        at = at_tile(j)
        far = r.eoutx[:, at] * dot(r.bproj[...], r.dstate[:, at])
        r.sums[1] = r.sums[1] + head_sums(r.inner[:, at] * far, j)
        return r.dxs[:, at] + r.stepx[:, at] * far

    def unconvolve(j, grad):
        at = at_tile(j)
        pre = r.pre[:, at]
        sig = sigmoid(pre)
        grad = grad * (sig * (1.0 + pre * (1.0 - sig)))
        taps = []
        for k in range(KC):
            kept = grad if k == KC - 1 else grad * r.same[k]
            r.dpre[k, 8 : 8 + ROWS, :] = kept
            taps.append(jnp.sum(kept * r.proj[13 + k : 13 + k + ROWS, at], axis=0, keepdims=True))
        taps += [jnp.sum(grad, axis=0, keepdims=True), jnp.zeros((3, TILE), f32)]
        r.gconv[:, at] = jnp.concatenate(taps, axis=0)
        total = 0.0
        for k in range(KC):
            total = total + r.conv[k : k + 1, at] * r.dpre[k, 3 - k : 3 - k + 8 + ROWS, :]
        r.tail[:, at] = total[0:8, :]
        r.dx[0:HALO, at] = low(jnp.concatenate([jnp.zeros((8, TILE), f32), total[0:8, :]], axis=0))
        r.dx[HALO:, at] = low(total[8:, :])
        r.late[:, at] = total[ROWS : ROWS + 8, :]

    reduce_first = Reduce(r.part_a.at[0], r.grad_a.at[0], 48, "columns", red_a, planes)
    reduce_second = Reduce(r.part_a.at[1], r.grad_a.at[1], 48, "columns", red_b, planes)

    def weights_a(group, k):
        half = lax.rem(k + 1 + c, 2)
        at = pl.ds(pl.multiple_of(half * (WIDE // 4), 512), 512)
        from_ = pl.ds(pl.multiple_of(group * (WIDE // 2) + half * (WIDE // 4), 512), 512)
        r.part_a[group, :, at] = low(dot(r.normed[...], r.dx[:, from_], TRANS))

    def columns_back(j):
        unconvolve(j, last_sums(j))

    r.dx[0:HALO, CH:] = jnp.zeros((HALO, WIDE - CH), jnp.bfloat16)
    r.dx[HALO:, CH + 128 :] = jnp.zeros((ROWS, WIDE - CH - 128), jnp.bfloat16)
    r.dpre[...] = jnp.zeros((KC, ROWS + HALO, TILE), f32)
    loop(0, 8, columns_back)
    weights_a(0, 0)
    for d in every:
        reduce_first.start(d)
    weights_a(0, 1)
    reduce_column(1)
    loop(8, 12, columns_back)
    for d in every:
        reduce_first.fold(d)
    dscores = low(r.dscores[...])
    dbproj = dot(dscores, r.cproj[...], TRANS) + dot(r.xso[...], r.dstate[...], TRANS_B)
    dcproj = dot(dscores, r.bproj[...]) + dot(r.dyin[...], r.state[...], TRANS_B)
    pick = jnp.where(iota((DI, 128), 0) // P_SIZE == iota((DI, 128), 1), 1.0, 0.0)
    crossing = jnp.sum(r.dstate[...].astype(f32) * r.state[...].astype(f32), axis=0, keepdims=True) * r.factors[c, 0:1, :]
    rows = jnp.concatenate([jnp.broadcast_to(crossing, (8, DI)), r.gskip[...]], axis=0)
    rows = jnp.dot(rows, pick, precision=HIGHEST, preferred_element_type=f32)
    at_end, gskip = rows[0:1, :], jnp.sum(rows[8:16, :], axis=0, keepdims=True)
    upper = jnp.where(iota((ROWS, ROWS), 0) <= iota((ROWS, ROWS), 1), 1.0, 0.0)
    strict = jnp.where(iota((ROWS, ROWS), 0) > iota((ROWS, ROWS), 1), 1.0, 0.0)
    dlog = (
        jnp.dot(upper, r.sums[0], precision=HIGHEST, preferred_element_type=f32)
        + jnp.dot(strict, r.step[...] * r.sums[1], precision=HIGHEST, preferred_element_type=f32)
        + at_end
    )
    step = r.step[...]
    dstep = r.sums[1] + r.sums[2] + rate * dlog
    draw = dstep * sigmoid(r.proj[HALO:, CH : CH + 128] + r.small_in[8:9, :])
    lanes = iota((1, 128), 1) < H
    draw = jnp.where(lanes, draw, 0.0)
    gbias = jnp.sum(draw, axis=0, keepdims=True)
    glog = jnp.where(lanes, jnp.sum(step * dlog, axis=0, keepdims=True) * rate, 0.0)
    r.dx[HALO:, CH : CH + 128] = low(draw)
    unconvolve(TILES, dbproj)
    unconvolve(TILES + 1, dcproj)
    tails = [
        pltpu.make_async_remote_copy(
            src_ref=r.tail, dst_ref=r.tail_in, send_sem=r.tail_sem.at[0], recv_sem=r.tail_sem.at[1],
            device_id=(1 - c, chip(x, y, z - 1 + c)), device_id_type=MESH,
        )
    ]
    pl.when(z + c > 0)(tails[0].start)

    @pl.when(z + c == planes)
    def _():
        r.tail_in[...] = jnp.zeros((8, CH), f32)

    weights_a(1, 0)
    for d in every:
        reduce_second.start(d)
    weights_a(1, 1)
    reduce_first.sides(3)
    reduce_column(0)
    for d in every:
        reduce_second.fold(d)
    reduce_first.sides(2)
    reduce_out.close()
    reduce_z.close()
    pl.when(z + c < planes)(tails[0].wait_recv)
    r.dx[HALO + ROWS - 16 :, 0:CH] = low(
        jnp.concatenate([r.dx[HALO + ROWS - 16 : HALO + ROWS - 8, 0:CH].astype(f32), r.late[...] + r.tail_in[...]], axis=0)
    )

    def back_in(k):
        at = at_rows(k, 256)
        r.y[:, at] = r.einx[:, at] + dot(r.dx[HALO:, :], r.wa[at, :], TRANS_B)

    loop(0, 3, back_in)
    reduce_first.sides(1)
    reduce_first.column(3)
    reduce_second.sides(3)
    r.ngrad[...] = jnp.zeros((8, 768), f32)

    def norm_back(k):
        rows = at_rows(k, 16)
        dnormed = r.y[rows, 0:768]
        u = r.tok[pl.ds(pl.multiple_of(HALO + 16 * k, 16), 16), :].astype(f32)
        scale = lax.rsqrt(jnp.mean(u * u, axis=-1, keepdims=True) + EPSILON)
        weighed = dnormed * u * scale
        r.ngrad[...] = r.ngrad[...] + weighed[0:8] + weighed[8:16]
        a = r.ngain[5:6, :] * dnormed
        grad = scale * (a - u * (scale * scale) * jnp.mean(u * a, axis=-1, keepdims=True))
        r.gtok[rows, :] = low(r.cot_own[rows, :].astype(f32) + grad)

    loop(0, 8, norm_back)
    reduce_first.sides(0)
    reduce_first.column(2)
    reduce_second.sides(2)
    reduce_second.column(3)
    loop(8, 16, norm_back)
    grads = Shuffle(r.gtok, r.tokens_out, r.back_sem, back=True)
    grads.start()
    reduce_first.column(1)
    reduce_second.sides(1)
    reduce_second.column(2)
    ngain = jnp.sum(r.ngrad[...], axis=0, keepdims=True)
    ggain = jnp.sum(r.ggain[...], axis=0, keepdims=True)
    lane_heads = jnp.concatenate([gbias[:, 0:H], glog[:, 0:H], gskip[:, 0:H], jnp.zeros((1, 128 - 3 * H), f32)], axis=1)
    for k in range(16):
        convs = jnp.concatenate([r.gconv[0:5, 112 * k : 112 * k + 112], jnp.zeros((5, 16), f32)], axis=1)
        first = jnp.concatenate([ngain[:, 48 * k : 48 * k + 48], jnp.zeros((1, 80), f32)], axis=1)
        second = jnp.concatenate([ggain[:, 96 * k : 96 * k + 96], jnp.zeros((1, 32), f32)], axis=1)
        r.table[k] = jnp.concatenate([convs, first, second, lane_heads], axis=0)

    def to_all(k, act):
        other = lax.rem(me + k, 16)
        for far in range(2):
            copy = pltpu.make_async_remote_copy(
                src_ref=r.table.at[other], dst_ref=r.inbox.at[c, me], send_sem=r.table_sem.at[0, far, other],
                recv_sem=r.table_sem.at[1, c, me], device_id=(far, other), device_id_type=MESH,
            )
            pl.when(jnp.logical_or(k > 0, far != c))(functools.partial(act, copy))

    def from_all(k):
        other = lax.rem(me + k, 16)
        for far in range(2):
            copy = pltpu.make_async_remote_copy(
                src_ref=r.table.at[other], dst_ref=r.inbox.at[far, other], send_sem=r.table_sem.at[0, far, other],
                recv_sem=r.table_sem.at[1, far, other], device_id=(far, other), device_id_type=MESH,
            )
            pl.when(jnp.logical_or(k > 0, far != c))(copy.wait_recv)

    loop(0, 16, lambda k: to_all(k, lambda copy: copy.start()))
    r.inbox[c, me] = r.table[me]
    for item in (reduce_out, reduce_z):
        item.drain_early()
        item.drain_late()
        item.finish()
    for item in (backward, acts):
        item.finish()
    acts.arrived()
    reduce_second.sides(0)
    reduce_first.column(0)
    reduce_second.column(1)
    reduce_first.close()
    reduce_first.drain_early()
    reduce_second.drain_early()
    reduce_first.drain_late()
    loop(0, 16, lambda k: to_all(k, lambda copy: copy.wait_send()))
    pl.when(z + c > 0)(tails[0].wait_send)
    reduce_second.column(0)
    reduce_second.close()
    loop(0, 16, from_all)
    r.small_out[...] = jnp.sum(jnp.sum(r.inbox[...], axis=0), axis=0)
    reduce_second.drain_late()
    grads.finish()
    grads.arrived()
    reduce_first.finish()
    reduce_second.finish()


def block(given, planes):
    f32, bf16 = jnp.float32, jnp.bfloat16
    shape = jax.ShapeDtypeStruct
    named = block_scratch(planes)
    extra = Chain.scratch() + Chain.scratch()[:6] + Chain.scratch()[8:]
    extra += Reduce.scratch(48, WIDE // 2, "columns", planes) + Reduce.scratch(48, WIDE // 2, "columns", planes) + Reduce.scratch(48, DI, "columns", planes)
    extra += Reduce.scratch(96, 768, "rows", planes)
    return pl.pallas_call(
        functools.partial(block_kernel, planes, list(named)),
        out_shape=[
            shape((2, 128, 768), bf16), shape((2, 128, 768), bf16), shape((2, 48, WIDE // 2), f32),
            shape((48, DI), f32), shape((96, 768), f32), shape((8, 128), f32),
        ],
        in_specs=[VMEM] * len(GIVEN),
        out_specs=[VMEM] * len(MADE),
        scratch_shapes=list(named.values()) + extra,
        compiler_params=pltpu.CompilerParams(collective_id=0, has_side_effects=True, vmem_limit_bytes=62 << 20),
    )(*given)


def deliver_kernel(acts, tokens, grad_a, grad_z, grad_out, sums, *out):
    out[0][...] = acts[...]
    out[1][...] = tokens[...]
    out[2][...] = sums[5:6, 0:48]
    out[3][:, 0:DI] = grad_z[...]
    out[3][:, DI : DI + WIDE // 2] = grad_a[0]
    out[3][:, DI + WIDE // 2 :] = grad_a[1, :, 0 : CH + H - WIDE // 2]
    out[4][...] = sums[0:4, 0:112]
    out[5][...] = sums[4:5, 0:112]
    out[6][...] = sums[7:8, 0:H]
    out[7][...] = sums[7:8, H : 2 * H]
    out[8][...] = sums[7:8, 2 * H : 3 * H]
    out[9][...] = sums[6:7, 0:96]
    out[10][...] = grad_out[...]


def deliver(made):
    f32, bf16 = jnp.float32, jnp.bfloat16
    shapes = [
        ((2, 128, 768), bf16), ((2, 128, 768), bf16), ((1, 48), f32), ((48, DI + CH + H), f32), ((4, 112), f32), ((1, 112), f32),
        ((1, H), f32), ((1, H), f32), ((1, H), f32), ((1, 96), f32), ((96, 768), f32),
    ]
    return pl.pallas_call(
        deliver_kernel,
        out_shape=[jax.ShapeDtypeStruct(*s) for s in shapes],
        in_specs=[VMEM] * len(made),
        out_specs=[VMEM] * len(shapes),
    )(*made)


def fast_body(
    planes, tokens, cotangent, segments, norm_gain, w_in, conv_weight, conv_bias, step_bias, log_rate, skip_gain, gate_gain, w_out
):
    def at_row(row, values):
        values = values.astype(jnp.float32).reshape(-1, values.shape[-1])
        return jnp.pad(values, ((row, 16 - row - values.shape[0]), (0, 128 - values.shape[1])))

    rows = ((0, conv_weight), (4, conv_bias), (5, norm_gain), (6, gate_gain), (8, step_bias), (9, log_rate), (10, skip_gain))
    small = sum(at_row(row, values) for row, values in rows)
    made = block((tokens[:, 0], cotangent[:, 0], segments[:, 0], small, w_in, w_out), planes)
    out = deliver(made)
    return (
        out[0][:, None], out[1][:, None], out[2][0], out[3], out[4], out[5][0], out[6][0], out[7][0], out[8][0], out[9][0], out[10],
    )


def solution(mesh):
    in_specs = (
        P(None, "dp", "seq", None),
        P(None, "dp", "seq", None),
        P(None, "dp", "seq"),
        P("seq"),
        P("seq", None),
        P(None, "seq"),
        P("seq"),
        P(),
        P(),
        P(),
        P("seq"),
        P("seq", None),
    )
    out_specs = (
        P(None, "dp", "seq", None),
        P(None, "dp", "seq", None),
        P("seq"),
        P("seq", None),
        P(None, "seq"),
        P("seq"),
        P(),
        P(),
        P(),
        P("seq"),
        P("seq", None),
    )
    work = partial(fast_body, mesh.shape["seq"] // 4) if mesh.shape["seq"] == 16 else body
    return jax.shard_map(work, mesh=mesh, in_specs=in_specs, out_specs=out_specs, check_vma=False)
```
